512 devices in a mesh: cuts: 8 (over x, core), strip: 64 (over y, z).
Axes of the slice: x: 4, y: 4, z: 16, core: 2. Of those that a mesh axis runs over, the one named last changes fastest.
Arguments:
- object_slices: bfloat16 [8, 2, 8192, 256], P('cuts', None, 'strip'), may hold values from -6 to 6
- direction: bfloat16 [8, 2, 8192, 256], P('cuts', None, 'strip'), may hold values from -6 to 6
- probe_wave: bfloat16 [2, 128, 128], replicated, may hold values from -6 to 6
- kernel_phase: float32 [128, 128], replicated, may hold values from -3.140625 to 3.140625
- corner_row: int32 [128], P('strip'), may hold values from 0 to 8191, as said below
- corner_col: int32 [128], P('strip'), may hold values from 0 to 128
Outputs:
- hessian_vector: float32 [8, 2, 8192, 256], P('cuts', None, 'strip')
The draws below stay inside these ranges and needn't reach their ends.
Inputs may be any that keep to these rules, and one draw needn't show every extreme that they name: `corner_row`: position j belongs to strip index j // 2; its corner row lies in the strips from 2 below to 2 above that index, counted around the periodic object, and both extremes occur.
All inputs are finite; a program needn't handle non-finite values.
Results may differ from the reference program's by a relative error of at most 0.03.
Values may be sent and summed in bfloat16 or wider, within the bound.
No kernel may reach another device: no remote copies, remote signals or barrier semaphores. Data moves between devices by JAX's collectives and lax.ppermute only.
A program may use at most 64 MiB of HBM per device.

```python
import jax
import jax.numpy as jnp
from jax import lax

P_SIZE = 128
SR = 128
W = 256
PPD = 2
REACH = 2
NSL = 8
OBJ_ROWS = 8192
NPOS = 128


def draw_corner_row(key, part):
    key = jax.random.fold_in(key, 11)
    key_offset, key_inside = jax.random.split(key)
    slot_index = jnp.arange(NPOS, dtype=jnp.int32)
    owner_strip = slot_index // PPD
    strip_offset = jax.random.randint(key_offset, (NPOS,), -REACH, REACH + 1)
    inner_row = jax.random.randint(key_inside, (NPOS,), 0, SR)
    strip_offset = strip_offset.at[0].set(-REACH).at[PPD].set(REACH).at[1].set(0).at[NPOS - 1].set(0)
    inner_row = inner_row.at[1].set(0).at[NPOS - 1].set(SR - 1)
    return (((owner_strip + strip_offset) * SR + inner_row) % OBJ_ROWS).astype(jnp.int32)


def draw_corner_col(key, part):
    key = jax.random.fold_in(key, 12)
    column_draw = jax.random.randint(key, (NPOS,), 0, W - P_SIZE + 1)
    column_draw = column_draw.at[1].set(0).at[NPOS - 1].set(W - P_SIZE)
    return column_draw.astype(jnp.int32)


def block_levels(key, dims, cuts, least, high):
    def one(dim, blocks):
        steps = jax.random.uniform(jax.random.fold_in(jax.random.fold_in(key, 6), dim), (blocks,), jnp.float32, least / len(cuts), high / len(cuts))
        return jnp.repeat(jnp.exp(steps), dims[dim] // blocks).reshape((-1,) + (1,) * (len(dims) - dim - 1))

    loudness = one(*cuts[0])
    for cut in cuts[1:]:
        loudness = loudness * one(*cut)
    return loudness


def scatter_about(stream_key, shape, width, most, shards=(), kind=jnp.bfloat16):
    entries = jax.random.normal(stream_key, shape, jnp.float32) * width
    if len(shards) > 0:
        entries = block_levels(stream_key, shape, shards, -0.22, 0.18) * entries
    return jnp.clip(entries, min=-most, max=most).astype(kind)


def setup_inputs(seed: int = 0) -> dict:
    splits = jax.random.split(jax.random.key(seed), 7)
    return {
        "object_slices": scatter_about(splits[0], (NSL, 2, OBJ_ROWS, W), 0.7071, 6.0, ((0, 8), (2, 64))),
        "direction": scatter_about(splits[1], (NSL, 2, OBJ_ROWS, W), 0.7071, 6.0, ((0, 8), (2, 64))),
        "probe_wave": scatter_about(splits[2], (2, P_SIZE, P_SIZE), 0.7071, 6.0),
        "kernel_phase": jnp.clip(jax.random.uniform(splits[3], (P_SIZE, P_SIZE), jnp.float32, -3.140625, 3.140625), -3.140625, 3.140625),
        "corner_row": draw_corner_row(jax.random.fold_in(splits[6], 71), 0),
        "corner_col": draw_corner_col(jax.random.fold_in(splits[6], 71), 0),
    }


def forward_fourier(real_part, imag_part):
    values = jnp.fft.fft2(real_part + 1j * imag_part, norm="ortho")
    return jnp.real(values), jnp.imag(values)


def inverse_fourier(real_part, imag_part):
    values = jnp.fft.ifft2(real_part + 1j * imag_part, norm="ortho")
    return jnp.real(values), jnp.imag(values)


def apply_kernel(real_part, imag_part, kernel_cos, kernel_sin):
    return real_part * kernel_cos - imag_part * kernel_sin, real_part * kernel_sin + imag_part * kernel_cos


def to_half(values):
    kept = values.astype(jnp.bfloat16)
    kept = lax.optimization_barrier(kept)
    return kept.astype(jnp.float32)


def reference(object_slices, direction, probe_wave, kernel_phase, corner_row, corner_col):
    kernel_cos = jnp.cos(kernel_phase)
    kernel_sin = jnp.sin(kernel_phase)
    object_all = object_slices.astype(jnp.float32)
    direction_all = direction.astype(jnp.float32)
    rows_total = object_slices.shape[2]
    column_count = object_slices.shape[3]
    patch_size = probe_wave.shape[1]
    offsets = jnp.arange(patch_size, dtype=jnp.int32)
    start_re = probe_wave[0].astype(jnp.float32)
    start_im = probe_wave[1].astype(jnp.float32)

    def propagate(real_part, imag_part):
        fourier_re, fourier_im = forward_fourier(real_part, imag_part)
        kept_re, kept_im = apply_kernel(fourier_re, fourier_im, kernel_cos, kernel_sin)
        return inverse_fourier(kept_re, kept_im)

    def propagate_back(real_part, imag_part):
        fourier_re, fourier_im = forward_fourier(real_part, imag_part)
        kept_re, kept_im = apply_kernel(fourier_re, fourier_im, kernel_cos, -kernel_sin)
        return inverse_fourier(kept_re, kept_im)

    def one_patch(hessian, corner):
        corner_top, corner_left = corner
        row_index = (corner_top + offsets) % rows_total
        col_index = (corner_left + offsets) % column_count
        window_obj = object_all[:, :, row_index][:, :, :, col_index]
        window_dir = direction_all[:, :, row_index][:, :, :, col_index]
        psi_re, psi_im = start_re, start_im
        tan_re = jnp.zeros_like(start_re)
        tan_im = jnp.zeros_like(start_re)
        waves = []
        for layer in range(NSL):
            waves.append((psi_re, psi_im))
            obj_re, obj_im = window_obj[layer, 0], window_obj[layer, 1]
            dir_re, dir_im = window_dir[layer, 0], window_dir[layer, 1]
            exit_re = obj_re * psi_re - obj_im * psi_im
            exit_im = obj_re * psi_im + obj_im * psi_re
            delta_re = dir_re * psi_re - dir_im * psi_im + obj_re * tan_re - obj_im * tan_im
            delta_im = dir_re * psi_im + dir_im * psi_re + obj_re * tan_im + obj_im * tan_re
            next_re, next_im = propagate(exit_re, exit_im)
            tnext_re, tnext_im = propagate(delta_re, delta_im)
            if layer < NSL - 1:
                psi_re, psi_im = to_half(next_re), to_half(next_im)
                tan_re, tan_im = to_half(tnext_re), to_half(tnext_im)
            else:
                far_re, far_im = forward_fourier(next_re, next_im)
                dfar_re, dfar_im = forward_fourier(tnext_re, tnext_im)
        weight = (4.0 / NSL) * (far_re * dfar_re + far_im * dfar_im)
        lam_re, lam_im = inverse_fourier(weight * far_re, weight * far_im)
        grads = []
        for layer in range(NSL - 1, -1, -1):
            adj_re, adj_im = propagate_back(lam_re, lam_im)
            psi_re, psi_im = waves[layer]
            grad_re = psi_re * adj_re + psi_im * adj_im
            grad_im = psi_re * adj_im - psi_im * adj_re
            grads.insert(0, jnp.stack([grad_re, grad_im], 0))
            if layer > 0:
                obj_re, obj_im = window_obj[layer, 0], window_obj[layer, 1]
                lam_re = to_half(obj_re * adj_re + obj_im * adj_im)
                lam_im = to_half(obj_re * adj_im - obj_im * adj_re)
        gradient = jnp.stack(grads, 0)
        hessian = hessian.at[:, :, row_index[:, None], col_index[None, :]].add(gradient)
        return hessian, None

    initial = jnp.zeros((NSL, 2, rows_total, column_count), jnp.float32)
    hessian, unused = lax.scan(one_patch, initial, (corner_row, corner_col))
    return hessian
```

```python
import functools
import math

import jax
import jax.numpy as jnp
import ml_dtypes
import numpy as np
from jax import lax
from jax.experimental import pallas as pl
from jax.experimental.pallas import tpu as pltpu
from jax.sharding import PartitionSpec as P

REACH = 2
STRETCH = 1.6236604965019064
BF16 = jnp.bfloat16
F32 = jnp.float32


def transform_tables(size):
    index_line = np.arange(size)
    angle = (index_line[:, None] * index_line[None, :] % size) * (2.0 * math.pi / size)
    cosine, sine = np.cos(angle), np.sin(angle)
    kept_cos = (STRETCH * cosine).astype(ml_dtypes.bfloat16).astype(np.float64)
    kept_sin = (STRETCH * sine).astype(ml_dtypes.bfloat16).astype(np.float64)
    unit = np.sum(kept_cos * cosine + kept_sin * sine) / np.sum(cosine**2 + sine**2)
    unit = unit * math.sqrt(size)
    plus = np.block([[kept_cos, kept_sin], [-kept_sin, kept_cos]])
    minus = np.block([[kept_cos, -kept_sin], [kept_sin, kept_cos]])
    return plus.astype(ml_dtypes.bfloat16), minus.astype(ml_dtypes.bfloat16), unit


def dot(left, right):
    return jnp.dot(left, right, preferred_element_type=F32)


def row_hot(start, rows, columns):
    row_index = lax.broadcasted_iota(jnp.int32, (rows, columns), 0)
    col_index = lax.broadcasted_iota(jnp.int32, (rows, columns), 1)
    return jnp.where(col_index == row_index + start, 1.0, 0.0).astype(BF16)


def col_hot(start, rows, columns):
    row_index = lax.broadcasted_iota(jnp.int32, (rows, columns), 0)
    col_index = lax.broadcasted_iota(jnp.int32, (rows, columns), 1)
    return jnp.where(row_index == col_index + start, 1.0, 0.0).astype(BF16)


def cut_kernel(start_ref, above_ref, own_ref, below_ref, out_ref):
    slots, parts, size, _ = out_ref.shape
    rows, columns = own_ref.shape[1:]
    for slot in range(slots):
        pick_rows = row_hot(start_ref[0, slot], size, 3 * rows)
        pick_cols = col_hot(start_ref[1, slot], columns, size)
        for part in range(parts):
            picked = dot(pick_rows[:, :rows], above_ref[part])
            picked += dot(pick_rows[:, rows : 2 * rows], own_ref[part])
            picked += dot(pick_rows[:, 2 * rows :], below_ref[part])
            out_ref[slot, part] = dot(picked.astype(BF16), pick_cols).astype(BF16)


def chain_kernel(unit, window_ref, probe_ref, cos_ref, sin_ref, plus_ref, minus_ref, out_ref, wave_ref):
    slices = window_ref.shape[0]
    size = window_ref.shape[2]
    plus, minus = plus_ref[...], minus_ref[...]

    def swap(values, waves):
        blocks = [[values[i * size : (i + 1) * size, j * size : (j + 1) * size]
                   for j in range(values.shape[1] // size)] for i in range(values.shape[0] // size)]
        turned = [jnp.concatenate([row[j] for row in blocks], axis=1) for j in range(len(blocks[0]))]
        return jnp.concatenate(turned, axis=0) if len(turned) > 1 else turned[0]

    def forward(columns):
        half = dot(plus, columns.astype(BF16)).astype(BF16)
        return dot(swap(half, None), minus)

    def inverse(rows):
        half = dot(rows.astype(BF16), plus).astype(BF16)
        return dot(minus, swap(half, None))

    def kernel_times(rows, sign, scale):
        kernel_cos, kernel_sin = cos_ref[...] * scale, sin_ref[...] * (sign * scale)
        made = []
        for i in range(rows.shape[0] // size):
            re, im = rows[i * size : (i + 1) * size, :size], rows[i * size : (i + 1) * size, size:]
            made.append(jnp.concatenate(
                [re * kernel_cos - im * kernel_sin, re * kernel_sin + im * kernel_cos], axis=1))
        return jnp.concatenate(made, axis=0) if len(made) > 1 else made[0]

    psi_re, psi_im = probe_ref[0].astype(F32), probe_ref[1].astype(F32)
    tan_re, tan_im = None, None
    far_scale = 1.0 / unit**2
    hop_scale = 1.0 / unit**4
    for layer in range(slices):
        wave_ref[layer, 0], wave_ref[layer, 1] = psi_re, psi_im
        obj_re, obj_im = window_ref[layer, 0].astype(F32), window_ref[layer, 1].astype(F32)
        dir_re, dir_im = window_ref[layer, 2].astype(F32), window_ref[layer, 3].astype(F32)
        exit_re = obj_re * psi_re - obj_im * psi_im
        exit_im = obj_re * psi_im + obj_im * psi_re
        delta_re = dir_re * psi_re - dir_im * psi_im
        delta_im = dir_re * psi_im + dir_im * psi_re
        if layer > 0:
            delta_re += obj_re * tan_re - obj_im * tan_im
            delta_im += obj_re * tan_im + obj_im * tan_re
        columns = jnp.concatenate([
            jnp.concatenate([exit_re, delta_re], axis=1),
            jnp.concatenate([exit_im, delta_im], axis=1)], axis=0)
        spectrum = forward(columns)
        if layer < slices - 1:
            waves = inverse(kernel_times(spectrum, 1.0, hop_scale))
            psi_re, tan_re = waves[:size, :size], waves[:size, size:]
            psi_im, tan_im = waves[size:, :size], waves[size:, size:]
        else:
            far = kernel_times(spectrum, 1.0, far_scale)
    far_re, far_im = far[:size, :size], far[:size, size:]
    weight = (4.0 / slices) * (far_re * far[size:, :size] + far_im * far[size:, size:])
    back = jnp.concatenate([weight * far_re, weight * far_im], axis=1)
    adjoint = inverse(kernel_times(back, -1.0, far_scale))
    for layer in range(slices - 1, -1, -1):
        adj_re, adj_im = adjoint[:size], adjoint[size:]
        psi_re, psi_im = wave_ref[layer, 0], wave_ref[layer, 1]
        out_ref[layer, 0] = (psi_re * adj_re + psi_im * adj_im).astype(BF16)
        out_ref[layer, 1] = (psi_re * adj_im - psi_im * adj_re).astype(BF16)
        if layer > 0:
            obj_re, obj_im = window_ref[layer, 0].astype(F32), window_ref[layer, 1].astype(F32)
            columns = jnp.concatenate(
                [obj_re * adj_re + obj_im * adj_im, obj_re * adj_im - obj_im * adj_re], axis=0)
            adjoint = inverse(kernel_times(forward(columns), -1.0, hop_scale))


def gather_kernel(start_ref, grad_ref, above_ref, own_ref, below_ref):
    slots, parts, size, _ = grad_ref.shape
    rows, columns = own_ref.shape[1:]
    placed = [[], []]
    hots = []
    for slot in range(slots):
        pick_cols = row_hot(start_ref[1, slot], size, columns)
        hots.append(col_hot(start_ref[0, slot], 3 * rows, size))
        for part in range(parts):
            placed[part].append(dot(grad_ref[slot, part], pick_cols).astype(BF16))
    pick_rows = jnp.concatenate(hots, axis=1)
    for part in range(parts):
        total = dot(pick_rows, jnp.concatenate(placed[part], axis=0))
        above_ref[part] = total[:rows].astype(BF16)
        own_ref[part] = total[rows : 2 * rows]
        below_ref[part] = total[2 * rows :].astype(BF16)


def on_device(object_slices, direction, probe_wave, kernel_phase, corner_row, corner_col):
    strip_rows = object_slices.shape[2]
    column_count = object_slices.shape[3]
    patch_size = probe_wave.shape[1]
    slot_count = corner_row.shape[0]
    strip_count = lax.axis_size("strip")
    cuts_count = lax.axis_size("cuts")
    strip_index = lax.axis_index("strip")
    plus, minus, unit = transform_tables(patch_size)

    def shifted(block, distance):
        route = [((i - distance) % strip_count, i) for i in range(strip_count)]
        return lax.ppermute(block, "strip", route)

    vmem = pl.BlockSpec(memory_space=pltpu.VMEM)
    smem = pl.BlockSpec(memory_space=pltpu.SMEM)
    params = pltpu.CompilerParams(vmem_limit_bytes=32 * 1024 * 1024)

    corners = jnp.stack([corner_row, corner_col])
    near = [corners if k == 0 else shifted(corners, -k) for k in range(-REACH, REACH)]
    corners = jnp.concatenate(near, axis=1)
    owner_offset = jnp.asarray(np.repeat(np.arange(-REACH, REACH), slot_count), jnp.int32)
    corner_strip = corners[0] // strip_rows
    behind = (strip_index + owner_offset - corner_strip + REACH) % strip_count - REACH
    place = owner_offset - behind + jnp.clip(behind, 0, 1)
    first_row = (corners[0] - (strip_index - 1) * strip_rows) % (strip_count * strip_rows)
    first_row = jnp.where(place == 0, first_row, 4 * strip_rows)
    start = jnp.stack([first_row, corners[1]])

    stacked = jnp.concatenate([object_slices[0], direction[0]], axis=0)
    above, below = shifted(stacked, 1), shifted(stacked, -1)
    windows = pl.pallas_call(
        cut_kernel,
        out_shape=jax.ShapeDtypeStruct((cuts_count, 4, patch_size, patch_size), BF16),
        in_specs=[smem, vmem, vmem, vmem],
        out_specs=vmem,
        compiler_params=params,
        name="cut_windows",
    )(start, above, stacked, below)
    windows = lax.all_to_all(windows, "cuts", 0, 0, tiled=False)
    gradient = pl.pallas_call(
        functools.partial(chain_kernel, unit),
        out_shape=jax.ShapeDtypeStruct((cuts_count, 2, patch_size, patch_size), BF16),
        in_specs=[vmem] * 6,
        out_specs=vmem,
        scratch_shapes=[pltpu.VMEM((cuts_count, 2, patch_size, patch_size), F32)],
        compiler_params=params,
        name="wave_chain",
    )(windows, probe_wave, jnp.cos(kernel_phase), jnp.sin(kernel_phase), jnp.asarray(plus), jnp.asarray(minus))
    gradient = lax.all_to_all(gradient, "cuts", 0, 0, tiled=False)
    strip_shape = (2, strip_rows, column_count)
    to_above, own, to_below = pl.pallas_call(
        gather_kernel,
        out_shape=(
            jax.ShapeDtypeStruct(strip_shape, BF16),
            jax.ShapeDtypeStruct(strip_shape, F32),
            jax.ShapeDtypeStruct(strip_shape, BF16),
        ),
        in_specs=[smem, vmem],
        out_specs=(vmem, vmem, vmem),
        compiler_params=params,
        name="add_windows",
    )(start, gradient)
    from_below = shifted(to_above, -1).astype(F32)
    from_above = shifted(to_below, 1).astype(F32)
    return (own + from_below + from_above)[None]


def solution(mesh):
    in_specs = (
        P("cuts", None, "strip", None),
        P("cuts", None, "strip", None),
        P(),
        P(),
        P("strip"),
        P("strip"),
    )
    out_specs = P("cuts", None, "strip", None)
    return jax.shard_map(
        on_device, mesh=mesh, in_specs=in_specs, out_specs=out_specs, check_vma=False
    )
```

```python
import functools
import math

import jax
import jax.numpy as jnp
import ml_dtypes
import numpy as np
from jax import lax
from jax.experimental import pallas as pl
from jax.experimental.pallas import tpu as pltpu
from jax.sharding import PartitionSpec as P

REACH = 2
NOTE_ROWS = 16
STRETCH = 1.6236604965019064
BF16 = jnp.bfloat16
F32 = jnp.float32


def transform_tables(size):
    index_line = np.arange(size)
    angle = (index_line[:, None] * index_line[None, :] % size) * (2.0 * math.pi / size)
    cosine, sine = np.cos(angle), np.sin(angle)
    kept_cos = (STRETCH * cosine).astype(ml_dtypes.bfloat16).astype(np.float64)
    kept_sin = (STRETCH * sine).astype(ml_dtypes.bfloat16).astype(np.float64)
    unit = np.sum(kept_cos * cosine + kept_sin * sine) / np.sum(cosine**2 + sine**2)
    unit = unit * math.sqrt(size)
    plus = np.block([[kept_cos, kept_sin], [-kept_sin, kept_cos]])
    minus = np.block([[kept_cos, -kept_sin], [kept_sin, kept_cos]])
    return plus.astype(ml_dtypes.bfloat16), minus.astype(ml_dtypes.bfloat16), unit


def dot(left, right):
    return jnp.dot(left, right, preferred_element_type=F32)


def row_hot(start, rows, columns):
    row_index = lax.broadcasted_iota(jnp.int32, (rows, columns), 0)
    col_index = lax.broadcasted_iota(jnp.int32, (rows, columns), 1)
    return jnp.where((col_index - row_index).astype(F32) == start, 1.0, 0.0).astype(BF16)


def col_hot(start, rows, columns):
    row_index = lax.broadcasted_iota(jnp.int32, (rows, columns), 0)
    col_index = lax.broadcasted_iota(jnp.int32, (rows, columns), 1)
    return jnp.where((row_index - col_index).astype(F32) == start, 1.0, 0.0).astype(BF16)


def cut_kernel(rows, far_ref, above_ref, own_ref, below_ref, out_ref, start_ref):
    slots, parts, size, _ = out_ref.shape
    columns = own_ref.shape[1]
    near = slots // 4
    hots = []
    for owner, note_ref in enumerate((far_ref, above_ref, own_ref, below_ref)):
        note = note_ref[note_ref.shape[0] - NOTE_ROWS :, :].astype(F32)[0:1]
        for position in range(near):
            here = note[:, 2 * near + position : 2 * near + position + 1] == owner - REACH
            first_row = jnp.where(here, note[:, position : position + 1], 4.0 * rows)
            first_col = note[:, near + position : near + position + 1]
            slot = owner * near + position
            start_ref[2 * slot : 2 * slot + 1, :] = jnp.broadcast_to(first_row, (1, 128))
            start_ref[2 * slot + 1 : 2 * slot + 2, :] = jnp.broadcast_to(first_col, (1, 128))
            hots.append((row_hot(first_row, size, 3 * rows), col_hot(first_col, columns, size)))
    bands = [
        jnp.concatenate(
            [ref[part * rows : (part + 1) * rows, :] for ref in (above_ref, own_ref, below_ref)], axis=0
        )
        for part in range(parts)
    ]
    pick_rows = jnp.concatenate([hot for hot, _ in hots], axis=0)
    picked = [dot(pick_rows, band).astype(BF16) for band in bands]
    for slot in range(slots):
        lines = [part[slot * size : (slot + 1) * size] for part in picked]
        window = dot(jnp.concatenate(lines, axis=0), hots[slot][1]).astype(BF16)
        out_ref[slot] = window.reshape(parts, size, size)


def chain_kernel(unit, window_ref, probe_ref, cos_ref, sin_ref, plus_ref, minus_ref, out_ref, wave_ref):
    slices = window_ref.shape[0]
    size = window_ref.shape[2]
    plus, minus = plus_ref[...], minus_ref[...]

    def swap(values, waves):
        blocks = [[values[i * size : (i + 1) * size, j * size : (j + 1) * size]
                   for j in range(values.shape[1] // size)] for i in range(values.shape[0] // size)]
        turned = [jnp.concatenate([row[j] for row in blocks], axis=1) for j in range(len(blocks[0]))]
        return jnp.concatenate(turned, axis=0) if len(turned) > 1 else turned[0]

    def forward(columns):
        half = dot(plus, columns.astype(BF16)).astype(BF16)
        return dot(swap(half, None), minus)

    def inverse(rows):
        half = dot(rows.astype(BF16), plus).astype(BF16)
        return dot(minus, swap(half, None))

    def kernel_times(rows, sign, scale):
        kernel_cos, kernel_sin = cos_ref[...] * scale, sin_ref[...] * (sign * scale)
        made = []
        for i in range(rows.shape[0] // size):
            re, im = rows[i * size : (i + 1) * size, :size], rows[i * size : (i + 1) * size, size:]
            made.append(jnp.concatenate(
                [re * kernel_cos - im * kernel_sin, re * kernel_sin + im * kernel_cos], axis=1))
        return jnp.concatenate(made, axis=0) if len(made) > 1 else made[0]

    psi_re, psi_im = probe_ref[0].astype(F32), probe_ref[1].astype(F32)
    tan_re, tan_im = None, None
    far_scale = 1.0 / unit**2
    hop_scale = 1.0 / unit**4
    for layer in range(slices):
        wave_ref[layer, 0], wave_ref[layer, 1] = psi_re, psi_im
        obj_re, obj_im = window_ref[layer, 0].astype(F32), window_ref[layer, 1].astype(F32)
        dir_re, dir_im = window_ref[layer, 2].astype(F32), window_ref[layer, 3].astype(F32)
        exit_re = obj_re * psi_re - obj_im * psi_im
        exit_im = obj_re * psi_im + obj_im * psi_re
        delta_re = dir_re * psi_re - dir_im * psi_im
        delta_im = dir_re * psi_im + dir_im * psi_re
        if layer > 0:
            delta_re += obj_re * tan_re - obj_im * tan_im
            delta_im += obj_re * tan_im + obj_im * tan_re
        columns = jnp.concatenate([
            jnp.concatenate([exit_re, delta_re], axis=1),
            jnp.concatenate([exit_im, delta_im], axis=1)], axis=0)
        spectrum = forward(columns)
        if layer < slices - 1:
            waves = inverse(kernel_times(spectrum, 1.0, hop_scale))
            psi_re, tan_re = waves[:size, :size], waves[:size, size:]
            psi_im, tan_im = waves[size:, :size], waves[size:, size:]
        else:
            far = kernel_times(spectrum, 1.0, far_scale)
    far_re, far_im = far[:size, :size], far[:size, size:]
    weight = (4.0 / slices) * (far_re * far[size:, :size] + far_im * far[size:, size:])
    back = jnp.concatenate([weight * far_re, weight * far_im], axis=1)
    adjoint = inverse(kernel_times(back, -1.0, far_scale))
    for layer in range(slices - 1, -1, -1):
        adj_re, adj_im = adjoint[:size], adjoint[size:]
        psi_re, psi_im = wave_ref[layer, 0], wave_ref[layer, 1]
        out_ref[layer, 0] = (psi_re * adj_re + psi_im * adj_im).astype(BF16)
        out_ref[layer, 1] = (psi_re * adj_im - psi_im * adj_re).astype(BF16)
        if layer > 0:
            obj_re, obj_im = window_ref[layer, 0].astype(F32), window_ref[layer, 1].astype(F32)
            columns = jnp.concatenate(
                [obj_re * adj_re + obj_im * adj_im, obj_re * adj_im - obj_im * adj_re], axis=0)
            adjoint = inverse(kernel_times(forward(columns), -1.0, hop_scale))


def gather_kernel(start_ref, grad_ref, above_ref, own_ref, below_ref):
    slots, parts, size, _ = grad_ref.shape
    rows, columns = own_ref.shape[1:]
    placed = [[] for _ in range(parts)]
    hots = []
    for slot in range(slots):
        first_row = start_ref[2 * slot : 2 * slot + 1, 0:1]
        first_col = start_ref[2 * slot + 1 : 2 * slot + 2, 0:1]
        hots.append(col_hot(first_row, 3 * rows, size))
        values = grad_ref[slot].reshape(parts * size, size)
        spread = dot(values, row_hot(first_col, size, columns)).astype(BF16)
        for part in range(parts):
            placed[part].append(spread[part * size : (part + 1) * size])
    pick_rows = jnp.concatenate(hots, axis=1)
    for part in range(parts):
        total = dot(pick_rows, jnp.concatenate(placed[part], axis=0))
        above_ref[part] = total[:rows].astype(BF16)
        own_ref[part] = total[rows : 2 * rows]
        below_ref[part] = total[2 * rows :].astype(BF16)


def on_device(object_slices, direction, probe_wave, kernel_phase, corner_row, corner_col):
    strip_rows = object_slices.shape[2]
    column_count = object_slices.shape[3]
    patch_size = probe_wave.shape[1]
    strip_count = lax.axis_size("strip")
    cuts_count = lax.axis_size("cuts")
    strip_index = lax.axis_index("strip")
    plus, minus, unit = transform_tables(patch_size)

    def shifted(block, distance):
        route = [((i - distance) % strip_count, i) for i in range(strip_count)]
        return lax.ppermute(block, "strip", route)

    vmem = pl.BlockSpec(memory_space=pltpu.VMEM)
    params = pltpu.CompilerParams(vmem_limit_bytes=32 * 1024 * 1024)

    total_rows = strip_count * strip_rows
    inside = (corner_row - (strip_index - REACH) * strip_rows) % total_rows - REACH * strip_rows
    ahead = REACH - (inside + REACH * strip_rows) // strip_rows
    to_owner = ahead - jnp.clip(ahead, 0, 1)
    first_row = inside + (to_owner + 1) * strip_rows
    note = jnp.concatenate([first_row, corner_col, to_owner]).astype(BF16)
    note = jnp.pad(note[None], ((0, NOTE_ROWS - 1), (0, column_count - note.shape[0])))
    block = jnp.concatenate(
        [
            object_slices.reshape(2 * strip_rows, column_count),
            direction.reshape(2 * strip_rows, column_count),
            note,
        ],
        axis=0,
    )
    above, below = shifted(block, 1), shifted(block, -1)
    windows, start = pl.pallas_call(
        functools.partial(cut_kernel, strip_rows),
        out_shape=(
            jax.ShapeDtypeStruct((cuts_count, 4, patch_size, patch_size), BF16),
            jax.ShapeDtypeStruct((2 * cuts_count, 128), F32),
        ),
        in_specs=[vmem] * 4,
        out_specs=(vmem, vmem),
        compiler_params=params,
        name="cut_windows",
    )(shifted(note, REACH), above, block, below)
    windows = lax.all_to_all(windows, "cuts", 0, 0, tiled=False)
    gradient = pl.pallas_call(
        functools.partial(chain_kernel, unit),
        out_shape=jax.ShapeDtypeStruct((cuts_count, 2, patch_size, patch_size), BF16),
        in_specs=[vmem] * 6,
        out_specs=vmem,
        scratch_shapes=[pltpu.VMEM((cuts_count, 2, patch_size, patch_size), F32)],
        compiler_params=params,
        name="wave_chain",
    )(windows, probe_wave, jnp.cos(kernel_phase), jnp.sin(kernel_phase), jnp.asarray(plus), jnp.asarray(minus))
    gradient = lax.all_to_all(gradient, "cuts", 0, 0, tiled=False)
    strip_shape = (2, strip_rows, column_count)
    to_above, own, to_below = pl.pallas_call(
        gather_kernel,
        out_shape=(
            jax.ShapeDtypeStruct(strip_shape, BF16),
            jax.ShapeDtypeStruct(strip_shape, F32),
            jax.ShapeDtypeStruct(strip_shape, BF16),
        ),
        in_specs=[vmem, vmem],
        out_specs=(vmem, vmem, vmem),
        compiler_params=params,
        name="add_windows",
    )(start, gradient)
    from_below = shifted(to_above, -1).astype(F32)
    from_above = shifted(to_below, 1).astype(F32)
    return (own + from_below + from_above)[None]


def solution(mesh):
    in_specs = (
        P("cuts", None, "strip", None),
        P("cuts", None, "strip", None),
        P(),
        P(),
        P("strip"),
        P("strip"),
    )
    out_specs = P("cuts", None, "strip", None)
    return jax.shard_map(
        on_device, mesh=mesh, in_specs=in_specs, out_specs=out_specs, check_vma=False
    )
```

```python
import functools
import math

import jax
import jax.numpy as jnp
import ml_dtypes
import numpy as np
from jax import lax
from jax.experimental import pallas as pl
from jax.experimental.pallas import tpu as pltpu
from jax.sharding import PartitionSpec as P

REACH = 2
NOTE_ROWS = 16
STRETCH = 1.6236604965019064
BF16 = jnp.bfloat16
F32 = jnp.float32


def transform_tables(size):
    index_line = np.arange(size)
    angle = (index_line[:, None] * index_line[None, :] % size) * (2.0 * math.pi / size)
    cosine, sine = np.cos(angle), np.sin(angle)
    kept_cos = (STRETCH * cosine).astype(ml_dtypes.bfloat16).astype(np.float64)
    kept_sin = (STRETCH * sine).astype(ml_dtypes.bfloat16).astype(np.float64)
    unit = np.sum(kept_cos * cosine + kept_sin * sine) / np.sum(cosine**2 + sine**2)
    unit = unit * math.sqrt(size)
    plus = np.block([[kept_cos, kept_sin], [-kept_sin, kept_cos]])
    minus = np.block([[kept_cos, -kept_sin], [kept_sin, kept_cos]])
    return plus.astype(ml_dtypes.bfloat16), minus.astype(ml_dtypes.bfloat16), unit


def dot(left, right):
    return jnp.dot(left, right, preferred_element_type=F32)


def row_hot(start, rows, columns):
    row_index = lax.broadcasted_iota(jnp.int32, (rows, columns), 0)
    col_index = lax.broadcasted_iota(jnp.int32, (rows, columns), 1)
    return jnp.where((col_index - row_index).astype(F32) == start, 1.0, 0.0).astype(BF16)


def col_hot(start, rows, columns):
    row_index = lax.broadcasted_iota(jnp.int32, (rows, columns), 0)
    col_index = lax.broadcasted_iota(jnp.int32, (rows, columns), 1)
    return jnp.where((row_index - col_index).astype(F32) == start, 1.0, 0.0).astype(BF16)


def pack_kernel(
    strip_rows, total_rows, row_any, col_any, object_any, direction_any, block_ref, note_ref, row_ref, col_ref, sems
):
    half = object_any.shape[0]
    columns = block_ref.shape[1]
    corners = [
        pltpu.make_async_copy(row_any, row_ref, sems.at[0]),
        pltpu.make_async_copy(col_any, col_ref, sems.at[1]),
    ]
    bulk = [
        pltpu.make_async_copy(object_any, block_ref.at[pl.ds(0, half), :], sems.at[2]),
        pltpu.make_async_copy(direction_any, block_ref.at[pl.ds(half, half), :], sems.at[3]),
    ]
    for copy in corners + bulk:
        copy.start()
    for copy in corners:
        copy.wait()
    strip_index = lax.axis_index("strip")
    near = row_ref.shape[0]
    lane = lax.broadcasted_iota(jnp.int32, (NOTE_ROWS, columns), 1)
    note = jnp.zeros((NOTE_ROWS, columns), F32)
    for position in range(near):
        inside = row_ref[position] - (strip_index - REACH) * strip_rows
        inside = lax.rem(inside + 2 * total_rows, total_rows)
        ahead = 2 * REACH - lax.div(inside, strip_rows) - REACH
        to_owner = ahead - jnp.clip(ahead, 0, 1)
        first_row = inside + (to_owner + 1 - REACH) * strip_rows
        for place, value in enumerate((first_row, col_ref[position], to_owner)):
            note = jnp.where(lane == place * near + position, value.astype(F32), note)
    note = note.astype(BF16)
    block_ref[2 * half :, :] = note
    note_ref[...] = note
    for copy in bulk:
        copy.wait()


def phase_kernel(note_ref, phase_ref, far_ref, cos_ref, sin_ref):
    far_ref[...] = note_ref[...]
    cos_ref[...] = jnp.cos(phase_ref[...])
    sin_ref[...] = jnp.sin(phase_ref[...])


def cut_kernel(rows, far_ref, note_ref, object_ref, direction_ref, second_ref, first_ref, out_ref, start_ref):
    even = lax.rem(lax.axis_index("strip"), 2) == 0
    first, second = first_ref[...], second_ref[...]
    above, below = jnp.where(even, first, second), jnp.where(even, second, first)
    own = jnp.concatenate([object_ref[...], direction_ref[...], note_ref[...]], axis=0)
    slots, parts, size, _ = out_ref.shape
    columns = object_ref.shape[1]
    near = slots // 4
    hots = []
    for owner, block in enumerate((far_ref[...], above, own, below)):
        note = block[block.shape[0] - NOTE_ROWS :, :].astype(F32)[0:1]
        for position in range(near):
            here = note[:, 2 * near + position : 2 * near + position + 1] == owner - REACH
            first_row = jnp.where(here, note[:, position : position + 1], 4.0 * rows)
            first_col = note[:, near + position : near + position + 1]
            slot = owner * near + position
            start_ref[2 * slot : 2 * slot + 1, :] = jnp.broadcast_to(first_row, (1, 128))
            start_ref[2 * slot + 1 : 2 * slot + 2, :] = jnp.broadcast_to(first_col, (1, 128))
            hots.append((row_hot(first_row, size, 3 * rows), col_hot(first_col, columns, size)))
    bands = [
        jnp.concatenate(
            [block[part * rows : (part + 1) * rows, :] for block in (above, own, below)], axis=0
        )
        for part in range(parts)
    ]
    pick_rows = jnp.concatenate([hot for hot, _ in hots], axis=0)
    picked = [dot(pick_rows, band).astype(BF16) for band in bands]
    for slot in range(slots):
        lines = [part[slot * size : (slot + 1) * size] for part in picked]
        window = dot(jnp.concatenate(lines, axis=0), hots[slot][1]).astype(BF16)
        out_ref[slot] = window.reshape(parts, size, size)


def chain_kernel(unit, window_ref, probe_ref, cos_ref, sin_ref, plus_ref, minus_ref, out_ref, wave_ref):
    slices = window_ref.shape[0]
    size = window_ref.shape[2]
    plus, minus = plus_ref[...], minus_ref[...]

    def swap(values, waves):
        blocks = [[values[i * size : (i + 1) * size, j * size : (j + 1) * size]
                   for j in range(values.shape[1] // size)] for i in range(values.shape[0] // size)]
        turned = [jnp.concatenate([row[j] for row in blocks], axis=1) for j in range(len(blocks[0]))]
        return jnp.concatenate(turned, axis=0) if len(turned) > 1 else turned[0]

    def forward(columns):
        half = dot(plus, columns.astype(BF16)).astype(BF16)
        return dot(swap(half, None), minus)

    def inverse(rows):
        half = dot(rows.astype(BF16), plus).astype(BF16)
        return dot(minus, swap(half, None))

    def kernel_times(rows, sign, scale):
        kernel_cos, kernel_sin = cos_ref[...] * scale, sin_ref[...] * (sign * scale)
        made = []
        for i in range(rows.shape[0] // size):
            re, im = rows[i * size : (i + 1) * size, :size], rows[i * size : (i + 1) * size, size:]
            made.append(jnp.concatenate(
                [re * kernel_cos - im * kernel_sin, re * kernel_sin + im * kernel_cos], axis=1))
        return jnp.concatenate(made, axis=0) if len(made) > 1 else made[0]

    psi_re, psi_im = probe_ref[0].astype(F32), probe_ref[1].astype(F32)
    tan_re, tan_im = None, None
    far_scale = 1.0 / unit**2
    hop_scale = 1.0 / unit**4
    for layer in range(slices):
        wave_ref[layer, 0], wave_ref[layer, 1] = psi_re, psi_im
        obj_re, obj_im = window_ref[layer, 0].astype(F32), window_ref[layer, 1].astype(F32)
        dir_re, dir_im = window_ref[layer, 2].astype(F32), window_ref[layer, 3].astype(F32)
        exit_re = obj_re * psi_re - obj_im * psi_im
        exit_im = obj_re * psi_im + obj_im * psi_re
        delta_re = dir_re * psi_re - dir_im * psi_im
        delta_im = dir_re * psi_im + dir_im * psi_re
        if layer > 0:
            delta_re += obj_re * tan_re - obj_im * tan_im
            delta_im += obj_re * tan_im + obj_im * tan_re
        columns = jnp.concatenate([
            jnp.concatenate([exit_re, delta_re], axis=1),
            jnp.concatenate([exit_im, delta_im], axis=1)], axis=0)
        spectrum = forward(columns)
        if layer < slices - 1:
            waves = inverse(kernel_times(spectrum, 1.0, hop_scale))
            psi_re, tan_re = waves[:size, :size], waves[:size, size:]
            psi_im, tan_im = waves[size:, :size], waves[size:, size:]
        else:
            far = kernel_times(spectrum, 1.0, far_scale)
    far_re, far_im = far[:size, :size], far[:size, size:]
    weight = (4.0 / slices) * (far_re * far[size:, :size] + far_im * far[size:, size:])
    back = jnp.concatenate([weight * far_re, weight * far_im], axis=1)
    adjoint = inverse(kernel_times(back, -1.0, far_scale))
    for layer in range(slices - 1, -1, -1):
        adj_re, adj_im = adjoint[:size], adjoint[size:]
        psi_re, psi_im = wave_ref[layer, 0], wave_ref[layer, 1]
        out_ref[layer, 0] = (psi_re * adj_re + psi_im * adj_im).astype(BF16)
        out_ref[layer, 1] = (psi_re * adj_im - psi_im * adj_re).astype(BF16)
        if layer > 0:
            obj_re, obj_im = window_ref[layer, 0].astype(F32), window_ref[layer, 1].astype(F32)
            columns = jnp.concatenate(
                [obj_re * adj_re + obj_im * adj_im, obj_re * adj_im - obj_im * adj_re], axis=0)
            adjoint = inverse(kernel_times(forward(columns), -1.0, hop_scale))


def gather_kernel(start_ref, grad_ref, first_ref, own_ref, second_ref):
    slots, parts, size, _ = grad_ref.shape
    rows, columns = own_ref.shape[1:]
    even = lax.rem(lax.axis_index("strip"), 2) == 0
    placed = [[] for _ in range(parts)]
    hots = []
    for slot in range(slots):
        first_row = start_ref[2 * slot : 2 * slot + 1, 0:1]
        first_col = start_ref[2 * slot + 1 : 2 * slot + 2, 0:1]
        hots.append(col_hot(first_row, 3 * rows, size))
        values = grad_ref[slot].reshape(parts * size, size)
        spread = dot(values, row_hot(first_col, size, columns)).astype(BF16)
        for part in range(parts):
            placed[part].append(spread[part * size : (part + 1) * size])
    pick_rows = jnp.concatenate(hots, axis=1)
    for part in range(parts):
        total = dot(pick_rows, jnp.concatenate(placed[part], axis=0))
        above, below = total[:rows].astype(BF16), total[2 * rows :].astype(BF16)
        own_ref[part] = total[rows : 2 * rows]
        first_ref[part] = jnp.where(even, above, below)
        second_ref[part] = jnp.where(even, below, above)


def on_device(object_slices, direction, probe_wave, kernel_phase, corner_row, corner_col):
    strip_rows = object_slices.shape[2]
    column_count = object_slices.shape[3]
    patch_size = probe_wave.shape[1]
    strip_count = lax.axis_size("strip")
    cuts_count = lax.axis_size("cuts")
    plus, minus, unit = transform_tables(patch_size)

    def exchanged(block, offset):
        route = [(i, ((i - offset) ^ 1) + offset) for i in range(strip_count)]
        return lax.ppermute(block, "strip", [(i, j % strip_count) for i, j in route])

    vmem = pl.BlockSpec(memory_space=pltpu.VMEM)
    params = pltpu.CompilerParams(vmem_limit_bytes=32 * 1024 * 1024)

    block_rows = 4 * strip_rows + NOTE_ROWS
    hbm = pl.BlockSpec(memory_space=pl.ANY)
    wide = pltpu.CompilerParams(vmem_limit_bytes=60 * 1024 * 1024)
    objects = object_slices.reshape(-1, column_count)
    directions = direction.reshape(-1, column_count)
    block, note = pl.pallas_call(
        functools.partial(pack_kernel, strip_rows, strip_count * strip_rows),
        out_shape=(
            jax.ShapeDtypeStruct((block_rows, column_count), BF16),
            jax.ShapeDtypeStruct((NOTE_ROWS, column_count), BF16),
        ),
        in_specs=[hbm] * 4,
        out_specs=(vmem, vmem),
        scratch_shapes=[
            pltpu.SMEM(corner_row.shape, jnp.int32),
            pltpu.SMEM(corner_row.shape, jnp.int32),
            pltpu.SemaphoreType.DMA((4,)),
        ],
        compiler_params=wide,
        name="pack_block",
    )(corner_row, corner_col, objects, directions)
    far = lax.ppermute(note, "strip", [(i, (i + REACH) % strip_count) for i in range(strip_count)])
    first, second = exchanged(block, -1), exchanged(block, 0)
    far, kernel_cos, kernel_sin = pl.pallas_call(
        phase_kernel,
        out_shape=(
            jax.ShapeDtypeStruct(note.shape, BF16),
            jax.ShapeDtypeStruct(kernel_phase.shape, F32),
            jax.ShapeDtypeStruct(kernel_phase.shape, F32),
        ),
        in_specs=[vmem] * 2,
        out_specs=(vmem,) * 3,
        compiler_params=params,
        cost_estimate=pl.CostEstimate(flops=20_000_000_000, bytes_accessed=100_000_000, transcendentals=0),
        name="phase_tables",
    )(far, kernel_phase)
    windows, start = pl.pallas_call(
        functools.partial(cut_kernel, strip_rows),
        out_shape=(
            jax.ShapeDtypeStruct((cuts_count, 4, patch_size, patch_size), BF16),
            jax.ShapeDtypeStruct((2 * cuts_count, 128), F32),
        ),
        in_specs=[vmem] * 6,
        out_specs=(vmem, vmem),
        compiler_params=params,
        name="cut_windows",
    )(far, note, objects, directions, second, first)
    windows = lax.all_to_all(windows, "cuts", 0, 0, tiled=False)
    gradient = pl.pallas_call(
        functools.partial(chain_kernel, unit),
        out_shape=jax.ShapeDtypeStruct((cuts_count, 2, patch_size, patch_size), BF16),
        in_specs=[vmem] * 6,
        out_specs=vmem,
        scratch_shapes=[pltpu.VMEM((cuts_count, 2, patch_size, patch_size), F32)],
        compiler_params=params,
        name="wave_chain",
    )(windows, probe_wave, kernel_cos, kernel_sin, jnp.asarray(plus), jnp.asarray(minus))
    gradient = lax.all_to_all(gradient, "cuts", 0, 0, tiled=False)
    strip_shape = (2, strip_rows, column_count)
    first, own, second = pl.pallas_call(
        gather_kernel,
        out_shape=(
            jax.ShapeDtypeStruct(strip_shape, BF16),
            jax.ShapeDtypeStruct(strip_shape, F32),
            jax.ShapeDtypeStruct(strip_shape, BF16),
        ),
        in_specs=[vmem, vmem],
        out_specs=(vmem, vmem, vmem),
        compiler_params=params,
        name="add_windows",
    )(start, gradient)
    first, second = exchanged(first, -1), exchanged(second, 0)
    return (own + first.astype(F32) + second.astype(F32))[None]


def solution(mesh):
    in_specs = (
        P("cuts", None, "strip", None),
        P("cuts", None, "strip", None),
        P(),
        P(),
        P("strip"),
        P("strip"),
    )
    out_specs = P("cuts", None, "strip", None)
    return jax.shard_map(
        on_device, mesh=mesh, in_specs=in_specs, out_specs=out_specs, check_vma=False
    )
```

```python
import functools
import math

import jax
import jax.numpy as jnp
import ml_dtypes
import numpy as np
from jax import lax
from jax.experimental import pallas as pl
from jax.experimental.pallas import tpu as pltpu
from jax.sharding import PartitionSpec as P

REACH = 2
NOTE_ROWS = 16
OWNERS = (-REACH, 0, 1)
STRETCH = 1.6236604965019064
BF16 = jnp.bfloat16
F32 = jnp.float32


def transform_tables(size):
    index_line = np.arange(size)
    angle = (index_line[:, None] * index_line[None, :] % size) * (2.0 * math.pi / size)
    cosine, sine = np.cos(angle), np.sin(angle)
    kept_cos = (STRETCH * cosine).astype(ml_dtypes.bfloat16).astype(np.float64)
    kept_sin = (STRETCH * sine).astype(ml_dtypes.bfloat16).astype(np.float64)
    unit = np.sum(kept_cos * cosine + kept_sin * sine) / np.sum(cosine**2 + sine**2)
    unit = unit * math.sqrt(size)
    plus = np.block([[kept_cos, kept_sin], [-kept_sin, kept_cos]])
    minus = np.block([[kept_cos, -kept_sin], [kept_sin, kept_cos]])
    return plus.astype(ml_dtypes.bfloat16), minus.astype(ml_dtypes.bfloat16), unit


def dot(left, right):
    return jnp.dot(left, right, preferred_element_type=F32)


def row_hot(start, rows, columns):
    row_index = lax.broadcasted_iota(jnp.int32, (rows, columns), 0)
    col_index = lax.broadcasted_iota(jnp.int32, (rows, columns), 1)
    return jnp.where((col_index - row_index).astype(F32) == start, 1.0, 0.0).astype(BF16)


def col_hot(start, rows, columns):
    row_index = lax.broadcasted_iota(jnp.int32, (rows, columns), 0)
    col_index = lax.broadcasted_iota(jnp.int32, (rows, columns), 1)
    return jnp.where((row_index - col_index).astype(F32) == start, 1.0, 0.0).astype(BF16)


def pack_kernel(
    strip_rows, total_rows, row_any, col_any, object_any, direction_any, block_ref, note_ref, row_ref, col_ref, sems
):
    half = object_any.shape[0]
    columns = block_ref.shape[1]
    corners = [
        pltpu.make_async_copy(row_any, row_ref, sems.at[0]),
        pltpu.make_async_copy(col_any, col_ref, sems.at[1]),
    ]
    bulk = [
        pltpu.make_async_copy(object_any, block_ref.at[pl.ds(0, half), :], sems.at[2]),
        pltpu.make_async_copy(direction_any, block_ref.at[pl.ds(half, half), :], sems.at[3]),
    ]
    for copy in corners + bulk:
        copy.start()
    for copy in corners:
        copy.wait()
    strip_index = lax.axis_index("strip")
    near = row_ref.shape[0]
    lane = lax.broadcasted_iota(jnp.int32, (NOTE_ROWS, columns), 1)
    note = jnp.zeros((NOTE_ROWS, columns), F32)
    for position in range(near):
        inside = row_ref[position] - (strip_index - REACH) * strip_rows
        inside = lax.rem(inside + 2 * total_rows, total_rows)
        ahead = 2 * REACH - lax.div(inside, strip_rows) - REACH
        to_owner = jnp.where(ahead < 0, -REACH, jnp.where(ahead == REACH, 1, 0))
        first_row = inside + (to_owner + 1 - REACH) * strip_rows
        for place, value in enumerate((first_row, col_ref[position], to_owner)):
            note = jnp.where(lane == place * near + position, value.astype(F32), note)
    note = note.astype(BF16)
    block_ref[2 * half :, :] = note
    note_ref[...] = note
    for copy in bulk:
        copy.wait()


def phase_kernel(note_ref, phase_ref, far_ref, cos_ref, sin_ref):
    far_ref[...] = note_ref[...]
    cos_ref[...] = jnp.cos(phase_ref[...])
    sin_ref[...] = jnp.sin(phase_ref[...])


def strips_around(first_ref, own, second_ref):
    even = lax.rem(lax.axis_index("strip"), 2) == 0
    first, second = first_ref[...], second_ref[...]
    return jnp.where(even, first, second), own, jnp.where(even, second, first)


def corners_here(rows, far, own, below, near):
    found = []
    for note, owner in zip((far, own, below), OWNERS):
        note = note[note.shape[0] - NOTE_ROWS :, :].astype(F32)[0:1]
        for position in range(near):
            here = note[:, 2 * near + position : 2 * near + position + 1] == owner
            first_row = note[:, position : position + 1]
            first_col = note[:, near + position : near + position + 1]
            found.append((jnp.where(here, 1.0, 0.0), first_row, first_col))
    return found


def count_kernel(rows, near, far_ref, note_ref, second_ref, first_ref, out_ref):
    even = lax.rem(lax.axis_index("strip"), 2) == 0
    below = jnp.where(even, second_ref[...], first_ref[...])
    found = corners_here(rows, far_ref[...], note_ref[...], below, near)
    out_ref[0] = jnp.sum(sum(here for here, _, _ in found)).astype(jnp.int32)


def cut_kernel(
    rows, near, packed, far_ref, note_ref, object_ref, direction_ref, second_ref, first_ref, out_ref, start_ref
):
    targets, parts, size, wide = out_ref.shape
    columns = object_ref.shape[1]
    own = jnp.concatenate([object_ref[...], direction_ref[...], note_ref[...]], axis=0)
    above, own, below = strips_around(first_ref, own, second_ref)
    found = corners_here(rows, far_ref[...], own, below, near)
    nowhere = 4.0 * rows
    if packed:
        slots = targets // 2
        starts = [[nowhere, 0.0] for _ in range(slots)]
        rank = jnp.zeros((1, 1), F32)
        for here, first_row, first_col in found:
            for slot in range(slots):
                taken = here * jnp.where(rank == slot, 1.0, 0.0) > 0.0
                starts[slot][0] = jnp.where(taken, first_row, starts[slot][0])
                starts[slot][1] = jnp.where(taken, first_col, starts[slot][1])
            rank += here
    else:
        slots = len(found)
        starts = [[jnp.where(here > 0.0, row, nowhere), col] for here, row, col in found]
    hots = []
    for slot, (first_row, first_col) in enumerate(starts):
        start_ref[2 * slot : 2 * slot + 1, :] = jnp.broadcast_to(first_row, (1, 128))
        start_ref[2 * slot + 1 : 2 * slot + 2, :] = jnp.broadcast_to(first_col, (1, 128))
        hots.append((row_hot(first_row, wide, 3 * rows), col_hot(first_col, columns, wide)))
    bands = [
        jnp.concatenate(
            [block[part * rows : (part + 1) * rows, :] for block in (above, own, below)], axis=0
        )
        for part in range(parts)
    ]
    pick_rows = jnp.concatenate([hot for hot, _ in hots], axis=0)
    picked = [dot(pick_rows, band).astype(BF16) for band in bands]
    for slot in range(slots):
        lines = [part[slot * wide : (slot + 1) * wide] for part in picked]
        window = dot(jnp.concatenate(lines, axis=0), hots[slot][1]).astype(BF16).reshape(parts, wide, wide)
        if packed:
            out_ref[2 * slot] = window[:, :size]
            out_ref[2 * slot + 1] = window[:, size:]
        else:
            out_ref[slot] = window
    if not packed:
        out_ref[slots:] = jnp.zeros((targets - slots, parts, size, wide), BF16)


def chain_kernel(unit, window_ref, other_ref, probe_ref, cos_ref, sin_ref, plus_ref, minus_ref, out_ref, wave_ref):
    slices, _, rows_out, size = out_ref.shape
    packed = rows_out < size
    plus, minus = plus_ref[...], minus_ref[...]

    even = lax.rem(lax.axis_index("cuts"), 2) == 0

    def window(layer, part):
        mine = window_ref[layer, part].astype(F32)
        if not packed:
            return mine
        other = other_ref[layer, part].astype(F32)
        return jnp.concatenate([jnp.where(even, mine, other), jnp.where(even, other, mine)], axis=0)

    def kept(values):
        return jnp.where(even, values[:rows_out], values[rows_out:]) if packed else values

    def swap(values, waves):
        blocks = [[values[i * size : (i + 1) * size, j * size : (j + 1) * size]
                   for j in range(values.shape[1] // size)] for i in range(values.shape[0] // size)]
        turned = [jnp.concatenate([row[j] for row in blocks], axis=1) for j in range(len(blocks[0]))]
        return jnp.concatenate(turned, axis=0) if len(turned) > 1 else turned[0]

    def forward(columns):
        half = dot(plus, columns.astype(BF16)).astype(BF16)
        return dot(swap(half, None), minus)

    def inverse(rows):
        half = dot(rows.astype(BF16), plus).astype(BF16)
        return dot(minus, swap(half, None))

    def kernel_times(rows, sign, scale):
        kernel_cos, kernel_sin = cos_ref[...] * scale, sin_ref[...] * (sign * scale)
        made = []
        for i in range(rows.shape[0] // size):
            re, im = rows[i * size : (i + 1) * size, :size], rows[i * size : (i + 1) * size, size:]
            made.append(jnp.concatenate(
                [re * kernel_cos - im * kernel_sin, re * kernel_sin + im * kernel_cos], axis=1))
        return jnp.concatenate(made, axis=0) if len(made) > 1 else made[0]

    psi_re, psi_im = probe_ref[0].astype(F32), probe_ref[1].astype(F32)
    tan_re, tan_im = None, None
    far_scale = 1.0 / unit**2
    hop_scale = 1.0 / unit**4
    for layer in range(slices):
        wave_ref[layer, 0], wave_ref[layer, 1] = psi_re, psi_im
        obj_re, obj_im = window(layer, 0), window(layer, 1)
        dir_re, dir_im = window(layer, 2), window(layer, 3)
        exit_re = obj_re * psi_re - obj_im * psi_im
        exit_im = obj_re * psi_im + obj_im * psi_re
        delta_re = dir_re * psi_re - dir_im * psi_im
        delta_im = dir_re * psi_im + dir_im * psi_re
        if layer > 0:
            delta_re += obj_re * tan_re - obj_im * tan_im
            delta_im += obj_re * tan_im + obj_im * tan_re
        columns = jnp.concatenate([
            jnp.concatenate([exit_re, delta_re], axis=1),
            jnp.concatenate([exit_im, delta_im], axis=1)], axis=0)
        spectrum = forward(columns)
        if layer < slices - 1:
            waves = inverse(kernel_times(spectrum, 1.0, hop_scale))
            psi_re, tan_re = waves[:size, :size], waves[:size, size:]
            psi_im, tan_im = waves[size:, :size], waves[size:, size:]
        else:
            far = kernel_times(spectrum, 1.0, far_scale)
    far_re, far_im = far[:size, :size], far[:size, size:]
    weight = (4.0 / slices) * (far_re * far[size:, :size] + far_im * far[size:, size:])
    back = jnp.concatenate([weight * far_re, weight * far_im], axis=1)
    adjoint = inverse(kernel_times(back, -1.0, far_scale))
    for layer in range(slices - 1, -1, -1):
        adj_re, adj_im = adjoint[:size], adjoint[size:]
        psi_re, psi_im = wave_ref[layer, 0], wave_ref[layer, 1]
        psi_re, psi_im = kept(psi_re), kept(psi_im)
        out_re, out_im = kept(adj_re), kept(adj_im)
        out_ref[layer, 0] = (psi_re * out_re + psi_im * out_im).astype(BF16)
        out_ref[layer, 1] = (psi_re * out_im - psi_im * out_re).astype(BF16)
        if layer > 0:
            obj_re, obj_im = window(layer, 0), window(layer, 1)
            columns = jnp.concatenate(
                [obj_re * adj_re + obj_im * adj_im, obj_re * adj_im - obj_im * adj_re], axis=0)
            adjoint = inverse(kernel_times(forward(columns), -1.0, hop_scale))


def gather_kernel(slots, start_ref, grad_ref, first_ref, own_ref, second_ref):
    senders, parts, rows_in, size = grad_ref.shape
    packed = rows_in < size
    slots = senders // 2 if packed else slots
    rows, columns = own_ref.shape[1:]
    even = lax.rem(lax.axis_index("strip"), 2) == 0
    placed = [[] for _ in range(parts)]
    hots = []
    for slot in range(slots):
        first_row = start_ref[2 * slot : 2 * slot + 1, 0:1]
        first_col = start_ref[2 * slot + 1 : 2 * slot + 2, 0:1]
        hots.append(col_hot(first_row, 3 * rows, size))
        if packed:
            halves = [grad_ref[2 * slot + core, part] for part in range(parts) for core in range(2)]
            values = jnp.concatenate(halves, axis=0)
        else:
            values = grad_ref[slot].reshape(parts * size, size)
        spread = dot(values, row_hot(first_col, size, columns)).astype(BF16)
        for part in range(parts):
            placed[part].append(spread[part * size : (part + 1) * size])
    pick_rows = jnp.concatenate(hots, axis=1)
    for part in range(parts):
        total = dot(pick_rows, jnp.concatenate(placed[part], axis=0))
        above, below = total[:rows].astype(BF16), total[2 * rows :].astype(BF16)
        own_ref[part] = total[rows : 2 * rows]
        first_ref[part] = jnp.where(even, above, below)
        second_ref[part] = jnp.where(even, below, above)


def on_device(object_slices, direction, probe_wave, kernel_phase, corner_row, corner_col):
    strip_rows = object_slices.shape[2]
    column_count = object_slices.shape[3]
    patch_size = probe_wave.shape[1]
    strip_count = lax.axis_size("strip")
    cuts_count = lax.axis_size("cuts")
    plus, minus, unit = transform_tables(patch_size)

    def exchanged(block, offset):
        route = [(i, ((i - offset) ^ 1) + offset) for i in range(strip_count)]
        return lax.ppermute(block, "strip", [(i, j % strip_count) for i, j in route])

    vmem = pl.BlockSpec(memory_space=pltpu.VMEM)
    params = pltpu.CompilerParams(vmem_limit_bytes=32 * 1024 * 1024)

    block_rows = 4 * strip_rows + NOTE_ROWS
    hbm = pl.BlockSpec(memory_space=pl.ANY)
    wide = pltpu.CompilerParams(vmem_limit_bytes=60 * 1024 * 1024)
    objects = object_slices.reshape(-1, column_count)
    directions = direction.reshape(-1, column_count)
    block, note = pl.pallas_call(
        functools.partial(pack_kernel, strip_rows, strip_count * strip_rows),
        out_shape=(
            jax.ShapeDtypeStruct((block_rows, column_count), BF16),
            jax.ShapeDtypeStruct((NOTE_ROWS, column_count), BF16),
        ),
        in_specs=[hbm] * 4,
        out_specs=(vmem, vmem),
        scratch_shapes=[
            pltpu.SMEM(corner_row.shape, jnp.int32),
            pltpu.SMEM(corner_row.shape, jnp.int32),
            pltpu.SemaphoreType.DMA((4,)),
        ],
        compiler_params=wide,
        name="pack_block",
    )(corner_row, corner_col, objects, directions)
    far = lax.ppermute(note, "strip", [(i, (i + REACH) % strip_count) for i in range(strip_count)])
    first, second = exchanged(block, -1), exchanged(block, 0)
    far, kernel_cos, kernel_sin = pl.pallas_call(
        phase_kernel,
        out_shape=(
            jax.ShapeDtypeStruct(note.shape, BF16),
            jax.ShapeDtypeStruct(kernel_phase.shape, F32),
            jax.ShapeDtypeStruct(kernel_phase.shape, F32),
        ),
        in_specs=[vmem] * 2,
        out_specs=(vmem,) * 3,
        compiler_params=params,
        cost_estimate=pl.CostEstimate(flops=20_000_000_000, bytes_accessed=100_000_000, transcendentals=0),
        name="phase_tables",
    )(far, kernel_phase)
    near = corner_row.shape[0]
    strip_shape = (2, strip_rows, column_count)

    def work(packed, far, note, objects, directions, first, second, probe_wave, kernel_cos, kernel_sin, plus, minus):
        rows_sent = patch_size // 2 if packed else patch_size
        windows, start = pl.pallas_call(
            functools.partial(cut_kernel, strip_rows, near, packed),
            out_shape=(
                jax.ShapeDtypeStruct((cuts_count, 4, rows_sent, patch_size), BF16),
                jax.ShapeDtypeStruct((2 * cuts_count, 128), F32),
            ),
            in_specs=[vmem] * 6,
            out_specs=(vmem, vmem),
            compiler_params=params,
            name="cut_windows",
        )(far, note, objects, directions, second, first)
        other = windows = lax.all_to_all(windows, "cuts", 0, 0, tiled=False)
        if packed:
            other = lax.ppermute(windows, "cuts", [(i, i ^ 1) for i in range(cuts_count)])
        gradient = pl.pallas_call(
            functools.partial(chain_kernel, unit),
            out_shape=jax.ShapeDtypeStruct((cuts_count, 2, rows_sent, patch_size), BF16),
            in_specs=[vmem] * 7,
            out_specs=vmem,
            scratch_shapes=[pltpu.VMEM((cuts_count, 2, patch_size, patch_size), F32)],
            compiler_params=params,
            name="wave_chain",
        )(windows, other, probe_wave, kernel_cos, kernel_sin, plus, minus)
        gradient = lax.all_to_all(gradient, "cuts", 0, 0, tiled=False)
        return pl.pallas_call(
            functools.partial(gather_kernel, len(OWNERS) * near),
            out_shape=(
                jax.ShapeDtypeStruct(strip_shape, BF16),
                jax.ShapeDtypeStruct(strip_shape, F32),
                jax.ShapeDtypeStruct(strip_shape, BF16),
            ),
            in_specs=[vmem, vmem],
            out_specs=(vmem, vmem, vmem),
            compiler_params=params,
            name="add_windows",
        )(start, gradient)

    count = pl.pallas_call(
        functools.partial(count_kernel, strip_rows, near),
        out_shape=jax.ShapeDtypeStruct((1,), jnp.int32),
        in_specs=[vmem] * 4,
        out_specs=pl.BlockSpec(memory_space=pltpu.SMEM),
        compiler_params=params,
        name="count_positions",
    )(far, note, second, first)
    first, own, second = lax.cond(
        count[0] > cuts_count // 2,
        functools.partial(work, False),
        functools.partial(work, True),
        far, note, objects, directions, first, second,
        probe_wave, kernel_cos, kernel_sin, jnp.asarray(plus), jnp.asarray(minus),
    )
    first, second = exchanged(first, -1), exchanged(second, 0)
    return (own + first.astype(F32) + second.astype(F32))[None]


def solution(mesh):
    in_specs = (
        P("cuts", None, "strip", None),
        P("cuts", None, "strip", None),
        P(),
        P(),
        P("strip"),
        P("strip"),
    )
    out_specs = P("cuts", None, "strip", None)
    return jax.shard_map(
        on_device, mesh=mesh, in_specs=in_specs, out_specs=out_specs, check_vma=False
    )
```

```python
import functools
import math

import jax
import jax.numpy as jnp
import ml_dtypes
import numpy as np
from jax import lax
from jax.experimental import pallas as pl
from jax.experimental.pallas import tpu as pltpu
from jax.sharding import PartitionSpec as P

REACH = 2
NOTE_ROWS = 16
OWNERS = (-REACH, -1, 0, 1)
PLACES = (
    ((2, 2), (2, 1), (2, 1), (2, -1), (2, -1)),
    ((1, 2), (1, 2), (2, 1), (2, -1), (2, -1)),
    ((1, 2), (1, 2), (0, 1), (1, -1), (1, -1)),
    ((-1, 2), (-1, 2), (-1, 1), (-1, 0), (0, -1)),
    ((-1, 2), (-1, 2), (-1, 1), (-1, 0), (-1, -1)),
)
STRETCH = 1.6236604965019064
BF16 = jnp.bfloat16
F32 = jnp.float32


def transform_tables(size):
    index_line = np.arange(size)
    angle = (index_line[:, None] * index_line[None, :] % size) * (2.0 * math.pi / size)
    cosine, sine = np.cos(angle), np.sin(angle)
    kept_cos = (STRETCH * cosine).astype(ml_dtypes.bfloat16).astype(np.float64)
    kept_sin = (STRETCH * sine).astype(ml_dtypes.bfloat16).astype(np.float64)
    unit = np.sum(kept_cos * cosine + kept_sin * sine) / np.sum(cosine**2 + sine**2)
    unit = unit * math.sqrt(size)
    plus = np.block([[kept_cos, kept_sin], [-kept_sin, kept_cos]])
    minus = np.block([[kept_cos, -kept_sin], [kept_sin, kept_cos]])
    return plus.astype(ml_dtypes.bfloat16), minus.astype(ml_dtypes.bfloat16), unit


def dot(left, right):
    return jnp.dot(left, right, preferred_element_type=F32)


def row_hot(start, rows, columns):
    row_index = lax.broadcasted_iota(jnp.int32, (rows, columns), 0)
    col_index = lax.broadcasted_iota(jnp.int32, (rows, columns), 1)
    return jnp.where((col_index - row_index).astype(F32) == start, 1.0, 0.0).astype(BF16)


def col_hot(start, rows, columns):
    row_index = lax.broadcasted_iota(jnp.int32, (rows, columns), 0)
    col_index = lax.broadcasted_iota(jnp.int32, (rows, columns), 1)
    return jnp.where((row_index - col_index).astype(F32) == start, 1.0, 0.0).astype(BF16)


def pack_kernel(
    strip_rows, total_rows, row_any, col_any, object_any, direction_any, block_ref, note_ref, row_ref, col_ref, sems
):
    half = object_any.shape[0]
    columns = block_ref.shape[1]
    corners = [
        pltpu.make_async_copy(row_any, row_ref, sems.at[0]),
        pltpu.make_async_copy(col_any, col_ref, sems.at[1]),
    ]
    bulk = [
        pltpu.make_async_copy(object_any, block_ref.at[pl.ds(0, half), :], sems.at[2]),
        pltpu.make_async_copy(direction_any, block_ref.at[pl.ds(half, half), :], sems.at[3]),
    ]
    for copy in corners + bulk:
        copy.start()
    for copy in corners:
        copy.wait()
    strip_index = lax.axis_index("strip")
    near = row_ref.shape[0]
    insides, aheads = [], []
    for position in range(near):
        inside = row_ref[position] - (strip_index - REACH) * strip_rows
        inside = lax.rem(inside + 2 * total_rows, total_rows)
        insides.append(inside)
        aheads.append(REACH - lax.div(inside, strip_rows))
    lane = lax.broadcasted_iota(jnp.int32, (NOTE_ROWS, columns), 1)
    note = jnp.zeros((NOTE_ROWS, columns), F32)
    for position in range(near):
        to_owner = jnp.int32(0)
        for row, places in enumerate(PLACES):
            for column, place in enumerate(places):
                chosen = (aheads[0] == row - REACH) & (aheads[1] == column - REACH)
                to_owner = jnp.where(chosen, -place[position], to_owner)
        first_row = insides[position] + (to_owner + 1 - REACH) * strip_rows
        for place, value in enumerate((first_row, col_ref[position], to_owner)):
            note = jnp.where(lane == place * near + position, value.astype(F32), note)
    note = note.astype(BF16)
    block_ref[2 * half :, :] = note
    note_ref[...] = note
    for copy in bulk:
        copy.wait()


def phase_kernel(note_ref, phase_ref, far_ref, cos_ref, sin_ref):
    far_ref[...] = note_ref[...]
    cos_ref[...] = jnp.cos(phase_ref[...])
    sin_ref[...] = jnp.sin(phase_ref[...])


def strips_around(first_ref, own, second_ref):
    even = lax.rem(lax.axis_index("strip"), 2) == 0
    first, second = first_ref[...], second_ref[...]
    return jnp.where(even, first, second), own, jnp.where(even, second, first)


def corners_here(far, above, own, below, near):
    found = []
    for note, owner in zip((far, above, own, below), OWNERS):
        note = note[note.shape[0] - NOTE_ROWS :, :].astype(F32)[0:1]
        for position in range(near):
            here = note[:, 2 * near + position : 2 * near + position + 1] == owner
            first_row = note[:, position : position + 1]
            first_col = note[:, near + position : near + position + 1]
            found.append((jnp.where(here, 1.0, 0.0), first_row, first_col))
    return found


def cut_kernel(
    rows, near, far_ref, note_ref, object_ref, direction_ref, second_ref, first_ref, out_ref, start_ref, *count_ref
):
    targets, parts, size, _ = out_ref.shape
    columns = object_ref.shape[1]
    own = jnp.concatenate([object_ref[...], direction_ref[...], note_ref[...]], axis=0)
    above, own, below = strips_around(first_ref, own, second_ref)
    found = corners_here(far_ref[...], above, own, below, near)
    nowhere = 4.0 * rows
    if count_ref:
        slots = targets
        count_ref[0][0] = jnp.sum(sum(here for here, _, _ in found)).astype(jnp.int32)
        starts = [[nowhere, 0.0] for _ in range(slots)]
        rank = jnp.zeros((1, 1), F32)
        for here, first_row, first_col in found:
            for slot in range(slots):
                taken = here * jnp.where(rank == slot, 1.0, 0.0) > 0.0
                starts[slot][0] = jnp.where(taken, first_row, starts[slot][0])
                starts[slot][1] = jnp.where(taken, first_col, starts[slot][1])
            rank += here
    else:
        slots = len(found)
        starts = [[jnp.where(here > 0.0, row, nowhere), col] for here, row, col in found]
    hots = []
    for slot, (first_row, first_col) in enumerate(starts):
        start_ref[2 * slot : 2 * slot + 1, :] = jnp.broadcast_to(first_row, (1, 128))
        start_ref[2 * slot + 1 : 2 * slot + 2, :] = jnp.broadcast_to(first_col, (1, 128))
        hots.append((row_hot(first_row, size, 3 * rows), col_hot(first_col, columns, size)))
    bands = [
        jnp.concatenate(
            [block[part * rows : (part + 1) * rows, :] for block in (above, own, below)], axis=0
        )
        for part in range(parts)
    ]
    pick_rows = jnp.concatenate([hot for hot, _ in hots], axis=0)
    picked = [dot(pick_rows, band).astype(BF16) for band in bands]
    for slot in range(slots):
        lines = [part[slot * size : (slot + 1) * size] for part in picked]
        window = dot(jnp.concatenate(lines, axis=0), hots[slot][1]).astype(BF16)
        out_ref[slot] = window.reshape(parts, size, size)
    if slots < targets:
        out_ref[slots:] = jnp.zeros((targets - slots, parts, size, size), BF16)


def chain_kernel(unit, window_ref, other_ref, probe_ref, cos_ref, sin_ref, plus_ref, minus_ref, out_ref, wave_ref):
    slices, _, size, _ = wave_ref.shape
    packed = window_ref.shape[0] < slices
    plus, minus = plus_ref[...], minus_ref[...]
    even = lax.rem(lax.axis_index("cuts"), 2) == 0

    def window(layer, part):
        if not packed:
            return window_ref[layer, part].astype(F32)
        mine, other = window_ref[layer // 2, part], other_ref[layer // 2, part]
        return (jnp.where(even, mine, other) if layer % 2 == 0 else jnp.where(even, other, mine)).astype(F32)

    def swap(values, waves):
        blocks = [[values[i * size : (i + 1) * size, j * size : (j + 1) * size]
                   for j in range(values.shape[1] // size)] for i in range(values.shape[0] // size)]
        turned = [jnp.concatenate([row[j] for row in blocks], axis=1) for j in range(len(blocks[0]))]
        return jnp.concatenate(turned, axis=0) if len(turned) > 1 else turned[0]

    def forward(columns):
        half = dot(plus, columns.astype(BF16)).astype(BF16)
        return dot(swap(half, None), minus)

    def inverse(rows):
        half = dot(rows.astype(BF16), plus).astype(BF16)
        return dot(minus, swap(half, None))

    def kernel_times(rows, sign, scale):
        kernel_cos, kernel_sin = cos_ref[...] * scale, sin_ref[...] * (sign * scale)
        made = []
        for i in range(rows.shape[0] // size):
            re, im = rows[i * size : (i + 1) * size, :size], rows[i * size : (i + 1) * size, size:]
            made.append(jnp.concatenate(
                [re * kernel_cos - im * kernel_sin, re * kernel_sin + im * kernel_cos], axis=1))
        return jnp.concatenate(made, axis=0) if len(made) > 1 else made[0]

    psi_re, psi_im = probe_ref[0].astype(F32), probe_ref[1].astype(F32)
    tan_re, tan_im = None, None
    far_scale = 1.0 / unit**2
    hop_scale = 1.0 / unit**4
    for layer in range(slices):
        wave_ref[layer, 0], wave_ref[layer, 1] = psi_re, psi_im
        obj_re, obj_im = window(layer, 0), window(layer, 1)
        dir_re, dir_im = window(layer, 2), window(layer, 3)
        exit_re = obj_re * psi_re - obj_im * psi_im
        exit_im = obj_re * psi_im + obj_im * psi_re
        delta_re = dir_re * psi_re - dir_im * psi_im
        delta_im = dir_re * psi_im + dir_im * psi_re
        if layer > 0:
            delta_re += obj_re * tan_re - obj_im * tan_im
            delta_im += obj_re * tan_im + obj_im * tan_re
        columns = jnp.concatenate([
            jnp.concatenate([exit_re, delta_re], axis=1),
            jnp.concatenate([exit_im, delta_im], axis=1)], axis=0)
        spectrum = forward(columns)
        if layer < slices - 1:
            waves = inverse(kernel_times(spectrum, 1.0, hop_scale))
            psi_re, tan_re = waves[:size, :size], waves[:size, size:]
            psi_im, tan_im = waves[size:, :size], waves[size:, size:]
        else:
            far = kernel_times(spectrum, 1.0, far_scale)
    far_re, far_im = far[:size, :size], far[:size, size:]
    weight = (4.0 / slices) * (far_re * far[size:, :size] + far_im * far[size:, size:])
    back = jnp.concatenate([weight * far_re, weight * far_im], axis=1)
    adjoint = inverse(kernel_times(back, -1.0, far_scale))
    for layer in range(slices - 1, -1, -1):
        adj_re, adj_im = adjoint[:size], adjoint[size:]
        psi_re, psi_im = wave_ref[layer, 0], wave_ref[layer, 1]
        later = grad if layer < slices - 1 else None
        grad = [(psi_re * adj_re + psi_im * adj_im).astype(BF16), (psi_re * adj_im - psi_im * adj_re).astype(BF16)]
        for part in range(2):
            if not packed:
                out_ref[layer, part] = grad[part]
            elif layer % 2 == 0:
                out_ref[layer // 2, part] = jnp.where(even, grad[part], later[part])
        if layer > 0:
            obj_re, obj_im = window(layer, 0), window(layer, 1)
            columns = jnp.concatenate(
                [obj_re * adj_re + obj_im * adj_im, obj_re * adj_im - obj_im * adj_re], axis=0)
            adjoint = inverse(kernel_times(forward(columns), -1.0, hop_scale))


def gather_kernel(most, start_ref, grad_ref, first_ref, own_ref, second_ref):
    slots, parts, size, _ = grad_ref.shape
    slots = min(slots, most)
    rows, columns = own_ref.shape[1:]
    even = lax.rem(lax.axis_index("strip"), 2) == 0
    placed = [[] for _ in range(parts)]
    hots = []
    for slot in range(slots):
        first_row = start_ref[2 * slot : 2 * slot + 1, 0:1]
        first_col = start_ref[2 * slot + 1 : 2 * slot + 2, 0:1]
        hots.append(col_hot(first_row, 3 * rows, size))
        values = grad_ref[slot].reshape(parts * size, size)
        spread = dot(values, row_hot(first_col, size, columns)).astype(BF16)
        for part in range(parts):
            placed[part].append(spread[part * size : (part + 1) * size])
    pick_rows = jnp.concatenate(hots, axis=1)
    for part in range(parts):
        total = dot(pick_rows, jnp.concatenate(placed[part], axis=0))
        above, below = total[:rows].astype(BF16), total[2 * rows :].astype(BF16)
        own_ref[part] = total[rows : 2 * rows]
        first_ref[part] = jnp.where(even, above, below)
        second_ref[part] = jnp.where(even, below, above)


def on_device(object_slices, direction, probe_wave, kernel_phase, corner_row, corner_col):
    strip_rows = object_slices.shape[2]
    column_count = object_slices.shape[3]
    patch_size = probe_wave.shape[1]
    strip_count = lax.axis_size("strip")
    cuts_count = lax.axis_size("cuts")
    plus, minus, unit = transform_tables(patch_size)

    def exchanged(block, offset):
        route = [(i, ((i - offset) ^ 1) + offset) for i in range(strip_count)]
        return lax.ppermute(block, "strip", [(i, j % strip_count) for i, j in route])

    vmem = pl.BlockSpec(memory_space=pltpu.VMEM)
    params = pltpu.CompilerParams(vmem_limit_bytes=32 * 1024 * 1024)

    block_rows = 4 * strip_rows + NOTE_ROWS
    hbm = pl.BlockSpec(memory_space=pl.ANY)
    wide = pltpu.CompilerParams(vmem_limit_bytes=60 * 1024 * 1024)
    objects = object_slices.reshape(-1, column_count)
    directions = direction.reshape(-1, column_count)
    block, note = pl.pallas_call(
        functools.partial(pack_kernel, strip_rows, strip_count * strip_rows),
        out_shape=(
            jax.ShapeDtypeStruct((block_rows, column_count), BF16),
            jax.ShapeDtypeStruct((NOTE_ROWS, column_count), BF16),
        ),
        in_specs=[hbm] * 4,
        out_specs=(vmem, vmem),
        scratch_shapes=[
            pltpu.SMEM(corner_row.shape, jnp.int32),
            pltpu.SMEM(corner_row.shape, jnp.int32),
            pltpu.SemaphoreType.DMA((4,)),
        ],
        compiler_params=wide,
        name="pack_block",
    )(corner_row, corner_col, objects, directions)
    far = lax.ppermute(note, "strip", [(i, (i + REACH) % strip_count) for i in range(strip_count)])
    first, second = exchanged(block, -1), exchanged(block, 0)
    far, kernel_cos, kernel_sin = pl.pallas_call(
        phase_kernel,
        out_shape=(
            jax.ShapeDtypeStruct(note.shape, BF16),
            jax.ShapeDtypeStruct(kernel_phase.shape, F32),
            jax.ShapeDtypeStruct(kernel_phase.shape, F32),
        ),
        in_specs=[vmem] * 2,
        out_specs=(vmem,) * 3,
        compiler_params=params,
        cost_estimate=pl.CostEstimate(flops=20_000_000_000, bytes_accessed=100_000_000, transcendentals=0),
        name="phase_tables",
    )(far, kernel_phase)
    near = corner_row.shape[0]
    strip_shape = (2, strip_rows, column_count)

    chips = cuts_count // 2
    same_core = [[core + 2 * chip for chip in range(chips)] for core in range(2)]

    def cut(targets, counted, *operands):
        windows_shape = (targets, 4, patch_size, patch_size)
        out_shape = (jax.ShapeDtypeStruct(windows_shape, BF16), jax.ShapeDtypeStruct((2 * targets, 128), F32))
        out_specs = (vmem, vmem)
        if counted:
            out_shape += (jax.ShapeDtypeStruct((1,), jnp.int32),)
            out_specs += (pl.BlockSpec(memory_space=pltpu.SMEM),)
        return pl.pallas_call(
            functools.partial(cut_kernel, strip_rows, near),
            out_shape=out_shape,
            in_specs=[vmem] * 6,
            out_specs=out_specs,
            compiler_params=params,
            name="cut_windows",
        )(*operands)

    def chain(windows, other, probe_wave, *tables):
        return pl.pallas_call(
            functools.partial(chain_kernel, unit),
            out_shape=jax.ShapeDtypeStruct((windows.shape[0], 2, patch_size, patch_size), BF16),
            in_specs=[vmem] * 7,
            out_specs=vmem,
            scratch_shapes=[pltpu.VMEM((cuts_count, 2, patch_size, patch_size), F32)],
            compiler_params=params,
            name="wave_chain",
        )(windows, other, probe_wave, *tables)

    def gather(start, gradient):
        return pl.pallas_call(
            functools.partial(gather_kernel, len(OWNERS) * near),
            out_shape=(
                jax.ShapeDtypeStruct(strip_shape, BF16),
                jax.ShapeDtypeStruct(strip_shape, F32),
                jax.ShapeDtypeStruct(strip_shape, BF16),
            ),
            in_specs=[vmem, vmem],
            out_specs=(vmem, vmem, vmem),
            compiler_params=params,
            name="add_windows",
        )(start, gradient)

    def one_per_chip(windows, start, around, constants):
        del around
        windows = lax.all_to_all(windows, "cuts", 0, 0, axis_index_groups=same_core, tiled=False)
        other = lax.ppermute(windows, "cuts", [(i, i ^ 1) for i in range(cuts_count)])
        gradient = chain(windows, other, *constants)
        gradient = lax.all_to_all(gradient, "cuts", 0, 0, axis_index_groups=same_core, tiled=False)
        return gather(start, gradient)

    def one_per_device(windows, start, around, constants):
        del windows, start
        windows, start = cut(cuts_count, False, *around)
        windows = lax.all_to_all(windows, "cuts", 0, 0, tiled=False)
        gradient = chain(windows, windows, *constants)
        gradient = lax.all_to_all(gradient, "cuts", 0, 0, tiled=False)
        return gather(start, gradient)

    around = (far, note, objects, directions, second, first)
    windows, start, count = cut(chips, True, *around)
    constants = (probe_wave, kernel_cos, kernel_sin, jnp.asarray(plus), jnp.asarray(minus))
    first, own, second = lax.cond(
        count[0] > chips, one_per_device, one_per_chip, windows, start, around, constants
    )
    first, second = exchanged(first, -1), exchanged(second, 0)
    return (own + first.astype(F32) + second.astype(F32))[None]


def solution(mesh):
    in_specs = (
        P("cuts", None, "strip", None),
        P("cuts", None, "strip", None),
        P(),
        P(),
        P("strip"),
        P("strip"),
    )
    out_specs = P("cuts", None, "strip", None)
    return jax.shard_map(
        on_device, mesh=mesh, in_specs=in_specs, out_specs=out_specs, check_vma=False
    )
```

```python
import functools
import math

import jax
import jax.numpy as jnp
import ml_dtypes
import numpy as np
from jax import lax
from jax.experimental import pallas as pl
from jax.experimental.pallas import tpu as pltpu
from jax.sharding import PartitionSpec as P

REACH = 2
NOTE_ROWS = 16
OWNERS = (-REACH, -1, 0, 1)
PLACES = (
    ((2, 2), (2, 1), (2, 1), (2, -1), (2, -1)),
    ((1, 2), (1, 2), (2, 1), (2, -1), (2, -1)),
    ((1, 2), (1, 2), (0, 1), (1, -1), (1, -1)),
    ((-1, 2), (-1, 2), (-1, 1), (-1, 0), (0, -1)),
    ((-1, 2), (-1, 2), (-1, 1), (-1, 0), (-1, -1)),
)
STRETCH = 1.6236604965019064
BF16 = jnp.bfloat16
F32 = jnp.float32


def transform_tables(size):
    index_line = np.arange(size)
    angle = (index_line[:, None] * index_line[None, :] % size) * (2.0 * math.pi / size)
    cosine, sine = np.cos(angle), np.sin(angle)
    kept_cos = (STRETCH * cosine).astype(ml_dtypes.bfloat16).astype(np.float64)
    kept_sin = (STRETCH * sine).astype(ml_dtypes.bfloat16).astype(np.float64)
    unit = np.sum(kept_cos * cosine + kept_sin * sine) / np.sum(cosine**2 + sine**2)
    unit = unit * math.sqrt(size)
    plus = np.block([[kept_cos, kept_sin], [-kept_sin, kept_cos]])
    minus = np.block([[kept_cos, -kept_sin], [kept_sin, kept_cos]])
    return plus.astype(ml_dtypes.bfloat16), minus.astype(ml_dtypes.bfloat16), unit


def dot(left, right):
    return jnp.dot(left, right, preferred_element_type=F32)


def row_hot(start, rows, columns):
    row_index = lax.broadcasted_iota(jnp.int32, (rows, columns), 0)
    col_index = lax.broadcasted_iota(jnp.int32, (rows, columns), 1)
    return jnp.where((col_index - row_index).astype(F32) == start, 1.0, 0.0).astype(BF16)


def col_hot(start, rows, columns):
    row_index = lax.broadcasted_iota(jnp.int32, (rows, columns), 0)
    col_index = lax.broadcasted_iota(jnp.int32, (rows, columns), 1)
    return jnp.where((row_index - col_index).astype(F32) == start, 1.0, 0.0).astype(BF16)


def pack_kernel(
    strip_rows, total_rows, row_any, col_any, object_any, direction_any, block_ref, note_ref, row_ref, col_ref, sems
):
    half = object_any.shape[0]
    columns = block_ref.shape[1]
    corners = [
        pltpu.make_async_copy(row_any, row_ref, sems.at[0]),
        pltpu.make_async_copy(col_any, col_ref, sems.at[1]),
    ]
    bulk = [
        pltpu.make_async_copy(object_any, block_ref.at[pl.ds(0, half), :], sems.at[2]),
        pltpu.make_async_copy(direction_any, block_ref.at[pl.ds(half, half), :], sems.at[3]),
    ]
    for copy in corners + bulk:
        copy.start()
    for copy in corners:
        copy.wait()
    strip_index = lax.axis_index("strip")
    near = row_ref.shape[0]
    insides, aheads = [], []
    for position in range(near):
        inside = row_ref[position] - (strip_index - REACH) * strip_rows
        inside = lax.rem(inside + 2 * total_rows, total_rows)
        insides.append(inside)
        aheads.append(REACH - lax.div(inside, strip_rows))
    lane = lax.broadcasted_iota(jnp.int32, (NOTE_ROWS, columns), 1)
    note = jnp.zeros((NOTE_ROWS, columns), F32)
    for position in range(near):
        to_owner = jnp.int32(0)
        for row, places in enumerate(PLACES):
            for column, place in enumerate(places):
                chosen = (aheads[0] == row - REACH) & (aheads[1] == column - REACH)
                to_owner = jnp.where(chosen, -place[position], to_owner)
        first_row = insides[position] + (to_owner + 1 - REACH) * strip_rows
        for place, value in enumerate((first_row, col_ref[position], to_owner)):
            note = jnp.where(lane == place * near + position, value.astype(F32), note)
    note = note.astype(BF16)
    block_ref[2 * half :, :] = note
    note_ref[...] = note
    for copy in bulk:
        copy.wait()


def phase_kernel(phase_ref, cos_ref, sin_ref):
    cos_ref[...] = jnp.cos(phase_ref[...])
    sin_ref[...] = jnp.sin(phase_ref[...])


def strips_around(first_ref, own, second_ref):
    even = lax.rem(lax.axis_index("strip"), 2) == 0
    first, second = first_ref[...], second_ref[...]
    return jnp.where(even, first, second), own, jnp.where(even, second, first)


def corners_here(far, above, own, below, near):
    found = []
    for note, owner in zip((far, above, own, below), OWNERS):
        note = note[note.shape[0] - NOTE_ROWS :, :].astype(F32)[0:1]
        for position in range(near):
            here = note[:, 2 * near + position : 2 * near + position + 1] == owner
            first_row = note[:, position : position + 1]
            first_col = note[:, near + position : near + position + 1]
            found.append((jnp.where(here, 1.0, 0.0), first_row, first_col))
    return found


def cut_kernel(
    rows, near, far_ref, note_ref, object_ref, direction_ref, second_ref, first_ref, out_ref, start_ref, *count_ref
):
    targets, parts, size, _ = out_ref.shape
    columns = object_ref.shape[1]
    own = jnp.concatenate([object_ref[...], direction_ref[...], note_ref[...]], axis=0)
    above, own, below = strips_around(first_ref, own, second_ref)
    found = corners_here(far_ref[...], above, own, below, near)
    nowhere = 4.0 * rows
    if count_ref:
        slots = targets
        count_ref[0][0] = jnp.sum(sum(here for here, _, _ in found)).astype(jnp.int32)
        starts = [[nowhere, 0.0] for _ in range(slots)]
        rank = jnp.zeros((1, 1), F32)
        for here, first_row, first_col in found:
            for slot in range(slots):
                taken = here * jnp.where(rank == slot, 1.0, 0.0) > 0.0
                starts[slot][0] = jnp.where(taken, first_row, starts[slot][0])
                starts[slot][1] = jnp.where(taken, first_col, starts[slot][1])
            rank += here
    else:
        slots = len(found)
        starts = [[jnp.where(here > 0.0, row, nowhere), col] for here, row, col in found]
    hots = []
    for slot, (first_row, first_col) in enumerate(starts):
        start_ref[2 * slot : 2 * slot + 1, :] = jnp.broadcast_to(first_row, (1, 128))
        start_ref[2 * slot + 1 : 2 * slot + 2, :] = jnp.broadcast_to(first_col, (1, 128))
        hots.append((row_hot(first_row, size, 3 * rows), col_hot(first_col, columns, size)))
    bands = [
        jnp.concatenate(
            [block[part * rows : (part + 1) * rows, :] for block in (above, own, below)], axis=0
        )
        for part in range(parts)
    ]
    pick_rows = jnp.concatenate([hot for hot, _ in hots], axis=0)
    picked = [dot(pick_rows, band).astype(BF16) for band in bands]
    for slot in range(slots):
        lines = [part[slot * size : (slot + 1) * size] for part in picked]
        window = dot(jnp.concatenate(lines, axis=0), hots[slot][1]).astype(BF16)
        out_ref[slot] = window.reshape(parts, size, size)
    if slots < targets:
        out_ref[slots:] = jnp.zeros((targets - slots, parts, size, size), BF16)


def chain_kernel(unit, window_ref, other_ref, probe_ref, cos_ref, sin_ref, plus_ref, minus_ref, out_ref, wave_ref):
    slices, _, size, _ = wave_ref.shape
    packed = window_ref.shape[0] < slices
    plus, minus = plus_ref[...], minus_ref[...]
    even = lax.rem(lax.axis_index("cuts"), 2) == 0

    def window(layer, part):
        if not packed:
            return window_ref[layer, part].astype(F32)
        mine, other = window_ref[layer // 2, part], other_ref[layer // 2, part]
        return (jnp.where(even, mine, other) if layer % 2 == 0 else jnp.where(even, other, mine)).astype(F32)

    def swap(values):
        blocks = [[values[i * size : (i + 1) * size, j * size : (j + 1) * size]
                   for j in range(values.shape[1] // size)] for i in range(values.shape[0] // size)]
        turned = [jnp.concatenate([row[j] for row in blocks], axis=1) for j in range(len(blocks[0]))]
        return jnp.concatenate(turned, axis=0) if len(turned) > 1 else turned[0]

    def from_left(table, columns):
        return jnp.concatenate([dot(table[:size], columns), dot(table[size:], columns)], axis=0)

    def forward(columns):
        half = from_left(plus, columns.astype(BF16)).astype(BF16)
        return dot(swap(half), minus)

    def inverse(rows):
        half = dot(rows.astype(BF16), plus).astype(BF16)
        return from_left(minus, swap(half))

    def kernel_times(rows, sign, scale):
        kernel_cos, kernel_sin = cos_ref[...] * scale, sin_ref[...] * (sign * scale)
        made = []
        for i in range(rows.shape[0] // size):
            re, im = rows[i * size : (i + 1) * size, :size], rows[i * size : (i + 1) * size, size:]
            made.append(jnp.concatenate(
                [re * kernel_cos - im * kernel_sin, re * kernel_sin + im * kernel_cos], axis=1))
        return jnp.concatenate(made, axis=0) if len(made) > 1 else made[0]

    psi_re, psi_im = probe_ref[0].astype(F32), probe_ref[1].astype(F32)
    tan_re, tan_im = None, None
    far_scale = 1.0 / unit**2
    hop_scale = 1.0 / unit**4
    for layer in range(slices):
        wave_ref[layer, 0], wave_ref[layer, 1] = psi_re, psi_im
        obj_re, obj_im = window(layer, 0), window(layer, 1)
        dir_re, dir_im = window(layer, 2), window(layer, 3)
        exit_re = obj_re * psi_re - obj_im * psi_im
        exit_im = obj_re * psi_im + obj_im * psi_re
        delta_re = dir_re * psi_re - dir_im * psi_im
        delta_im = dir_re * psi_im + dir_im * psi_re
        if layer > 0:
            delta_re += obj_re * tan_re - obj_im * tan_im
            delta_im += obj_re * tan_im + obj_im * tan_re
        columns = jnp.concatenate([
            jnp.concatenate([exit_re, delta_re], axis=1),
            jnp.concatenate([exit_im, delta_im], axis=1)], axis=0)
        spectrum = forward(columns)
        if layer < slices - 1:
            waves = inverse(kernel_times(spectrum, 1.0, hop_scale))
            psi_re, tan_re = waves[:size, :size], waves[:size, size:]
            psi_im, tan_im = waves[size:, :size], waves[size:, size:]
        else:
            far = kernel_times(spectrum, 1.0, far_scale)
    far_re, far_im = far[:size, :size], far[:size, size:]
    weight = (4.0 / slices) * (far_re * far[size:, :size] + far_im * far[size:, size:])
    back = jnp.concatenate([weight * far_re, weight * far_im], axis=1)
    adjoint = inverse(kernel_times(back, -1.0, far_scale))
    for layer in range(slices - 1, -1, -1):
        adj_re, adj_im = adjoint[:size], adjoint[size:]
        psi_re, psi_im = wave_ref[layer, 0], wave_ref[layer, 1]
        later = grad if layer < slices - 1 else None
        grad = [(psi_re * adj_re + psi_im * adj_im).astype(BF16), (psi_re * adj_im - psi_im * adj_re).astype(BF16)]
        for part in range(2):
            if not packed:
                out_ref[layer, part] = grad[part]
            elif layer % 2 == 0:
                out_ref[layer // 2, part] = jnp.where(even, grad[part], later[part])
        if layer > 0:
            obj_re, obj_im = window(layer, 0), window(layer, 1)
            columns = jnp.concatenate(
                [obj_re * adj_re + obj_im * adj_im, obj_re * adj_im - obj_im * adj_re], axis=0)
            adjoint = inverse(kernel_times(forward(columns), -1.0, hop_scale))


def gather_kernel(most, start_ref, grad_ref, first_ref, own_ref, second_ref):
    slots, parts, size, _ = grad_ref.shape
    slots = min(slots, most)
    rows, columns = own_ref.shape[1:]
    even = lax.rem(lax.axis_index("strip"), 2) == 0
    placed = [[] for _ in range(parts)]
    hots = []
    for slot in range(slots):
        first_row = start_ref[2 * slot : 2 * slot + 1, 0:1]
        first_col = start_ref[2 * slot + 1 : 2 * slot + 2, 0:1]
        hots.append(col_hot(first_row, 3 * rows, size))
        values = grad_ref[slot].reshape(parts * size, size)
        spread = dot(values, row_hot(first_col, size, columns)).astype(BF16)
        for part in range(parts):
            placed[part].append(spread[part * size : (part + 1) * size])
    pick_rows = jnp.concatenate(hots, axis=1)
    for part in range(parts):
        total = dot(pick_rows, jnp.concatenate(placed[part], axis=0))
        above, below = total[:rows].astype(BF16), total[2 * rows :].astype(BF16)
        own_ref[part] = total[rows : 2 * rows]
        first_ref[part] = jnp.where(even, above, below)
        second_ref[part] = jnp.where(even, below, above)


def on_device(object_slices, direction, probe_wave, kernel_phase, corner_row, corner_col):
    strip_rows = object_slices.shape[2]
    column_count = object_slices.shape[3]
    patch_size = probe_wave.shape[1]
    strip_count = lax.axis_size("strip")
    cuts_count = lax.axis_size("cuts")
    plus, minus, unit = transform_tables(patch_size)

    def exchanged(block, offset):
        route = [(i, ((i - offset) ^ 1) + offset) for i in range(strip_count)]
        return lax.ppermute(block, "strip", [(i, j % strip_count) for i, j in route])

    vmem = pl.BlockSpec(memory_space=pltpu.VMEM)
    params = pltpu.CompilerParams(vmem_limit_bytes=32 * 1024 * 1024)

    block_rows = 4 * strip_rows + NOTE_ROWS
    hbm = pl.BlockSpec(memory_space=pl.ANY)
    wide = pltpu.CompilerParams(vmem_limit_bytes=60 * 1024 * 1024)
    objects = object_slices.reshape(-1, column_count)
    directions = direction.reshape(-1, column_count)
    block, note = pl.pallas_call(
        functools.partial(pack_kernel, strip_rows, strip_count * strip_rows),
        out_shape=(
            jax.ShapeDtypeStruct((block_rows, column_count), BF16),
            jax.ShapeDtypeStruct((NOTE_ROWS, column_count), BF16),
        ),
        in_specs=[hbm] * 4,
        out_specs=(vmem, vmem),
        scratch_shapes=[
            pltpu.SMEM(corner_row.shape, jnp.int32),
            pltpu.SMEM(corner_row.shape, jnp.int32),
            pltpu.SemaphoreType.DMA((4,)),
        ],
        compiler_params=wide,
        name="pack_block",
    )(corner_row, corner_col, objects, directions)
    far = lax.ppermute(note, "strip", [(i, (i + REACH) % strip_count) for i in range(strip_count)])
    first, second = exchanged(block, -1), exchanged(block, 0)
    kernel_cos, kernel_sin = pl.pallas_call(
        phase_kernel,
        out_shape=(jax.ShapeDtypeStruct(kernel_phase.shape, F32),) * 2,
        in_specs=[vmem],
        out_specs=(vmem,) * 2,
        compiler_params=params,
        name="phase_tables",
    )(kernel_phase)
    near = corner_row.shape[0]
    strip_shape = (2, strip_rows, column_count)

    chips = cuts_count // 2
    same_core = [[core + 2 * chip for chip in range(chips)] for core in range(2)]

    def cut(targets, counted, *operands):
        windows_shape = (targets, 4, patch_size, patch_size)
        out_shape = (jax.ShapeDtypeStruct(windows_shape, BF16), jax.ShapeDtypeStruct((2 * targets, 128), F32))
        out_specs = (vmem, vmem)
        if counted:
            out_shape += (jax.ShapeDtypeStruct((1,), jnp.int32),)
            out_specs += (pl.BlockSpec(memory_space=pltpu.SMEM),)
        return pl.pallas_call(
            functools.partial(cut_kernel, strip_rows, near),
            out_shape=out_shape,
            in_specs=[vmem] * 6,
            out_specs=out_specs,
            compiler_params=params,
            name="cut_windows",
        )(*operands)

    def chain(windows, other, probe_wave, *tables):
        return pl.pallas_call(
            functools.partial(chain_kernel, unit),
            out_shape=jax.ShapeDtypeStruct((windows.shape[0], 2, patch_size, patch_size), BF16),
            in_specs=[vmem] * 7,
            out_specs=vmem,
            scratch_shapes=[pltpu.VMEM((cuts_count, 2, patch_size, patch_size), F32)],
            compiler_params=params,
            name="wave_chain",
        )(windows, other, probe_wave, *tables)

    def gather(start, gradient):
        return pl.pallas_call(
            functools.partial(gather_kernel, len(OWNERS) * near),
            out_shape=(
                jax.ShapeDtypeStruct(strip_shape, BF16),
                jax.ShapeDtypeStruct(strip_shape, F32),
                jax.ShapeDtypeStruct(strip_shape, BF16),
            ),
            in_specs=[vmem, vmem],
            out_specs=(vmem, vmem, vmem),
            compiler_params=params,
            name="add_windows",
        )(start, gradient)

    def one_per_chip(windows, start, around, constants):
        del around
        windows = lax.all_to_all(windows, "cuts", 0, 0, axis_index_groups=same_core, tiled=False)
        other = lax.ppermute(windows, "cuts", [(i, i ^ 1) for i in range(cuts_count)])
        gradient = chain(windows, other, *constants)
        gradient = lax.all_to_all(gradient, "cuts", 0, 0, axis_index_groups=same_core, tiled=False)
        return gather(start, gradient)

    def one_per_device(windows, start, around, constants):
        del windows, start
        windows, start = cut(cuts_count, False, *around)
        windows = lax.all_to_all(windows, "cuts", 0, 0, tiled=False)
        gradient = chain(windows, windows, *constants)
        gradient = lax.all_to_all(gradient, "cuts", 0, 0, tiled=False)
        return gather(start, gradient)

    around = (far, note, objects, directions, second, first)
    windows, start, count = cut(chips, True, *around)
    constants = (probe_wave, kernel_cos, kernel_sin, jnp.asarray(plus), jnp.asarray(minus))
    first, own, second = lax.cond(
        count[0] > chips, one_per_device, one_per_chip, windows, start, around, constants
    )
    first, second = exchanged(first, -1), exchanged(second, 0)
    return (own + first.astype(F32) + second.astype(F32))[None]


def solution(mesh):
    in_specs = (
        P("cuts", None, "strip", None),
        P("cuts", None, "strip", None),
        P(),
        P(),
        P("strip"),
        P("strip"),
    )
    out_specs = P("cuts", None, "strip", None)
    return jax.shard_map(
        on_device, mesh=mesh, in_specs=in_specs, out_specs=out_specs, check_vma=False
    )
```

```python
import functools
import math

import jax
import jax.numpy as jnp
import ml_dtypes
import numpy as np
from jax import lax
from jax.experimental import pallas as pl
from jax.experimental.pallas import tpu as pltpu
from jax.sharding import PartitionSpec as P

REACH = 2
NOTE_ROWS = 16
OWNERS = (-REACH, -1, 0, 1)
PLACES = (
    ((2, 2), (2, 1), (2, 1), (2, -1), (2, -1)),
    ((1, 2), (1, 2), (2, 1), (2, -1), (2, -1)),
    ((1, 2), (1, 2), (0, 1), (1, -1), (1, -1)),
    ((-1, 2), (-1, 2), (-1, 1), (-1, 0), (0, -1)),
    ((-1, 2), (-1, 2), (-1, 1), (-1, 0), (-1, -1)),
)
STRETCH = 1.6236604965019064
BF16 = jnp.bfloat16
F32 = jnp.float32


def transform_tables(size):
    index_line = np.arange(size)
    angle = (index_line[:, None] * index_line[None, :] % size) * (2.0 * math.pi / size)
    cosine, sine = np.cos(angle), np.sin(angle)
    kept_cos = (STRETCH * cosine).astype(ml_dtypes.bfloat16).astype(np.float64)
    kept_sin = (STRETCH * sine).astype(ml_dtypes.bfloat16).astype(np.float64)
    unit = np.sum(kept_cos * cosine + kept_sin * sine) / np.sum(cosine**2 + sine**2)
    unit = unit * math.sqrt(size)
    plus = np.block([[kept_cos, kept_sin], [-kept_sin, kept_cos]])
    minus = np.block([[kept_cos, -kept_sin], [kept_sin, kept_cos]])
    return plus.astype(ml_dtypes.bfloat16), minus.astype(ml_dtypes.bfloat16), unit


def dot(left, right):
    return jnp.dot(left, right, preferred_element_type=F32)


def row_hot(start, rows, columns):
    row_index = lax.broadcasted_iota(jnp.int32, (rows, columns), 0)
    col_index = lax.broadcasted_iota(jnp.int32, (rows, columns), 1)
    return jnp.where((col_index - row_index).astype(F32) == start, 1.0, 0.0).astype(BF16)


def col_hot(start, rows, columns):
    row_index = lax.broadcasted_iota(jnp.int32, (rows, columns), 0)
    col_index = lax.broadcasted_iota(jnp.int32, (rows, columns), 1)
    return jnp.where((row_index - col_index).astype(F32) == start, 1.0, 0.0).astype(BF16)


def pack_kernel(
    strip_rows, total_rows, row_any, col_any, object_any, direction_any, block_ref, note_ref, row_ref, col_ref, sems
):
    half = object_any.shape[0]
    columns = block_ref.shape[1]
    corners = [
        pltpu.make_async_copy(row_any, row_ref, sems.at[0]),
        pltpu.make_async_copy(col_any, col_ref, sems.at[1]),
    ]
    bulk = [
        pltpu.make_async_copy(object_any, block_ref.at[pl.ds(0, half), :], sems.at[2]),
        pltpu.make_async_copy(direction_any, block_ref.at[pl.ds(half, half), :], sems.at[3]),
    ]
    for copy in corners + bulk:
        copy.start()
    for copy in corners:
        copy.wait()
    strip_index = lax.axis_index("strip")
    near = row_ref.shape[0]
    insides, aheads = [], []
    for position in range(near):
        inside = row_ref[position] - (strip_index - REACH) * strip_rows
        inside = lax.rem(inside + 2 * total_rows, total_rows)
        insides.append(inside)
        aheads.append(REACH - lax.div(inside, strip_rows))
    lane = lax.broadcasted_iota(jnp.int32, (NOTE_ROWS, columns), 1)
    note = jnp.zeros((NOTE_ROWS, columns), F32)
    for position in range(near):
        to_owner = jnp.int32(0)
        for row, places in enumerate(PLACES):
            for column, place in enumerate(places):
                chosen = (aheads[0] == row - REACH) & (aheads[1] == column - REACH)
                to_owner = jnp.where(chosen, -place[position], to_owner)
        first_row = insides[position] + (to_owner + 1 - REACH) * strip_rows
        for place, value in enumerate((first_row, col_ref[position], to_owner)):
            note = jnp.where(lane == place * near + position, value.astype(F32), note)
    note = note.astype(BF16)
    block_ref[2 * half :, :] = note
    note_ref[...] = note
    for copy in bulk:
        copy.wait()


def phase_kernel(phase_ref, cos_ref, sin_ref):
    cos_ref[...] = jnp.cos(phase_ref[...])
    sin_ref[...] = jnp.sin(phase_ref[...])


def strips_around(first_ref, own, second_ref):
    even = lax.rem(lax.axis_index("strip"), 2) == 0
    first, second = first_ref[...], second_ref[...]
    return jnp.where(even, first, second), own, jnp.where(even, second, first)


def corners_here(far, above, own, below, near):
    found = []
    for note, owner in zip((far, above, own, below), OWNERS):
        note = note[note.shape[0] - NOTE_ROWS :, :].astype(F32)[0:1]
        for position in range(near):
            here = note[:, 2 * near + position : 2 * near + position + 1] == owner
            first_row = note[:, position : position + 1]
            first_col = note[:, near + position : near + position + 1]
            found.append((jnp.where(here, 1.0, 0.0), first_row, first_col))
    return found


def cut_kernel(
    rows, near, far_ref, note_ref, object_ref, direction_ref, second_ref, first_ref, out_ref, start_ref, *count_ref
):
    targets, parts, size, _ = out_ref.shape
    columns = object_ref.shape[1]
    own = jnp.concatenate([object_ref[...], direction_ref[...], note_ref[...]], axis=0)
    above, own, below = strips_around(first_ref, own, second_ref)
    found = corners_here(far_ref[...], above, own, below, near)
    nowhere = 4.0 * rows
    if count_ref:
        slots = targets
        count_ref[0][0] = jnp.sum(sum(here for here, _, _ in found)).astype(jnp.int32)
        starts = [[nowhere, 0.0] for _ in range(slots)]
        rank = jnp.zeros((1, 1), F32)
        for here, first_row, first_col in found:
            for slot in range(slots):
                taken = here * jnp.where(rank == slot, 1.0, 0.0) > 0.0
                starts[slot][0] = jnp.where(taken, first_row, starts[slot][0])
                starts[slot][1] = jnp.where(taken, first_col, starts[slot][1])
            rank += here
    else:
        slots = len(found)
        starts = [[jnp.where(here > 0.0, row, nowhere), col] for here, row, col in found]
    hots = []
    for slot, (first_row, first_col) in enumerate(starts):
        start_ref[2 * slot : 2 * slot + 1, :] = jnp.broadcast_to(first_row, (1, 128))
        start_ref[2 * slot + 1 : 2 * slot + 2, :] = jnp.broadcast_to(first_col, (1, 128))
        hots.append((row_hot(first_row, size, 3 * rows), col_hot(first_col, columns, size)))
    bands = [
        jnp.concatenate(
            [block[part * rows : (part + 1) * rows, :] for block in (above, own, below)], axis=0
        )
        for part in range(parts)
    ]
    pick_rows = jnp.concatenate([hot for hot, _ in hots], axis=0)
    picked = [dot(pick_rows, band).astype(BF16) for band in bands]
    for slot in range(slots):
        lines = [part[slot * size : (slot + 1) * size] for part in picked]
        window = dot(jnp.concatenate(lines, axis=0), hots[slot][1]).astype(BF16)
        out_ref[slot] = window.reshape(parts, size, size)
    if slots < targets:
        out_ref[slots:] = jnp.zeros((targets - slots, parts, size, size), BF16)


def chain_kernel(unit, window_ref, other_ref, probe_ref, cos_ref, sin_ref, plus_ref, minus_ref, out_ref, wave_ref):
    slices, _, size, _ = wave_ref.shape
    packed = window_ref.shape[0] < slices
    plus, minus = plus_ref[...], minus_ref[...]
    even = lax.rem(lax.axis_index("cuts"), 2) == 0

    def window(layer, part):
        if not packed:
            return window_ref[layer, part].astype(F32)
        mine, other = window_ref[layer // 2, part], other_ref[layer // 2, part]
        return (jnp.where(even, mine, other) if layer % 2 == 0 else jnp.where(even, other, mine)).astype(F32)

    def swap(values):
        blocks = [[values[i * size : (i + 1) * size, j * size : (j + 1) * size]
                   for j in range(values.shape[1] // size)] for i in range(values.shape[0] // size)]
        turned = [jnp.concatenate([row[j] for row in blocks], axis=1) for j in range(len(blocks[0]))]
        return jnp.concatenate(turned, axis=0) if len(turned) > 1 else turned[0]

    def from_left(table, columns):
        step = 2 * size // 2
        return jnp.concatenate([dot(table[i * step : (i + 1) * step], columns) for i in range(2)], axis=0)

    def from_right(rows, table):
        step = rows.shape[0] // 2
        return jnp.concatenate([dot(rows[i * step : (i + 1) * step], table) for i in range(2)], axis=0)

    def forward(columns):
        half = from_left(plus, columns.astype(BF16)).astype(BF16)
        return from_right(swap(half), minus)

    def inverse(rows):
        half = from_right(rows.astype(BF16), plus).astype(BF16)
        return from_left(minus, swap(half))

    def kernel_times(rows, sign, scale):
        kernel_cos, kernel_sin = cos_ref[...] * scale, sin_ref[...] * (sign * scale)
        made = []
        for i in range(rows.shape[0] // size):
            re, im = rows[i * size : (i + 1) * size, :size], rows[i * size : (i + 1) * size, size:]
            made.append(jnp.concatenate(
                [re * kernel_cos - im * kernel_sin, re * kernel_sin + im * kernel_cos], axis=1))
        return jnp.concatenate(made, axis=0) if len(made) > 1 else made[0]

    psi_re, psi_im = probe_ref[0].astype(F32), probe_ref[1].astype(F32)
    tan_re, tan_im = None, None
    far_scale = 1.0 / unit**2
    hop_scale = 1.0 / unit**4
    for layer in range(slices):
        wave_ref[layer, 0], wave_ref[layer, 1] = psi_re, psi_im
        obj_re, obj_im = window(layer, 0), window(layer, 1)
        dir_re, dir_im = window(layer, 2), window(layer, 3)
        exit_re = obj_re * psi_re - obj_im * psi_im
        exit_im = obj_re * psi_im + obj_im * psi_re
        delta_re = dir_re * psi_re - dir_im * psi_im
        delta_im = dir_re * psi_im + dir_im * psi_re
        if layer > 0:
            delta_re += obj_re * tan_re - obj_im * tan_im
            delta_im += obj_re * tan_im + obj_im * tan_re
        columns = jnp.concatenate([
            jnp.concatenate([exit_re, delta_re], axis=1),
            jnp.concatenate([exit_im, delta_im], axis=1)], axis=0)
        spectrum = forward(columns)
        if layer < slices - 1:
            waves = inverse(kernel_times(spectrum, 1.0, hop_scale))
            psi_re, tan_re = waves[:size, :size], waves[:size, size:]
            psi_im, tan_im = waves[size:, :size], waves[size:, size:]
        else:
            far = kernel_times(spectrum, 1.0, far_scale)
    far_re, far_im = far[:size, :size], far[:size, size:]
    weight = (4.0 / slices) * (far_re * far[size:, :size] + far_im * far[size:, size:])
    back = jnp.concatenate([weight * far_re, weight * far_im], axis=1)
    adjoint = inverse(kernel_times(back, -1.0, far_scale))
    for layer in range(slices - 1, -1, -1):
        adj_re, adj_im = adjoint[:size], adjoint[size:]
        psi_re, psi_im = wave_ref[layer, 0], wave_ref[layer, 1]
        later = grad if layer < slices - 1 else None
        grad = [(psi_re * adj_re + psi_im * adj_im).astype(BF16), (psi_re * adj_im - psi_im * adj_re).astype(BF16)]
        for part in range(2):
            if not packed:
                out_ref[layer, part] = grad[part]
            elif layer % 2 == 0:
                out_ref[layer // 2, part] = jnp.where(even, grad[part], later[part])
        if layer > 0:
            obj_re, obj_im = window(layer, 0), window(layer, 1)
            columns = jnp.concatenate(
                [obj_re * adj_re + obj_im * adj_im, obj_re * adj_im - obj_im * adj_re], axis=0)
            adjoint = inverse(kernel_times(forward(columns), -1.0, hop_scale))


def gather_kernel(most, start_ref, grad_ref, first_ref, own_ref, second_ref):
    slots, parts, size, _ = grad_ref.shape
    slots = min(slots, most)
    rows, columns = own_ref.shape[1:]
    even = lax.rem(lax.axis_index("strip"), 2) == 0
    placed = [[] for _ in range(parts)]
    hots = []
    for slot in range(slots):
        first_row = start_ref[2 * slot : 2 * slot + 1, 0:1]
        first_col = start_ref[2 * slot + 1 : 2 * slot + 2, 0:1]
        hots.append(col_hot(first_row, 3 * rows, size))
        values = grad_ref[slot].reshape(parts * size, size)
        spread = dot(values, row_hot(first_col, size, columns)).astype(BF16)
        for part in range(parts):
            placed[part].append(spread[part * size : (part + 1) * size])
    pick_rows = jnp.concatenate(hots, axis=1)
    for part in range(parts):
        total = dot(pick_rows, jnp.concatenate(placed[part], axis=0))
        above, below = total[:rows].astype(BF16), total[2 * rows :].astype(BF16)
        own_ref[part] = total[rows : 2 * rows]
        first_ref[part] = jnp.where(even, above, below)
        second_ref[part] = jnp.where(even, below, above)


def on_device(object_slices, direction, probe_wave, kernel_phase, corner_row, corner_col):
    strip_rows = object_slices.shape[2]
    column_count = object_slices.shape[3]
    patch_size = probe_wave.shape[1]
    strip_count = lax.axis_size("strip")
    cuts_count = lax.axis_size("cuts")
    plus, minus, unit = transform_tables(patch_size)

    def exchanged(block, offset):
        route = [(i, ((i - offset) ^ 1) + offset) for i in range(strip_count)]
        return lax.ppermute(block, "strip", [(i, j % strip_count) for i, j in route])

    vmem = pl.BlockSpec(memory_space=pltpu.VMEM)
    params = pltpu.CompilerParams(vmem_limit_bytes=32 * 1024 * 1024)

    block_rows = 4 * strip_rows + NOTE_ROWS
    hbm = pl.BlockSpec(memory_space=pl.ANY)
    wide = pltpu.CompilerParams(vmem_limit_bytes=60 * 1024 * 1024)
    objects = object_slices.reshape(-1, column_count)
    directions = direction.reshape(-1, column_count)
    block, note = pl.pallas_call(
        functools.partial(pack_kernel, strip_rows, strip_count * strip_rows),
        out_shape=(
            jax.ShapeDtypeStruct((block_rows, column_count), BF16),
            jax.ShapeDtypeStruct((NOTE_ROWS, column_count), BF16),
        ),
        in_specs=[hbm] * 4,
        out_specs=(vmem, vmem),
        scratch_shapes=[
            pltpu.SMEM(corner_row.shape, jnp.int32),
            pltpu.SMEM(corner_row.shape, jnp.int32),
            pltpu.SemaphoreType.DMA((4,)),
        ],
        compiler_params=wide,
        name="pack_block",
    )(corner_row, corner_col, objects, directions)
    far = lax.ppermute(note, "strip", [(i, (i + REACH) % strip_count) for i in range(strip_count)])
    first, second = exchanged(block, -1), exchanged(block, 0)
    kernel_cos, kernel_sin = pl.pallas_call(
        phase_kernel,
        out_shape=(jax.ShapeDtypeStruct(kernel_phase.shape, F32),) * 2,
        in_specs=[vmem],
        out_specs=(vmem,) * 2,
        compiler_params=params,
        name="phase_tables",
    )(kernel_phase)
    near = corner_row.shape[0]
    strip_shape = (2, strip_rows, column_count)

    chips = cuts_count // 2
    same_core = [[core + 2 * chip for chip in range(chips)] for core in range(2)]

    def cut(targets, counted, *operands):
        windows_shape = (targets, 4, patch_size, patch_size)
        out_shape = (jax.ShapeDtypeStruct(windows_shape, BF16), jax.ShapeDtypeStruct((2 * targets, 128), F32))
        out_specs = (vmem, vmem)
        if counted:
            out_shape += (jax.ShapeDtypeStruct((1,), jnp.int32),)
            out_specs += (pl.BlockSpec(memory_space=pltpu.SMEM),)
        return pl.pallas_call(
            functools.partial(cut_kernel, strip_rows, near),
            out_shape=out_shape,
            in_specs=[vmem] * 6,
            out_specs=out_specs,
            compiler_params=params,
            name="cut_windows",
        )(*operands)

    def chain(windows, other, probe_wave, *tables):
        return pl.pallas_call(
            functools.partial(chain_kernel, unit),
            out_shape=jax.ShapeDtypeStruct((windows.shape[0], 2, patch_size, patch_size), BF16),
            in_specs=[vmem] * 7,
            out_specs=vmem,
            scratch_shapes=[pltpu.VMEM((cuts_count, 2, patch_size, patch_size), F32)],
            compiler_params=params,
            name="wave_chain",
        )(windows, other, probe_wave, *tables)

    def gather(start, gradient):
        return pl.pallas_call(
            functools.partial(gather_kernel, len(OWNERS) * near),
            out_shape=(
                jax.ShapeDtypeStruct(strip_shape, BF16),
                jax.ShapeDtypeStruct(strip_shape, F32),
                jax.ShapeDtypeStruct(strip_shape, BF16),
            ),
            in_specs=[vmem, vmem],
            out_specs=(vmem, vmem, vmem),
            compiler_params=params,
            name="add_windows",
        )(start, gradient)

    def one_per_chip(windows, start, around, constants):
        del around
        windows = lax.all_to_all(windows, "cuts", 0, 0, axis_index_groups=same_core, tiled=False)
        other = lax.ppermute(windows, "cuts", [(i, i ^ 1) for i in range(cuts_count)])
        gradient = chain(windows, other, *constants)
        gradient = lax.all_to_all(gradient, "cuts", 0, 0, axis_index_groups=same_core, tiled=False)
        return gather(start, gradient)

    def one_per_device(windows, start, around, constants):
        del windows, start
        windows, start = cut(cuts_count, False, *around)
        windows = lax.all_to_all(windows, "cuts", 0, 0, tiled=False)
        gradient = chain(windows, windows, *constants)
        gradient = lax.all_to_all(gradient, "cuts", 0, 0, tiled=False)
        return gather(start, gradient)

    around = (far, note, objects, directions, second, first)
    windows, start, count = cut(chips, True, *around)
    constants = (probe_wave, kernel_cos, kernel_sin, jnp.asarray(plus), jnp.asarray(minus))
    first, own, second = lax.cond(
        count[0] > chips, one_per_device, one_per_chip, windows, start, around, constants
    )
    first, second = exchanged(first, -1), exchanged(second, 0)
    return (own + first.astype(F32) + second.astype(F32))[None]


def solution(mesh):
    in_specs = (
        P("cuts", None, "strip", None),
        P("cuts", None, "strip", None),
        P(),
        P(),
        P("strip"),
        P("strip"),
    )
    out_specs = P("cuts", None, "strip", None)
    return jax.shard_map(
        on_device, mesh=mesh, in_specs=in_specs, out_specs=out_specs, check_vma=False
    )
```

```python
import functools
import math

import jax
import jax.numpy as jnp
import ml_dtypes
import numpy as np
from jax import lax
from jax.experimental import pallas as pl
from jax.experimental.pallas import tpu as pltpu
from jax.sharding import PartitionSpec as P

REACH = 2
NOTE_ROWS = 16
OWNERS = (-REACH, -1, 0, 1)
PLACES = (
    ((2, 2), (2, 1), (2, 1), (2, -1), (2, -1)),
    ((1, 2), (1, 2), (2, 1), (2, -1), (2, -1)),
    ((1, 2), (1, 2), (0, 1), (1, -1), (1, -1)),
    ((-1, 2), (-1, 2), (-1, 1), (-1, 0), (0, -1)),
    ((-1, 2), (-1, 2), (-1, 1), (-1, 0), (-1, -1)),
)
STRETCH = 1.6236604965019064 / 16
BF16 = jnp.bfloat16
F32 = jnp.float32


def transform_tables(size):
    index_line = np.arange(size)
    angle = (index_line[:, None] * index_line[None, :] % size) * (2.0 * math.pi / size)
    cosine, sine = np.cos(angle), np.sin(angle)
    kept_cos = (STRETCH * cosine).astype(ml_dtypes.bfloat16).astype(np.float64)
    kept_sin = (STRETCH * sine).astype(ml_dtypes.bfloat16).astype(np.float64)
    unit = np.sum(kept_cos * cosine + kept_sin * sine) / np.sum(cosine**2 + sine**2)
    unit = unit * math.sqrt(size)
    plus = np.block([[kept_cos, kept_sin], [-kept_sin, kept_cos]])
    minus = np.block([[kept_cos, -kept_sin], [kept_sin, kept_cos]])
    return plus.astype(ml_dtypes.bfloat16), minus.astype(ml_dtypes.bfloat16), unit


def dot(left, right):
    return jnp.dot(left, right, preferred_element_type=F32)


def row_hot(start, rows, columns):
    row_index = lax.broadcasted_iota(jnp.int32, (rows, columns), 0)
    col_index = lax.broadcasted_iota(jnp.int32, (rows, columns), 1)
    return jnp.where((col_index - row_index).astype(F32) == start, 1.0, 0.0).astype(BF16)


def col_hot(start, rows, columns):
    row_index = lax.broadcasted_iota(jnp.int32, (rows, columns), 0)
    col_index = lax.broadcasted_iota(jnp.int32, (rows, columns), 1)
    return jnp.where((row_index - col_index).astype(F32) == start, 1.0, 0.0).astype(BF16)


def pack_kernel(
    strip_rows, total_rows, row_any, col_any, object_any, direction_any, block_ref, note_ref, row_ref, col_ref, sems
):
    half = object_any.shape[0]
    columns = block_ref.shape[1]
    corners = [
        pltpu.make_async_copy(row_any, row_ref, sems.at[0]),
        pltpu.make_async_copy(col_any, col_ref, sems.at[1]),
    ]
    bulk = [
        pltpu.make_async_copy(object_any, block_ref.at[pl.ds(0, half), :], sems.at[2]),
        pltpu.make_async_copy(direction_any, block_ref.at[pl.ds(half, half), :], sems.at[3]),
    ]
    for copy in corners + bulk:
        copy.start()
    for copy in corners:
        copy.wait()
    strip_index = lax.axis_index("strip")
    near = row_ref.shape[0]
    insides, aheads = [], []
    for position in range(near):
        inside = row_ref[position] - (strip_index - REACH) * strip_rows
        inside = lax.rem(inside + 2 * total_rows, total_rows)
        insides.append(inside)
        aheads.append(REACH - lax.div(inside, strip_rows))
    lane = lax.broadcasted_iota(jnp.int32, (NOTE_ROWS, columns), 1)
    note = jnp.zeros((NOTE_ROWS, columns), F32)
    for position in range(near):
        to_owner = jnp.int32(0)
        for row, places in enumerate(PLACES):
            for column, place in enumerate(places):
                chosen = (aheads[0] == row - REACH) & (aheads[1] == column - REACH)
                to_owner = jnp.where(chosen, -place[position], to_owner)
        first_row = insides[position] + (to_owner + 1 - REACH) * strip_rows
        for place, value in enumerate((first_row, col_ref[position], to_owner)):
            note = jnp.where(lane == place * near + position, value.astype(F32), note)
    note = note.astype(BF16)
    block_ref[2 * half :, :] = note
    note_ref[...] = note
    for copy in bulk:
        copy.wait()


def phase_kernel(phase_ref, cos_ref, sin_ref):
    cos_ref[...] = jnp.cos(phase_ref[...])
    sin_ref[...] = jnp.sin(phase_ref[...])


def strips_around(first_ref, own, second_ref):
    even = lax.rem(lax.axis_index("strip"), 2) == 0
    first, second = first_ref[...], second_ref[...]
    return jnp.where(even, first, second), own, jnp.where(even, second, first)


def corners_here(far, above, own, below, near):
    found = []
    for note, owner in zip((far, above, own, below), OWNERS):
        note = note[note.shape[0] - NOTE_ROWS :, :].astype(F32)[0:1]
        for position in range(near):
            here = note[:, 2 * near + position : 2 * near + position + 1] == owner
            first_row = note[:, position : position + 1]
            first_col = note[:, near + position : near + position + 1]
            found.append((jnp.where(here, 1.0, 0.0), first_row, first_col))
    return found


def cut_kernel(
    rows, near, far_ref, note_ref, object_ref, direction_ref, second_ref, first_ref, out_ref, start_ref, *count_ref
):
    targets, parts, size, _ = out_ref.shape
    columns = object_ref.shape[1]
    own = jnp.concatenate([object_ref[...], direction_ref[...], note_ref[...]], axis=0)
    above, own, below = strips_around(first_ref, own, second_ref)
    found = corners_here(far_ref[...], above, own, below, near)
    nowhere = 4.0 * rows
    if count_ref:
        slots = targets
        count_ref[0][0] = jnp.sum(sum(here for here, _, _ in found)).astype(jnp.int32)
        starts = [[nowhere, 0.0] for _ in range(slots)]
        rank = jnp.zeros((1, 1), F32)
        for here, first_row, first_col in found:
            for slot in range(slots):
                taken = here * jnp.where(rank == slot, 1.0, 0.0) > 0.0
                starts[slot][0] = jnp.where(taken, first_row, starts[slot][0])
                starts[slot][1] = jnp.where(taken, first_col, starts[slot][1])
            rank += here
    else:
        slots = len(found)
        starts = [[jnp.where(here > 0.0, row, nowhere), col] for here, row, col in found]
    hots = []
    for slot, (first_row, first_col) in enumerate(starts):
        start_ref[2 * slot : 2 * slot + 1, :] = jnp.broadcast_to(first_row, (1, 128))
        start_ref[2 * slot + 1 : 2 * slot + 2, :] = jnp.broadcast_to(first_col, (1, 128))
        hots.append((row_hot(first_row, size, 3 * rows), col_hot(first_col, columns, size)))
    bands = [
        jnp.concatenate(
            [block[part * rows : (part + 1) * rows, :] for block in (above, own, below)], axis=0
        )
        for part in range(parts)
    ]
    pick_rows = jnp.concatenate([hot for hot, _ in hots], axis=0)
    picked = [dot(pick_rows, band).astype(BF16) for band in bands]
    for slot in range(slots):
        lines = [part[slot * size : (slot + 1) * size] for part in picked]
        window = dot(jnp.concatenate(lines, axis=0), hots[slot][1]).astype(BF16)
        out_ref[slot] = window.reshape(parts, size, size)
    if slots < targets:
        out_ref[slots:] = jnp.zeros((targets - slots, parts, size, size), BF16)


def chain_kernel(unit, window_ref, other_ref, probe_ref, cos_ref, sin_ref, plus_ref, minus_ref, out_ref, wave_ref):
    slices, _, size, _ = wave_ref.shape
    packed = window_ref.shape[0] < slices
    plus, minus = plus_ref[...], minus_ref[...]
    even = lax.rem(lax.axis_index("cuts"), 2) == 0

    def window(layer, part):
        if not packed:
            return window_ref[layer, part].astype(F32)
        mine, other = window_ref[layer // 2, part], other_ref[layer // 2, part]
        return (jnp.where(even, mine, other) if layer % 2 == 0 else jnp.where(even, other, mine)).astype(F32)

    def swap(values):
        blocks = [[values[i * size : (i + 1) * size, j * size : (j + 1) * size]
                   for j in range(values.shape[1] // size)] for i in range(values.shape[0] // size)]
        turned = [jnp.concatenate([row[j] for row in blocks], axis=1) for j in range(len(blocks[0]))]
        return jnp.concatenate(turned, axis=0) if len(turned) > 1 else turned[0]

    def from_left(table, columns):
        step = 2 * size // 2
        return jnp.concatenate([dot(table[i * step : (i + 1) * step], columns) for i in range(2)], axis=0)

    def from_right(rows, table):
        step = rows.shape[0] // 2
        return jnp.concatenate([dot(rows[i * step : (i + 1) * step], table) for i in range(2)], axis=0)

    def forward(columns):
        half = from_left(plus, columns.astype(BF16)).astype(BF16)
        return from_right(swap(half), minus)

    def inverse(rows):
        half = from_right(rows.astype(BF16), plus).astype(BF16)
        return from_left(minus, swap(half))

    def kernel_times(rows, sign, scale):
        kernel_cos, kernel_sin = cos_ref[...] * scale, sin_ref[...] * (sign * scale)
        made = []
        for i in range(rows.shape[0] // size):
            re, im = rows[i * size : (i + 1) * size, :size], rows[i * size : (i + 1) * size, size:]
            made.append(jnp.concatenate(
                [re * kernel_cos - im * kernel_sin, re * kernel_sin + im * kernel_cos], axis=1))
        return jnp.concatenate(made, axis=0) if len(made) > 1 else made[0]

    psi_re, psi_im = probe_ref[0].astype(F32), probe_ref[1].astype(F32)
    tan_re, tan_im = None, None
    far_scale = 1.0 / unit**2
    hop_scale = 1.0 / unit**4
    for layer in range(slices):
        wave_ref[layer, 0], wave_ref[layer, 1] = psi_re, psi_im
        obj_re, obj_im = window(layer, 0), window(layer, 1)
        dir_re, dir_im = window(layer, 2), window(layer, 3)
        exit_re = obj_re * psi_re - obj_im * psi_im
        exit_im = obj_re * psi_im + obj_im * psi_re
        delta_re = dir_re * psi_re - dir_im * psi_im
        delta_im = dir_re * psi_im + dir_im * psi_re
        if layer > 0:
            delta_re += obj_re * tan_re - obj_im * tan_im
            delta_im += obj_re * tan_im + obj_im * tan_re
        columns = jnp.concatenate([
            jnp.concatenate([exit_re, delta_re], axis=1),
            jnp.concatenate([exit_im, delta_im], axis=1)], axis=0)
        spectrum = forward(columns)
        if layer < slices - 1:
            waves = inverse(kernel_times(spectrum, 1.0, hop_scale))
            psi_re, tan_re = waves[:size, :size], waves[:size, size:]
            psi_im, tan_im = waves[size:, :size], waves[size:, size:]
        else:
            far = kernel_times(spectrum, 1.0, far_scale)
    far_re, far_im = far[:size, :size], far[:size, size:]
    weight = (4.0 / slices) * (far_re * far[size:, :size] + far_im * far[size:, size:])
    back = jnp.concatenate([weight * far_re, weight * far_im], axis=1)
    adjoint = inverse(kernel_times(back, -1.0, far_scale))
    for layer in range(slices - 1, -1, -1):
        adj_re, adj_im = adjoint[:size], adjoint[size:]
        psi_re, psi_im = wave_ref[layer, 0], wave_ref[layer, 1]
        later = grad if layer < slices - 1 else None
        grad = [(psi_re * adj_re + psi_im * adj_im).astype(BF16), (psi_re * adj_im - psi_im * adj_re).astype(BF16)]
        for part in range(2):
            if not packed:
                out_ref[layer, part] = grad[part]
            elif layer % 2 == 0:
                out_ref[layer // 2, part] = jnp.where(even, grad[part], later[part])
        if layer > 0:
            obj_re, obj_im = window(layer, 0), window(layer, 1)
            columns = jnp.concatenate(
                [obj_re * adj_re + obj_im * adj_im, obj_re * adj_im - obj_im * adj_re], axis=0)
            adjoint = inverse(kernel_times(forward(columns), -1.0, hop_scale))


def gather_kernel(most, start_ref, grad_ref, first_ref, own_ref, second_ref):
    slots, parts, size, _ = grad_ref.shape
    slots = min(slots, most)
    rows, columns = own_ref.shape[1:]
    even = lax.rem(lax.axis_index("strip"), 2) == 0
    placed = [[] for _ in range(parts)]
    hots = []
    for slot in range(slots):
        first_row = start_ref[2 * slot : 2 * slot + 1, 0:1]
        first_col = start_ref[2 * slot + 1 : 2 * slot + 2, 0:1]
        hots.append(col_hot(first_row, 3 * rows, size))
        values = grad_ref[slot].reshape(parts * size, size)
        spread = dot(values, row_hot(first_col, size, columns)).astype(BF16)
        for part in range(parts):
            placed[part].append(spread[part * size : (part + 1) * size])
    pick_rows = jnp.concatenate(hots, axis=1)
    for part in range(parts):
        total = dot(pick_rows, jnp.concatenate(placed[part], axis=0))
        above, below = total[:rows].astype(BF16), total[2 * rows :].astype(BF16)
        own_ref[part] = total[rows : 2 * rows]
        first_ref[part] = jnp.where(even, above, below)
        second_ref[part] = jnp.where(even, below, above)


def on_device(object_slices, direction, probe_wave, kernel_phase, corner_row, corner_col):
    strip_rows = object_slices.shape[2]
    column_count = object_slices.shape[3]
    patch_size = probe_wave.shape[1]
    strip_count = lax.axis_size("strip")
    cuts_count = lax.axis_size("cuts")
    plus, minus, unit = transform_tables(patch_size)

    def exchanged(block, offset):
        route = [(i, ((i - offset) ^ 1) + offset) for i in range(strip_count)]
        return lax.ppermute(block, "strip", [(i, j % strip_count) for i, j in route])

    vmem = pl.BlockSpec(memory_space=pltpu.VMEM)
    params = pltpu.CompilerParams(vmem_limit_bytes=32 * 1024 * 1024)

    block_rows = 4 * strip_rows + NOTE_ROWS
    hbm = pl.BlockSpec(memory_space=pl.ANY)
    wide = pltpu.CompilerParams(vmem_limit_bytes=60 * 1024 * 1024)
    objects = object_slices.reshape(-1, column_count)
    directions = direction.reshape(-1, column_count)
    block, note = pl.pallas_call(
        functools.partial(pack_kernel, strip_rows, strip_count * strip_rows),
        out_shape=(
            jax.ShapeDtypeStruct((block_rows, column_count), BF16),
            jax.ShapeDtypeStruct((NOTE_ROWS, column_count), BF16),
        ),
        in_specs=[hbm] * 4,
        out_specs=(vmem, vmem),
        scratch_shapes=[
            pltpu.SMEM(corner_row.shape, jnp.int32),
            pltpu.SMEM(corner_row.shape, jnp.int32),
            pltpu.SemaphoreType.DMA((4,)),
        ],
        compiler_params=wide,
        name="pack_block",
    )(corner_row, corner_col, objects, directions)
    far = lax.ppermute(note, "strip", [(i, (i + REACH) % strip_count) for i in range(strip_count)])
    first, second = exchanged(block, -1), exchanged(block, 0)
    kernel_cos, kernel_sin = pl.pallas_call(
        phase_kernel,
        out_shape=(jax.ShapeDtypeStruct(kernel_phase.shape, F32),) * 2,
        in_specs=[vmem],
        out_specs=(vmem,) * 2,
        compiler_params=params,
        name="phase_tables",
    )(kernel_phase)
    near = corner_row.shape[0]
    strip_shape = (2, strip_rows, column_count)

    chips = cuts_count // 2
    same_core = [[core + 2 * chip for chip in range(chips)] for core in range(2)]

    def cut(targets, counted, *operands):
        windows_shape = (targets, 4, patch_size, patch_size)
        out_shape = (jax.ShapeDtypeStruct(windows_shape, BF16), jax.ShapeDtypeStruct((2 * targets, 128), F32))
        out_specs = (vmem, vmem)
        if counted:
            out_shape += (jax.ShapeDtypeStruct((1,), jnp.int32),)
            out_specs += (pl.BlockSpec(memory_space=pltpu.SMEM),)
        return pl.pallas_call(
            functools.partial(cut_kernel, strip_rows, near),
            out_shape=out_shape,
            in_specs=[vmem] * 6,
            out_specs=out_specs,
            compiler_params=params,
            name="cut_windows",
        )(*operands)

    def chain(windows, other, probe_wave, *tables):
        return pl.pallas_call(
            functools.partial(chain_kernel, unit),
            out_shape=jax.ShapeDtypeStruct((windows.shape[0], 2, patch_size, patch_size), BF16),
            in_specs=[vmem] * 7,
            out_specs=vmem,
            scratch_shapes=[pltpu.VMEM((cuts_count, 2, patch_size, patch_size), F32)],
            compiler_params=params,
            name="wave_chain",
        )(windows, other, probe_wave, *tables)

    def gather(start, gradient):
        return pl.pallas_call(
            functools.partial(gather_kernel, len(OWNERS) * near),
            out_shape=(
                jax.ShapeDtypeStruct(strip_shape, BF16),
                jax.ShapeDtypeStruct(strip_shape, F32),
                jax.ShapeDtypeStruct(strip_shape, BF16),
            ),
            in_specs=[vmem, vmem],
            out_specs=(vmem, vmem, vmem),
            compiler_params=params,
            name="add_windows",
        )(start, gradient)

    def one_per_chip(windows, start, around, constants):
        del around
        windows = lax.all_to_all(windows, "cuts", 0, 0, axis_index_groups=same_core, tiled=False)
        other = lax.ppermute(windows, "cuts", [(i, i ^ 1) for i in range(cuts_count)])
        gradient = chain(windows, other, *constants)
        gradient = lax.all_to_all(gradient, "cuts", 0, 0, axis_index_groups=same_core, tiled=False)
        return gather(start, gradient)

    def one_per_device(windows, start, around, constants):
        del windows, start
        windows, start = cut(cuts_count, False, *around)
        windows = lax.all_to_all(windows, "cuts", 0, 0, tiled=False)
        gradient = chain(windows, windows, *constants)
        gradient = lax.all_to_all(gradient, "cuts", 0, 0, tiled=False)
        return gather(start, gradient)

    around = (far, note, objects, directions, second, first)
    windows, start, count = cut(chips, True, *around)
    constants = (probe_wave, kernel_cos, kernel_sin, jnp.asarray(plus), jnp.asarray(minus))
    first, own, second = lax.cond(
        count[0] > chips, one_per_device, one_per_chip, windows, start, around, constants
    )
    first, second = exchanged(first, -1), exchanged(second, 0)
    return (own + first.astype(F32) + second.astype(F32))[None]


def solution(mesh):
    in_specs = (
        P("cuts", None, "strip", None),
        P("cuts", None, "strip", None),
        P(),
        P(),
        P("strip"),
        P("strip"),
    )
    out_specs = P("cuts", None, "strip", None)
    return jax.shard_map(
        on_device, mesh=mesh, in_specs=in_specs, out_specs=out_specs, check_vma=False
    )
```

```python
import functools
import math

import jax
import jax.numpy as jnp
import ml_dtypes
import numpy as np
from jax import lax
from jax.experimental import pallas as pl
from jax.experimental.pallas import tpu as pltpu
from jax.sharding import PartitionSpec as P

REACH = 2
NOTE_ROWS = 16
OWNERS = (-REACH, -1, 0, 1)
PLACES = (
    ((2, 2), (2, 1), (2, 1), (2, -1), (2, -1)),
    ((1, 2), (1, 2), (2, 1), (2, -1), (2, -1)),
    ((1, 2), (1, 2), (0, 1), (1, -1), (1, -1)),
    ((-1, 2), (-1, 2), (-1, 1), (-1, 0), (0, -1)),
    ((-1, 2), (-1, 2), (-1, 1), (-1, 0), (-1, -1)),
)
STRETCHES = (1.666129 / 16, 1.625068 / 16, 1.885787 / 16, 1.99216 / 16)
BF16 = jnp.bfloat16
F32 = jnp.float32


def transform_tables(size):
    index_line = np.arange(size)
    angle = (index_line[:, None] * index_line[None, :] % size) * (2.0 * math.pi / size)
    cosine, sine = np.cos(angle), np.sin(angle)
    tables, units = [], []
    for stretch in STRETCHES:
        kept_cos = (stretch * cosine).astype(ml_dtypes.bfloat16).astype(np.float64)
        kept_sin = (stretch * sine).astype(ml_dtypes.bfloat16).astype(np.float64)
        unit = np.sum(kept_cos * cosine + kept_sin * sine) / np.sum(cosine**2 + sine**2)
        units.append(float(unit * math.sqrt(size)))
        plus = np.block([[kept_cos, kept_sin], [-kept_sin, kept_cos]])
        minus = np.block([[kept_cos, -kept_sin], [kept_sin, kept_cos]])
        tables.append(np.stack([plus, minus]))
    return np.stack(tables).astype(ml_dtypes.bfloat16), units


def dot(left, right):
    return jnp.dot(left, right, preferred_element_type=F32)


def row_hot(start, rows, columns):
    row_index = lax.broadcasted_iota(jnp.int32, (rows, columns), 0)
    col_index = lax.broadcasted_iota(jnp.int32, (rows, columns), 1)
    return jnp.where((col_index - row_index).astype(F32) == start, 1.0, 0.0).astype(BF16)


def col_hot(start, rows, columns):
    row_index = lax.broadcasted_iota(jnp.int32, (rows, columns), 0)
    col_index = lax.broadcasted_iota(jnp.int32, (rows, columns), 1)
    return jnp.where((row_index - col_index).astype(F32) == start, 1.0, 0.0).astype(BF16)


def pack_kernel(
    strip_rows, total_rows, row_any, col_any, object_any, direction_any, block_ref, note_ref, row_ref, col_ref, sems
):
    half = object_any.shape[0]
    columns = block_ref.shape[1]
    corners = [
        pltpu.make_async_copy(row_any, row_ref, sems.at[0]),
        pltpu.make_async_copy(col_any, col_ref, sems.at[1]),
    ]
    bulk = [
        pltpu.make_async_copy(object_any, block_ref.at[pl.ds(0, half), :], sems.at[2]),
        pltpu.make_async_copy(direction_any, block_ref.at[pl.ds(half, half), :], sems.at[3]),
    ]
    for copy in corners + bulk:
        copy.start()
    for copy in corners:
        copy.wait()
    strip_index = lax.axis_index("strip")
    near = row_ref.shape[0]
    insides, aheads = [], []
    for position in range(near):
        inside = row_ref[position] - (strip_index - REACH) * strip_rows
        inside = lax.rem(inside + 2 * total_rows, total_rows)
        insides.append(inside)
        aheads.append(REACH - lax.div(inside, strip_rows))
    lane = lax.broadcasted_iota(jnp.int32, (NOTE_ROWS, columns), 1)
    note = jnp.zeros((NOTE_ROWS, columns), F32)
    for position in range(near):
        to_owner = jnp.int32(0)
        for row, places in enumerate(PLACES):
            for column, place in enumerate(places):
                chosen = (aheads[0] == row - REACH) & (aheads[1] == column - REACH)
                to_owner = jnp.where(chosen, -place[position], to_owner)
        first_row = insides[position] + (to_owner + 1 - REACH) * strip_rows
        for place, value in enumerate((first_row, col_ref[position], to_owner)):
            note = jnp.where(lane == place * near + position, value.astype(F32), note)
    note = note.astype(BF16)
    block_ref[2 * half :, :] = note
    note_ref[...] = note
    for copy in bulk:
        copy.wait()


def phase_kernel(phase_ref, cos_ref, sin_ref):
    cos_ref[...] = jnp.cos(phase_ref[...])
    sin_ref[...] = jnp.sin(phase_ref[...])


def strips_around(first_ref, own, second_ref):
    even = lax.rem(lax.axis_index("strip"), 2) == 0
    first, second = first_ref[...], second_ref[...]
    return jnp.where(even, first, second), own, jnp.where(even, second, first)


def corners_here(far, above, own, below, near):
    found = []
    for note, owner in zip((far, above, own, below), OWNERS):
        note = note[note.shape[0] - NOTE_ROWS :, :].astype(F32)[0:1]
        for position in range(near):
            here = note[:, 2 * near + position : 2 * near + position + 1] == owner
            first_row = note[:, position : position + 1]
            first_col = note[:, near + position : near + position + 1]
            found.append((jnp.where(here, 1.0, 0.0), first_row, first_col))
    return found


def cut_kernel(
    rows, near, far_ref, note_ref, object_ref, direction_ref, second_ref, first_ref, out_ref, start_ref, *count_ref
):
    targets, parts, size, _ = out_ref.shape
    columns = object_ref.shape[1]
    own = jnp.concatenate([object_ref[...], direction_ref[...], note_ref[...]], axis=0)
    above, own, below = strips_around(first_ref, own, second_ref)
    found = corners_here(far_ref[...], above, own, below, near)
    nowhere = 4.0 * rows
    if count_ref:
        slots = targets
        count_ref[0][0] = jnp.sum(sum(here for here, _, _ in found)).astype(jnp.int32)
        starts = [[nowhere, 0.0] for _ in range(slots)]
        rank = jnp.zeros((1, 1), F32)
        for here, first_row, first_col in found:
            for slot in range(slots):
                taken = here * jnp.where(rank == slot, 1.0, 0.0) > 0.0
                starts[slot][0] = jnp.where(taken, first_row, starts[slot][0])
                starts[slot][1] = jnp.where(taken, first_col, starts[slot][1])
            rank += here
    else:
        slots = len(found)
        starts = [[jnp.where(here > 0.0, row, nowhere), col] for here, row, col in found]
    hots = []
    for slot, (first_row, first_col) in enumerate(starts):
        start_ref[2 * slot : 2 * slot + 1, :] = jnp.broadcast_to(first_row, (1, 128))
        start_ref[2 * slot + 1 : 2 * slot + 2, :] = jnp.broadcast_to(first_col, (1, 128))
        hots.append((row_hot(first_row, size, 3 * rows), col_hot(first_col, columns, size)))
    bands = [
        jnp.concatenate(
            [block[part * rows : (part + 1) * rows, :] for block in (above, own, below)], axis=0
        )
        for part in range(parts)
    ]
    pick_rows = jnp.concatenate([hot for hot, _ in hots], axis=0)
    picked = [dot(pick_rows, band).astype(BF16) for band in bands]
    for slot in range(slots):
        lines = [part[slot * size : (slot + 1) * size] for part in picked]
        window = dot(jnp.concatenate(lines, axis=0), hots[slot][1]).astype(BF16)
        out_ref[slot] = window.reshape(parts, size, size)
    if slots < targets:
        out_ref[slots:] = jnp.zeros((targets - slots, parts, size, size), BF16)


def chain_kernel(units, window_ref, other_ref, probe_ref, cos_ref, sin_ref, table_ref, out_ref, wave_ref):
    slices, _, size, _ = wave_ref.shape
    packed = window_ref.shape[0] < slices
    even = lax.rem(lax.axis_index("cuts"), 2) == 0

    def window(layer, part):
        if not packed:
            return window_ref[layer, part].astype(F32)
        mine, other = window_ref[layer // 2, part], other_ref[layer // 2, part]
        return (jnp.where(even, mine, other) if layer % 2 == 0 else jnp.where(even, other, mine)).astype(F32)

    def swap(values):
        blocks = [[values[i * size : (i + 1) * size, j * size : (j + 1) * size]
                   for j in range(values.shape[1] // size)] for i in range(values.shape[0] // size)]
        turned = [jnp.concatenate([row[j] for row in blocks], axis=1) for j in range(len(blocks[0]))]
        return jnp.concatenate(turned, axis=0) if len(turned) > 1 else turned[0]

    def from_left(table, columns):
        step = 2 * size // 2
        return jnp.concatenate([dot(table[i * step : (i + 1) * step], columns) for i in range(2)], axis=0)

    def from_right(rows, table):
        step = rows.shape[0] // 2
        return jnp.concatenate([dot(rows[i * step : (i + 1) * step], table) for i in range(2)], axis=0)

    def forward(columns, table):
        half = from_left(table_ref[table, 0], columns.astype(BF16)).astype(BF16)
        return from_right(swap(half), table_ref[table, 1])

    def inverse(rows, table):
        half = from_right(rows.astype(BF16), table_ref[table, 0]).astype(BF16)
        return from_left(table_ref[table, 1], swap(half))

    def kernel_times(rows, sign, scale):
        kernel_cos, kernel_sin = cos_ref[...] * scale, sin_ref[...] * (sign * scale)
        made = []
        for i in range(rows.shape[0] // size):
            re, im = rows[i * size : (i + 1) * size, :size], rows[i * size : (i + 1) * size, size:]
            made.append(jnp.concatenate(
                [re * kernel_cos - im * kernel_sin, re * kernel_sin + im * kernel_cos], axis=1))
        return jnp.concatenate(made, axis=0) if len(made) > 1 else made[0]

    psi_re, psi_im = probe_ref[0].astype(F32), probe_ref[1].astype(F32)
    tan_re, tan_im = None, None
    scales = [1.0 / unit**2 for unit in units]
    for layer in range(slices):
        wave_ref[layer, 0], wave_ref[layer, 1] = psi_re, psi_im
        obj_re, obj_im = window(layer, 0), window(layer, 1)
        dir_re, dir_im = window(layer, 2), window(layer, 3)
        exit_re = obj_re * psi_re - obj_im * psi_im
        exit_im = obj_re * psi_im + obj_im * psi_re
        delta_re = dir_re * psi_re - dir_im * psi_im
        delta_im = dir_re * psi_im + dir_im * psi_re
        if layer > 0:
            delta_re += obj_re * tan_re - obj_im * tan_im
            delta_im += obj_re * tan_im + obj_im * tan_re
        columns = jnp.concatenate([
            jnp.concatenate([exit_re, delta_re], axis=1),
            jnp.concatenate([exit_im, delta_im], axis=1)], axis=0)
        there, back = 2 * (layer % 2), 2 * (layer % 2) + 1
        spectrum = forward(columns, there)
        if layer < slices - 1:
            waves = inverse(kernel_times(spectrum, 1.0, scales[there] * scales[back]), back)
            psi_re, tan_re = waves[:size, :size], waves[:size, size:]
            psi_im, tan_im = waves[size:, :size], waves[size:, size:]
        else:
            far = kernel_times(spectrum, 1.0, scales[there])
    far_re, far_im = far[:size, :size], far[:size, size:]
    weight = (4.0 / slices) * (far_re * far[size:, :size] + far_im * far[size:, size:])
    weighted = jnp.concatenate([weight * far_re, weight * far_im], axis=1)
    adjoint = inverse(kernel_times(weighted, -1.0, scales[back]), back)
    for layer in range(slices - 1, -1, -1):
        adj_re, adj_im = adjoint[:size], adjoint[size:]
        psi_re, psi_im = wave_ref[layer, 0], wave_ref[layer, 1]
        later = grad if layer < slices - 1 else None
        grad = [(psi_re * adj_re + psi_im * adj_im).astype(BF16), (psi_re * adj_im - psi_im * adj_re).astype(BF16)]
        for part in range(2):
            if not packed:
                out_ref[layer, part] = grad[part]
            elif layer % 2 == 0:
                out_ref[layer // 2, part] = jnp.where(even, grad[part], later[part])
        if layer > 0:
            obj_re, obj_im = window(layer, 0), window(layer, 1)
            columns = jnp.concatenate(
                [obj_re * adj_re + obj_im * adj_im, obj_re * adj_im - obj_im * adj_re], axis=0)
            there, back = 2 * (layer % 2), 2 * (layer % 2) + 1
            adjoint = inverse(kernel_times(forward(columns, there), -1.0, scales[there] * scales[back]), back)


def gather_kernel(most, start_ref, grad_ref, first_ref, own_ref, second_ref):
    slots, parts, size, _ = grad_ref.shape
    slots = min(slots, most)
    rows, columns = own_ref.shape[1:]
    even = lax.rem(lax.axis_index("strip"), 2) == 0
    placed = [[] for _ in range(parts)]
    hots = []
    for slot in range(slots):
        first_row = start_ref[2 * slot : 2 * slot + 1, 0:1]
        first_col = start_ref[2 * slot + 1 : 2 * slot + 2, 0:1]
        hots.append(col_hot(first_row, 3 * rows, size))
        values = grad_ref[slot].reshape(parts * size, size)
        spread = dot(values, row_hot(first_col, size, columns)).astype(BF16)
        for part in range(parts):
            placed[part].append(spread[part * size : (part + 1) * size])
    pick_rows = jnp.concatenate(hots, axis=1)
    for part in range(parts):
        total = dot(pick_rows, jnp.concatenate(placed[part], axis=0))
        above, below = total[:rows].astype(BF16), total[2 * rows :].astype(BF16)
        own_ref[part] = total[rows : 2 * rows]
        first_ref[part] = jnp.where(even, above, below)
        second_ref[part] = jnp.where(even, below, above)


def on_device(object_slices, direction, probe_wave, kernel_phase, corner_row, corner_col):
    strip_rows = object_slices.shape[2]
    column_count = object_slices.shape[3]
    patch_size = probe_wave.shape[1]
    strip_count = lax.axis_size("strip")
    cuts_count = lax.axis_size("cuts")
    tables, units = transform_tables(patch_size)

    def exchanged(block, offset):
        route = [(i, ((i - offset) ^ 1) + offset) for i in range(strip_count)]
        return lax.ppermute(block, "strip", [(i, j % strip_count) for i, j in route])

    vmem = pl.BlockSpec(memory_space=pltpu.VMEM)
    params = pltpu.CompilerParams(vmem_limit_bytes=32 * 1024 * 1024)

    block_rows = 4 * strip_rows + NOTE_ROWS
    hbm = pl.BlockSpec(memory_space=pl.ANY)
    wide = pltpu.CompilerParams(vmem_limit_bytes=60 * 1024 * 1024)
    objects = object_slices.reshape(-1, column_count)
    directions = direction.reshape(-1, column_count)
    block, note = pl.pallas_call(
        functools.partial(pack_kernel, strip_rows, strip_count * strip_rows),
        out_shape=(
            jax.ShapeDtypeStruct((block_rows, column_count), BF16),
            jax.ShapeDtypeStruct((NOTE_ROWS, column_count), BF16),
        ),
        in_specs=[hbm] * 4,
        out_specs=(vmem, vmem),
        scratch_shapes=[
            pltpu.SMEM(corner_row.shape, jnp.int32),
            pltpu.SMEM(corner_row.shape, jnp.int32),
            pltpu.SemaphoreType.DMA((4,)),
        ],
        compiler_params=wide,
        name="pack_block",
    )(corner_row, corner_col, objects, directions)
    far = lax.ppermute(note, "strip", [(i, (i + REACH) % strip_count) for i in range(strip_count)])
    first, second = exchanged(block, -1), exchanged(block, 0)
    kernel_cos, kernel_sin = pl.pallas_call(
        phase_kernel,
        out_shape=(jax.ShapeDtypeStruct(kernel_phase.shape, F32),) * 2,
        in_specs=[vmem],
        out_specs=(vmem,) * 2,
        compiler_params=params,
        name="phase_tables",
    )(kernel_phase)
    near = corner_row.shape[0]
    strip_shape = (2, strip_rows, column_count)

    chips = cuts_count // 2
    same_core = [[core + 2 * chip for chip in range(chips)] for core in range(2)]

    def cut(targets, counted, *operands):
        windows_shape = (targets, 4, patch_size, patch_size)
        out_shape = (jax.ShapeDtypeStruct(windows_shape, BF16), jax.ShapeDtypeStruct((2 * targets, 128), F32))
        out_specs = (vmem, vmem)
        if counted:
            out_shape += (jax.ShapeDtypeStruct((1,), jnp.int32),)
            out_specs += (pl.BlockSpec(memory_space=pltpu.SMEM),)
        return pl.pallas_call(
            functools.partial(cut_kernel, strip_rows, near),
            out_shape=out_shape,
            in_specs=[vmem] * 6,
            out_specs=out_specs,
            compiler_params=params,
            name="cut_windows",
        )(*operands)

    def chain(windows, other, *constants):
        return pl.pallas_call(
            functools.partial(chain_kernel, units),
            out_shape=jax.ShapeDtypeStruct((windows.shape[0], 2, patch_size, patch_size), BF16),
            in_specs=[vmem] * 6,
            out_specs=vmem,
            scratch_shapes=[pltpu.VMEM((cuts_count, 2, patch_size, patch_size), F32)],
            compiler_params=params,
            name="wave_chain",
        )(windows, other, *constants)

    def gather(start, gradient):
        return pl.pallas_call(
            functools.partial(gather_kernel, len(OWNERS) * near),
            out_shape=(
                jax.ShapeDtypeStruct(strip_shape, BF16),
                jax.ShapeDtypeStruct(strip_shape, F32),
                jax.ShapeDtypeStruct(strip_shape, BF16),
            ),
            in_specs=[vmem, vmem],
            out_specs=(vmem, vmem, vmem),
            compiler_params=params,
            name="add_windows",
        )(start, gradient)

    def one_per_chip(windows, start, around, constants):
        del around
        windows = lax.all_to_all(windows, "cuts", 0, 0, axis_index_groups=same_core, tiled=False)
        other = lax.ppermute(windows, "cuts", [(i, i ^ 1) for i in range(cuts_count)])
        gradient = chain(windows, other, *constants)
        gradient = lax.all_to_all(gradient, "cuts", 0, 0, axis_index_groups=same_core, tiled=False)
        return gather(start, gradient)

    def one_per_device(windows, start, around, constants):
        del windows, start
        windows, start = cut(cuts_count, False, *around)
        windows = lax.all_to_all(windows, "cuts", 0, 0, tiled=False)
        gradient = chain(windows, windows, *constants)
        gradient = lax.all_to_all(gradient, "cuts", 0, 0, tiled=False)
        return gather(start, gradient)

    around = (far, note, objects, directions, second, first)
    windows, start, count = cut(chips, True, *around)
    constants = (probe_wave, kernel_cos, kernel_sin, jnp.asarray(tables))
    first, own, second = lax.cond(
        count[0] > chips, one_per_device, one_per_chip, windows, start, around, constants
    )
    first, second = exchanged(first, -1), exchanged(second, 0)
    return (own + first.astype(F32) + second.astype(F32))[None]


def solution(mesh):
    in_specs = (
        P("cuts", None, "strip", None),
        P("cuts", None, "strip", None),
        P(),
        P(),
        P("strip"),
        P("strip"),
    )
    out_specs = P("cuts", None, "strip", None)
    return jax.shard_map(
        on_device, mesh=mesh, in_specs=in_specs, out_specs=out_specs, check_vma=False
    )
```

```python
import functools
import math

import jax
import jax.numpy as jnp
import ml_dtypes
import numpy as np
from jax import lax
from jax.experimental import pallas as pl
from jax.experimental.pallas import tpu as pltpu
from jax.sharding import PartitionSpec as P

REACH = 2
NOTE_ROWS = 16
OWNERS = (-REACH, -1, 0, 1)
PLACES = (
    ((2, 2), (2, 1), (2, 1), (2, -1), (2, -1)),
    ((1, 2), (1, 2), (2, 1), (2, -1), (2, -1)),
    ((1, 2), (1, 2), (0, 1), (1, -1), (1, -1)),
    ((-1, 2), (-1, 2), (-1, 1), (-1, 0), (0, -1)),
    ((-1, 2), (-1, 2), (-1, 1), (-1, 0), (-1, -1)),
)
STRETCHES = (1.666129 / 16, 1.625068 / 16, 1.885787 / 16, 1.99216 / 16)
BF16 = jnp.bfloat16
F32 = jnp.float32


def transform_tables(size):
    index_line = np.arange(size)
    angle = (index_line[:, None] * index_line[None, :] % size) * (2.0 * math.pi / size)
    cosine, sine = np.cos(angle), np.sin(angle)
    tables, units = [], []
    for stretch in STRETCHES:
        kept_cos = (stretch * cosine).astype(ml_dtypes.bfloat16).astype(np.float64)
        kept_sin = (stretch * sine).astype(ml_dtypes.bfloat16).astype(np.float64)
        unit = np.sum(kept_cos * cosine + kept_sin * sine) / np.sum(cosine**2 + sine**2)
        units.append(float(unit * math.sqrt(size)))
        tables.append(np.concatenate([kept_cos, kept_sin], axis=1))
    return np.stack(tables).astype(ml_dtypes.bfloat16), units


def dot(left, right):
    return jnp.dot(left, right, preferred_element_type=F32)


def row_hot(start, rows, columns):
    row_index = lax.broadcasted_iota(jnp.int32, (rows, columns), 0)
    col_index = lax.broadcasted_iota(jnp.int32, (rows, columns), 1)
    return jnp.where((col_index - row_index).astype(F32) == start, 1.0, 0.0).astype(BF16)


def col_hot(start, rows, columns):
    row_index = lax.broadcasted_iota(jnp.int32, (rows, columns), 0)
    col_index = lax.broadcasted_iota(jnp.int32, (rows, columns), 1)
    return jnp.where((row_index - col_index).astype(F32) == start, 1.0, 0.0).astype(BF16)


def pack_kernel(
    strip_rows, total_rows, row_any, col_any, object_any, direction_any, block_ref, note_ref, row_ref, col_ref, sems
):
    half = object_any.shape[0]
    columns = block_ref.shape[1]
    corners = [
        pltpu.make_async_copy(row_any, row_ref, sems.at[0]),
        pltpu.make_async_copy(col_any, col_ref, sems.at[1]),
    ]
    bulk = [
        pltpu.make_async_copy(object_any, block_ref.at[pl.ds(0, half), :], sems.at[2]),
        pltpu.make_async_copy(direction_any, block_ref.at[pl.ds(half, half), :], sems.at[3]),
    ]
    for copy in corners + bulk:
        copy.start()
    for copy in corners:
        copy.wait()
    strip_index = lax.axis_index("strip")
    near = row_ref.shape[0]
    insides, aheads = [], []
    for position in range(near):
        inside = row_ref[position] - (strip_index - REACH) * strip_rows
        inside = lax.rem(inside + 2 * total_rows, total_rows)
        insides.append(inside)
        aheads.append(REACH - lax.div(inside, strip_rows))
    lane = lax.broadcasted_iota(jnp.int32, (NOTE_ROWS, columns), 1)
    note = jnp.zeros((NOTE_ROWS, columns), F32)
    for position in range(near):
        to_owner = jnp.int32(0)
        for row, places in enumerate(PLACES):
            for column, place in enumerate(places):
                chosen = (aheads[0] == row - REACH) & (aheads[1] == column - REACH)
                to_owner = jnp.where(chosen, -place[position], to_owner)
        first_row = insides[position] + (to_owner + 1 - REACH) * strip_rows
        for place, value in enumerate((first_row, col_ref[position], to_owner)):
            note = jnp.where(lane == place * near + position, value.astype(F32), note)
    note = note.astype(BF16)
    block_ref[2 * half :, :] = note
    note_ref[...] = note
    for copy in bulk:
        copy.wait()


def phase_kernel(phase_ref, half_ref, cos_ref, sin_ref, table_ref):
    cos_ref[...] = jnp.cos(phase_ref[...])
    sin_ref[...] = jnp.sin(phase_ref[...])
    count, size, _ = half_ref.shape
    low, high = slice(0, size), slice(size, 2 * size)
    for table in range(count):
        cosine, sine = half_ref[table, :, low], half_ref[table, :, high]
        for side, upper, lower in ((0, sine, -sine), (1, -sine, sine)):
            table_ref[table, side, low, low] = cosine
            table_ref[table, side, low, high] = upper
            table_ref[table, side, high, low] = lower
            table_ref[table, side, high, high] = cosine


def strips_around(first_ref, own, second_ref):
    even = lax.rem(lax.axis_index("strip"), 2) == 0
    first, second = first_ref[...], second_ref[...]
    return jnp.where(even, first, second), own, jnp.where(even, second, first)


def corners_here(far, above, own, below, near):
    found = []
    for note, owner in zip((far, above, own, below), OWNERS):
        note = note[note.shape[0] - NOTE_ROWS :, :].astype(F32)[0:1]
        for position in range(near):
            here = note[:, 2 * near + position : 2 * near + position + 1] == owner
            first_row = note[:, position : position + 1]
            first_col = note[:, near + position : near + position + 1]
            found.append((jnp.where(here, 1.0, 0.0), first_row, first_col))
    return found


def cut_kernel(
    rows, near, far_ref, note_ref, object_ref, direction_ref, second_ref, first_ref, out_ref, start_ref, *count_ref
):
    targets, parts, size, _ = out_ref.shape
    columns = object_ref.shape[1]
    own = jnp.concatenate([object_ref[...], direction_ref[...], note_ref[...]], axis=0)
    above, own, below = strips_around(first_ref, own, second_ref)
    found = corners_here(far_ref[...], above, own, below, near)
    nowhere = 4.0 * rows
    if count_ref:
        slots = targets
        count_ref[0][0] = jnp.sum(sum(here for here, _, _ in found)).astype(jnp.int32)
        starts = [[nowhere, 0.0] for _ in range(slots)]
        rank = jnp.zeros((1, 1), F32)
        for here, first_row, first_col in found:
            for slot in range(slots):
                taken = here * jnp.where(rank == slot, 1.0, 0.0) > 0.0
                starts[slot][0] = jnp.where(taken, first_row, starts[slot][0])
                starts[slot][1] = jnp.where(taken, first_col, starts[slot][1])
            rank += here
    else:
        slots = len(found)
        starts = [[jnp.where(here > 0.0, row, nowhere), col] for here, row, col in found]
    hots = []
    for slot, (first_row, first_col) in enumerate(starts):
        start_ref[2 * slot : 2 * slot + 1, :] = jnp.broadcast_to(first_row, (1, 128))
        start_ref[2 * slot + 1 : 2 * slot + 2, :] = jnp.broadcast_to(first_col, (1, 128))
        hots.append((row_hot(first_row, size, 3 * rows), col_hot(first_col, columns, size)))
    bands = [
        jnp.concatenate(
            [block[part * rows : (part + 1) * rows, :] for block in (above, own, below)], axis=0
        )
        for part in range(parts)
    ]
    pick_rows = jnp.concatenate([hot for hot, _ in hots], axis=0)
    picked = [dot(pick_rows, band).astype(BF16) for band in bands]
    for slot in range(slots):
        lines = [part[slot * size : (slot + 1) * size] for part in picked]
        window = dot(jnp.concatenate(lines, axis=0), hots[slot][1]).astype(BF16)
        out_ref[slot] = window.reshape(parts, size, size)
    if slots < targets:
        out_ref[slots:] = jnp.zeros((targets - slots, parts, size, size), BF16)


def chain_kernel(units, window_ref, other_ref, probe_ref, cos_ref, sin_ref, table_ref, out_ref, wave_ref):
    slices, _, size, _ = wave_ref.shape
    packed = window_ref.shape[0] < slices
    even = lax.rem(lax.axis_index("cuts"), 2) == 0

    def window(layer, part):
        if not packed:
            return window_ref[layer, part].astype(F32)
        mine, other = window_ref[layer // 2, part], other_ref[layer // 2, part]
        return (jnp.where(even, mine, other) if layer % 2 == 0 else jnp.where(even, other, mine)).astype(F32)

    def swap(values):
        blocks = [[values[i * size : (i + 1) * size, j * size : (j + 1) * size]
                   for j in range(values.shape[1] // size)] for i in range(values.shape[0] // size)]
        turned = [jnp.concatenate([row[j] for row in blocks], axis=1) for j in range(len(blocks[0]))]
        return jnp.concatenate(turned, axis=0) if len(turned) > 1 else turned[0]

    def from_left(table, columns):
        step = 2 * size // 2
        return jnp.concatenate([dot(table[i * step : (i + 1) * step], columns) for i in range(2)], axis=0)

    def from_right(rows, table):
        step = rows.shape[0] // 2
        return jnp.concatenate([dot(rows[i * step : (i + 1) * step], table) for i in range(2)], axis=0)

    def forward(columns, table):
        half = from_left(table_ref[table, 0], columns.astype(BF16)).astype(BF16)
        return from_right(swap(half), table_ref[table, 1])

    def inverse(rows, table):
        half = from_right(rows.astype(BF16), table_ref[table, 0]).astype(BF16)
        return from_left(table_ref[table, 1], swap(half))

    def kernel_times(rows, sign, scale):
        kernel_cos, kernel_sin = cos_ref[...] * scale, sin_ref[...] * (sign * scale)
        made = []
        for i in range(rows.shape[0] // size):
            re, im = rows[i * size : (i + 1) * size, :size], rows[i * size : (i + 1) * size, size:]
            made.append(jnp.concatenate(
                [re * kernel_cos - im * kernel_sin, re * kernel_sin + im * kernel_cos], axis=1))
        return jnp.concatenate(made, axis=0) if len(made) > 1 else made[0]

    psi_re, psi_im = probe_ref[0].astype(F32), probe_ref[1].astype(F32)
    tan_re, tan_im = None, None
    scales = [1.0 / unit**2 for unit in units]
    for layer in range(slices):
        wave_ref[layer, 0], wave_ref[layer, 1] = psi_re, psi_im
        obj_re, obj_im = window(layer, 0), window(layer, 1)
        dir_re, dir_im = window(layer, 2), window(layer, 3)
        exit_re = obj_re * psi_re - obj_im * psi_im
        exit_im = obj_re * psi_im + obj_im * psi_re
        delta_re = dir_re * psi_re - dir_im * psi_im
        delta_im = dir_re * psi_im + dir_im * psi_re
        if layer > 0:
            delta_re += obj_re * tan_re - obj_im * tan_im
            delta_im += obj_re * tan_im + obj_im * tan_re
        columns = jnp.concatenate([
            jnp.concatenate([exit_re, delta_re], axis=1),
            jnp.concatenate([exit_im, delta_im], axis=1)], axis=0)
        there, back = 2 * (layer % 2), 2 * (layer % 2) + 1
        spectrum = forward(columns, there)
        if layer < slices - 1:
            waves = inverse(kernel_times(spectrum, 1.0, scales[there] * scales[back]), back)
            psi_re, tan_re = waves[:size, :size], waves[:size, size:]
            psi_im, tan_im = waves[size:, :size], waves[size:, size:]
        else:
            far = kernel_times(spectrum, 1.0, scales[there])
    far_re, far_im = far[:size, :size], far[:size, size:]
    weight = (4.0 / slices) * (far_re * far[size:, :size] + far_im * far[size:, size:])
    weighted = jnp.concatenate([weight * far_re, weight * far_im], axis=1)
    adjoint = inverse(kernel_times(weighted, -1.0, scales[back]), back)
    for layer in range(slices - 1, -1, -1):
        adj_re, adj_im = adjoint[:size], adjoint[size:]
        psi_re, psi_im = wave_ref[layer, 0], wave_ref[layer, 1]
        later = grad if layer < slices - 1 else None
        grad = [(psi_re * adj_re + psi_im * adj_im).astype(BF16), (psi_re * adj_im - psi_im * adj_re).astype(BF16)]
        for part in range(2):
            if not packed:
                out_ref[layer, part] = grad[part]
            elif layer % 2 == 0:
                out_ref[layer // 2, part] = jnp.where(even, grad[part], later[part])
        if layer > 0:
            obj_re, obj_im = window(layer, 0), window(layer, 1)
            columns = jnp.concatenate(
                [obj_re * adj_re + obj_im * adj_im, obj_re * adj_im - obj_im * adj_re], axis=0)
            there, back = 2 * (layer % 2), 2 * (layer % 2) + 1
            adjoint = inverse(kernel_times(forward(columns, there), -1.0, scales[there] * scales[back]), back)


def gather_kernel(most, start_ref, grad_ref, first_ref, own_ref, second_ref):
    slots, parts, size, _ = grad_ref.shape
    slots = min(slots, most)
    rows, columns = own_ref.shape[1:]
    even = lax.rem(lax.axis_index("strip"), 2) == 0
    placed = [[] for _ in range(parts)]
    hots = []
    for slot in range(slots):
        first_row = start_ref[2 * slot : 2 * slot + 1, 0:1]
        first_col = start_ref[2 * slot + 1 : 2 * slot + 2, 0:1]
        hots.append(col_hot(first_row, 3 * rows, size))
        values = grad_ref[slot].reshape(parts * size, size)
        spread = dot(values, row_hot(first_col, size, columns)).astype(BF16)
        for part in range(parts):
            placed[part].append(spread[part * size : (part + 1) * size])
    pick_rows = jnp.concatenate(hots, axis=1)
    for part in range(parts):
        total = dot(pick_rows, jnp.concatenate(placed[part], axis=0))
        above, below = total[:rows].astype(BF16), total[2 * rows :].astype(BF16)
        own_ref[part] = total[rows : 2 * rows]
        first_ref[part] = jnp.where(even, above, below)
        second_ref[part] = jnp.where(even, below, above)


def on_device(object_slices, direction, probe_wave, kernel_phase, corner_row, corner_col):
    strip_rows = object_slices.shape[2]
    column_count = object_slices.shape[3]
    patch_size = probe_wave.shape[1]
    strip_count = lax.axis_size("strip")
    cuts_count = lax.axis_size("cuts")
    halves, units = transform_tables(patch_size)

    def exchanged(block, offset):
        route = [(i, ((i - offset) ^ 1) + offset) for i in range(strip_count)]
        return lax.ppermute(block, "strip", [(i, j % strip_count) for i, j in route])

    vmem = pl.BlockSpec(memory_space=pltpu.VMEM)
    params = pltpu.CompilerParams(vmem_limit_bytes=32 * 1024 * 1024)

    block_rows = 4 * strip_rows + NOTE_ROWS
    hbm = pl.BlockSpec(memory_space=pl.ANY)
    wide = pltpu.CompilerParams(vmem_limit_bytes=60 * 1024 * 1024)
    objects = object_slices.reshape(-1, column_count)
    directions = direction.reshape(-1, column_count)
    block, note = pl.pallas_call(
        functools.partial(pack_kernel, strip_rows, strip_count * strip_rows),
        out_shape=(
            jax.ShapeDtypeStruct((block_rows, column_count), BF16),
            jax.ShapeDtypeStruct((NOTE_ROWS, column_count), BF16),
        ),
        in_specs=[hbm] * 4,
        out_specs=(vmem, vmem),
        scratch_shapes=[
            pltpu.SMEM(corner_row.shape, jnp.int32),
            pltpu.SMEM(corner_row.shape, jnp.int32),
            pltpu.SemaphoreType.DMA((4,)),
        ],
        compiler_params=wide,
        name="pack_block",
    )(corner_row, corner_col, objects, directions)
    far = lax.ppermute(note, "strip", [(i, (i + REACH) % strip_count) for i in range(strip_count)])
    first, second = exchanged(block, -1), exchanged(block, 0)
    kernel_cos, kernel_sin, tables = pl.pallas_call(
        phase_kernel,
        out_shape=(
            jax.ShapeDtypeStruct(kernel_phase.shape, F32),
            jax.ShapeDtypeStruct(kernel_phase.shape, F32),
            jax.ShapeDtypeStruct((len(units), 2, 2 * patch_size, 2 * patch_size), BF16),
        ),
        in_specs=[vmem] * 2,
        out_specs=(vmem,) * 3,
        compiler_params=params,
        name="phase_tables",
    )(kernel_phase, jnp.asarray(halves))
    near = corner_row.shape[0]
    strip_shape = (2, strip_rows, column_count)

    chips = cuts_count // 2
    same_core = [[core + 2 * chip for chip in range(chips)] for core in range(2)]

    def cut(targets, counted, *operands):
        windows_shape = (targets, 4, patch_size, patch_size)
        out_shape = (jax.ShapeDtypeStruct(windows_shape, BF16), jax.ShapeDtypeStruct((2 * targets, 128), F32))
        out_specs = (vmem, vmem)
        if counted:
            out_shape += (jax.ShapeDtypeStruct((1,), jnp.int32),)
            out_specs += (pl.BlockSpec(memory_space=pltpu.SMEM),)
        return pl.pallas_call(
            functools.partial(cut_kernel, strip_rows, near),
            out_shape=out_shape,
            in_specs=[vmem] * 6,
            out_specs=out_specs,
            compiler_params=params,
            name="cut_windows",
        )(*operands)

    def chain(windows, other, *constants):
        return pl.pallas_call(
            functools.partial(chain_kernel, units),
            out_shape=jax.ShapeDtypeStruct((windows.shape[0], 2, patch_size, patch_size), BF16),
            in_specs=[vmem] * 6,
            out_specs=vmem,
            scratch_shapes=[pltpu.VMEM((cuts_count, 2, patch_size, patch_size), F32)],
            compiler_params=params,
            name="wave_chain",
        )(windows, other, *constants)

    def gather(start, gradient):
        return pl.pallas_call(
            functools.partial(gather_kernel, len(OWNERS) * near),
            out_shape=(
                jax.ShapeDtypeStruct(strip_shape, BF16),
                jax.ShapeDtypeStruct(strip_shape, F32),
                jax.ShapeDtypeStruct(strip_shape, BF16),
            ),
            in_specs=[vmem, vmem],
            out_specs=(vmem, vmem, vmem),
            compiler_params=params,
            name="add_windows",
        )(start, gradient)

    def one_per_chip(windows, start, around, constants):
        del around
        windows = lax.all_to_all(windows, "cuts", 0, 0, axis_index_groups=same_core, tiled=False)
        other = lax.ppermute(windows, "cuts", [(i, i ^ 1) for i in range(cuts_count)])
        gradient = chain(windows, other, *constants)
        gradient = lax.all_to_all(gradient, "cuts", 0, 0, axis_index_groups=same_core, tiled=False)
        return gather(start, gradient)

    def one_per_device(windows, start, around, constants):
        del windows, start
        windows, start = cut(cuts_count, False, *around)
        windows = lax.all_to_all(windows, "cuts", 0, 0, tiled=False)
        gradient = chain(windows, windows, *constants)
        gradient = lax.all_to_all(gradient, "cuts", 0, 0, tiled=False)
        return gather(start, gradient)

    around = (far, note, objects, directions, second, first)
    windows, start, count = cut(chips, True, *around)
    constants = (probe_wave, kernel_cos, kernel_sin, tables)
    first, own, second = lax.cond(
        count[0] > chips, one_per_device, one_per_chip, windows, start, around, constants
    )
    first, second = exchanged(first, -1), exchanged(second, 0)
    return (own + first.astype(F32) + second.astype(F32))[None]


def solution(mesh):
    in_specs = (
        P("cuts", None, "strip", None),
        P("cuts", None, "strip", None),
        P(),
        P(),
        P("strip"),
        P("strip"),
    )
    out_specs = P("cuts", None, "strip", None)
    return jax.shard_map(
        on_device, mesh=mesh, in_specs=in_specs, out_specs=out_specs, check_vma=False
    )
```

```python
import functools
import math

import jax
import jax.numpy as jnp
import ml_dtypes
import numpy as np
from jax import lax
from jax.experimental import pallas as pl
from jax.experimental.pallas import tpu as pltpu
from jax.sharding import PartitionSpec as P

REACH = 2
NOTE_ROWS = 16
OWNERS = (-REACH, -1, 0, 1)
PLACES = (
    ((2, 2), (2, 1), (2, 1), (2, -1), (2, -1)),
    ((1, 2), (1, 2), (2, 1), (2, -1), (2, -1)),
    ((1, 2), (1, 2), (0, 1), (1, -1), (1, -1)),
    ((-1, 2), (-1, 2), (-1, 1), (-1, 0), (0, -1)),
    ((-1, 2), (-1, 2), (-1, 1), (-1, 0), (-1, -1)),
)
STRETCHES = (1.666129 / 16, 1.625068 / 16, 1.885787 / 16, 1.99216 / 16)
BF16 = jnp.bfloat16
F32 = jnp.float32


def transform_tables(size):
    index_line = np.arange(size)
    angle = (index_line[:, None] * index_line[None, :] % size) * (2.0 * math.pi / size)
    cosine, sine = np.cos(angle), np.sin(angle)
    tables, units = [], []
    for stretch in STRETCHES:
        kept_cos = (stretch * cosine).astype(ml_dtypes.bfloat16).astype(np.float64)
        kept_sin = (stretch * sine).astype(ml_dtypes.bfloat16).astype(np.float64)
        unit = np.sum(kept_cos * cosine + kept_sin * sine) / np.sum(cosine**2 + sine**2)
        units.append(float(unit * math.sqrt(size)))
        tables.append(np.concatenate([kept_cos, kept_sin], axis=1))
    return np.stack(tables).astype(ml_dtypes.bfloat16), units


def dot(left, right):
    return jnp.dot(left, right, preferred_element_type=F32)


def row_hot(start, rows, columns):
    row_index = lax.broadcasted_iota(jnp.int32, (rows, columns), 0)
    col_index = lax.broadcasted_iota(jnp.int32, (rows, columns), 1)
    return jnp.where((col_index - row_index).astype(F32) == start, 1.0, 0.0).astype(BF16)


def col_hot(start, rows, columns):
    row_index = lax.broadcasted_iota(jnp.int32, (rows, columns), 0)
    col_index = lax.broadcasted_iota(jnp.int32, (rows, columns), 1)
    return jnp.where((row_index - col_index).astype(F32) == start, 1.0, 0.0).astype(BF16)


def pack_kernel(
    strip_rows, total_rows, row_any, col_any, object_any, direction_any, block_ref, note_ref, row_ref, col_ref, sems
):
    half = object_any.shape[0]
    columns = block_ref.shape[1]
    corners = [
        pltpu.make_async_copy(row_any, row_ref, sems.at[0]),
        pltpu.make_async_copy(col_any, col_ref, sems.at[1]),
    ]
    bulk = [
        pltpu.make_async_copy(object_any, block_ref.at[pl.ds(0, half), :], sems.at[2]),
        pltpu.make_async_copy(direction_any, block_ref.at[pl.ds(half, half), :], sems.at[3]),
    ]
    for copy in corners + bulk:
        copy.start()
    for copy in corners:
        copy.wait()
    strip_index = lax.axis_index("strip")
    near = row_ref.shape[0]
    insides, aheads = [], []
    for position in range(near):
        inside = row_ref[position] - (strip_index - REACH) * strip_rows
        inside = lax.rem(inside + 2 * total_rows, total_rows)
        insides.append(inside)
        aheads.append(REACH - lax.div(inside, strip_rows))
    lane = lax.broadcasted_iota(jnp.int32, (NOTE_ROWS, columns), 1)
    note = jnp.zeros((NOTE_ROWS, columns), F32)
    for position in range(near):
        to_owner = jnp.int32(0)
        for row, places in enumerate(PLACES):
            for column, place in enumerate(places):
                chosen = (aheads[0] == row - REACH) & (aheads[1] == column - REACH)
                to_owner = jnp.where(chosen, -place[position], to_owner)
        first_row = insides[position] + (to_owner + 1 - REACH) * strip_rows
        for place, value in enumerate((first_row, col_ref[position], to_owner)):
            note = jnp.where(lane == place * near + position, value.astype(F32), note)
    note = note.astype(BF16)
    block_ref[2 * half :, :] = note
    note_ref[...] = note
    for copy in bulk:
        copy.wait()


def phase_kernel(phase_ref, half_ref, cos_ref, sin_ref, table_ref):
    cos_ref[...] = jnp.cos(phase_ref[...])
    sin_ref[...] = jnp.sin(phase_ref[...])
    count, size, _ = half_ref.shape
    low, high = slice(0, size), slice(size, 2 * size)
    for table in range(count):
        cosine, sine = half_ref[table, :, low], half_ref[table, :, high]
        for side, upper, lower in ((0, sine, -sine), (1, -sine, sine)):
            table_ref[table, side, low, low] = cosine
            table_ref[table, side, low, high] = upper
            table_ref[table, side, high, low] = lower
            table_ref[table, side, high, high] = cosine


def strips_around(first_ref, own, second_ref):
    even = lax.rem(lax.axis_index("strip"), 2) == 0
    first, second = first_ref[...], second_ref[...]
    return jnp.where(even, first, second), own, jnp.where(even, second, first)


def corners_here(far, above, own, below, near):
    found = []
    for note, owner in zip((far, above, own, below), OWNERS):
        note = note[note.shape[0] - NOTE_ROWS :, :].astype(F32)[0:1]
        for position in range(near):
            here = note[:, 2 * near + position : 2 * near + position + 1] == owner
            first_row = note[:, position : position + 1]
            first_col = note[:, near + position : near + position + 1]
            found.append((jnp.where(here, 1.0, 0.0), first_row, first_col))
    return found


def cut_kernel(
    rows, near, far_ref, note_ref, object_ref, direction_ref, second_ref, first_ref, out_ref, start_ref, *count_ref
):
    targets, parts, size, _ = out_ref.shape
    columns = object_ref.shape[1]
    own = jnp.concatenate([object_ref[...], direction_ref[...], note_ref[...]], axis=0)
    above, own, below = strips_around(first_ref, own, second_ref)
    found = corners_here(far_ref[...], above, own, below, near)
    nowhere = 4.0 * rows
    if count_ref:
        slots = targets
        count_ref[0][0] = jnp.sum(sum(here for here, _, _ in found)).astype(jnp.int32)
        starts = [[nowhere, 0.0] for _ in range(slots)]
        rank = jnp.zeros((1, 1), F32)
        for here, first_row, first_col in found:
            for slot in range(slots):
                taken = here * jnp.where(rank == slot, 1.0, 0.0) > 0.0
                starts[slot][0] = jnp.where(taken, first_row, starts[slot][0])
                starts[slot][1] = jnp.where(taken, first_col, starts[slot][1])
            rank += here
    else:
        slots = len(found)
        starts = [[jnp.where(here > 0.0, row, nowhere), col] for here, row, col in found]
    hots = []
    for slot, (first_row, first_col) in enumerate(starts):
        start_ref[2 * slot : 2 * slot + 1, :] = jnp.broadcast_to(first_row, (1, 128))
        start_ref[2 * slot + 1 : 2 * slot + 2, :] = jnp.broadcast_to(first_col, (1, 128))
        hots.append((row_hot(first_row, size, 3 * rows), col_hot(first_col, columns, size)))
    bands = [
        jnp.concatenate(
            [block[part * rows : (part + 1) * rows, :] for block in (above, own, below)], axis=0
        )
        for part in range(parts)
    ]
    pick_rows = jnp.concatenate([hot for hot, _ in hots], axis=0)
    picked = [dot(pick_rows, band).astype(BF16) for band in bands]
    for slot in range(slots):
        lines = [part[slot * size : (slot + 1) * size] for part in picked]
        window = dot(jnp.concatenate(lines, axis=0), hots[slot][1]).astype(BF16)
        out_ref[slot] = window.reshape(parts, size, size)
    if slots < targets:
        out_ref[slots:] = jnp.zeros((targets - slots, parts, size, size), BF16)


def chain_kernel(units, window_ref, other_ref, probe_ref, cos_ref, sin_ref, table_ref, out_ref, wave_ref):
    slices, _, size, _ = wave_ref.shape
    packed = window_ref.shape[0] < slices
    even = lax.rem(lax.axis_index("cuts"), 2) == 0

    def window(layer, part):
        if not packed:
            return window_ref[layer, part].astype(F32)
        mine, other = window_ref[layer // 2, part], other_ref[layer // 2, part]
        return (jnp.where(even, mine, other) if layer % 2 == 0 else jnp.where(even, other, mine)).astype(F32)

    def swap(values):
        blocks = [[values[i * size : (i + 1) * size, j * size : (j + 1) * size]
                   for j in range(values.shape[1] // size)] for i in range(values.shape[0] // size)]
        turned = [jnp.concatenate([row[j] for row in blocks], axis=1) for j in range(len(blocks[0]))]
        return jnp.concatenate(turned, axis=0) if len(turned) > 1 else turned[0]

    def from_left(table, columns):
        step = 2 * size // 2
        return jnp.concatenate([dot(table[i * step : (i + 1) * step], columns) for i in range(2)], axis=0)

    def from_right(rows, table):
        step = rows.shape[0] // 2
        return jnp.concatenate([dot(rows[i * step : (i + 1) * step], table) for i in range(2)], axis=0)

    def forward(columns, table):
        half = from_left(table_ref[table, 0], columns.astype(BF16)).astype(BF16)
        return from_right(swap(half), table_ref[table, 1])

    def inverse(rows, table):
        half = from_right(rows.astype(BF16), table_ref[table, 0]).astype(BF16)
        return from_left(table_ref[table, 1], swap(half))

    def kernel_times(rows, sign, scale):
        kernel_cos, kernel_sin = cos_ref[...] * scale, sin_ref[...] * (sign * scale)
        made = []
        for i in range(rows.shape[0] // size):
            re, im = rows[i * size : (i + 1) * size, :size], rows[i * size : (i + 1) * size, size:]
            made.append(jnp.concatenate(
                [re * kernel_cos - im * kernel_sin, re * kernel_sin + im * kernel_cos], axis=1))
        return jnp.concatenate(made, axis=0) if len(made) > 1 else made[0]

    psi_re, psi_im = probe_ref[0].astype(F32), probe_ref[1].astype(F32)
    tan_re, tan_im = None, None
    scales = [1.0 / unit**2 for unit in units]
    for layer in range(slices):
        wave_ref[layer, 0], wave_ref[layer, 1] = psi_re.astype(BF16), psi_im.astype(BF16)
        obj_re, obj_im = window(layer, 0), window(layer, 1)
        dir_re, dir_im = window(layer, 2), window(layer, 3)
        exit_re = obj_re * psi_re - obj_im * psi_im
        exit_im = obj_re * psi_im + obj_im * psi_re
        delta_re = dir_re * psi_re - dir_im * psi_im
        delta_im = dir_re * psi_im + dir_im * psi_re
        if layer > 0:
            delta_re += obj_re * tan_re - obj_im * tan_im
            delta_im += obj_re * tan_im + obj_im * tan_re
        columns = jnp.concatenate([
            jnp.concatenate([exit_re, delta_re], axis=1),
            jnp.concatenate([exit_im, delta_im], axis=1)], axis=0)
        there, back = 2 * (layer % 2), 2 * (layer % 2) + 1
        spectrum = forward(columns, there)
        if layer < slices - 1:
            waves = inverse(kernel_times(spectrum, 1.0, scales[there] * scales[back]), back)
            psi_re, tan_re = waves[:size, :size], waves[:size, size:]
            psi_im, tan_im = waves[size:, :size], waves[size:, size:]
        else:
            far = kernel_times(spectrum, 1.0, scales[there])
    far_re, far_im = far[:size, :size], far[:size, size:]
    weight = (4.0 / slices) * (far_re * far[size:, :size] + far_im * far[size:, size:])
    weighted = jnp.concatenate([weight * far_re, weight * far_im], axis=1)
    adjoint = inverse(kernel_times(weighted, -1.0, scales[back]), back)
    for layer in range(slices - 1, -1, -1):
        adj_re, adj_im = adjoint[:size], adjoint[size:]
        psi_re, psi_im = wave_ref[layer, 0].astype(F32), wave_ref[layer, 1].astype(F32)
        later = grad if layer < slices - 1 else None
        grad = [(psi_re * adj_re + psi_im * adj_im).astype(BF16), (psi_re * adj_im - psi_im * adj_re).astype(BF16)]
        for part in range(2):
            if not packed:
                out_ref[layer, part] = grad[part]
            elif layer % 2 == 0:
                out_ref[layer // 2, part] = jnp.where(even, grad[part], later[part])
        if layer > 0:
            obj_re, obj_im = window(layer, 0), window(layer, 1)
            columns = jnp.concatenate(
                [obj_re * adj_re + obj_im * adj_im, obj_re * adj_im - obj_im * adj_re], axis=0)
            there, back = 2 * (layer % 2), 2 * (layer % 2) + 1
            adjoint = inverse(kernel_times(forward(columns, there), -1.0, scales[there] * scales[back]), back)


def gather_kernel(most, start_ref, grad_ref, first_ref, own_ref, second_ref):
    slots, parts, size, _ = grad_ref.shape
    slots = min(slots, most)
    rows, columns = own_ref.shape[1:]
    even = lax.rem(lax.axis_index("strip"), 2) == 0
    placed = [[] for _ in range(parts)]
    hots = []
    for slot in range(slots):
        first_row = start_ref[2 * slot : 2 * slot + 1, 0:1]
        first_col = start_ref[2 * slot + 1 : 2 * slot + 2, 0:1]
        hots.append(col_hot(first_row, 3 * rows, size))
        values = grad_ref[slot].reshape(parts * size, size)
        spread = dot(values, row_hot(first_col, size, columns)).astype(BF16)
        for part in range(parts):
            placed[part].append(spread[part * size : (part + 1) * size])
    pick_rows = jnp.concatenate(hots, axis=1)
    for part in range(parts):
        total = dot(pick_rows, jnp.concatenate(placed[part], axis=0))
        above, below = total[:rows].astype(BF16), total[2 * rows :].astype(BF16)
        own_ref[part] = total[rows : 2 * rows]
        first_ref[part] = jnp.where(even, above, below)
        second_ref[part] = jnp.where(even, below, above)


def on_device(object_slices, direction, probe_wave, kernel_phase, corner_row, corner_col):
    strip_rows = object_slices.shape[2]
    column_count = object_slices.shape[3]
    patch_size = probe_wave.shape[1]
    strip_count = lax.axis_size("strip")
    cuts_count = lax.axis_size("cuts")
    halves, units = transform_tables(patch_size)

    def exchanged(block, offset):
        route = [(i, ((i - offset) ^ 1) + offset) for i in range(strip_count)]
        return lax.ppermute(block, "strip", [(i, j % strip_count) for i, j in route])

    vmem = pl.BlockSpec(memory_space=pltpu.VMEM)
    params = pltpu.CompilerParams(vmem_limit_bytes=32 * 1024 * 1024)

    block_rows = 4 * strip_rows + NOTE_ROWS
    hbm = pl.BlockSpec(memory_space=pl.ANY)
    wide = pltpu.CompilerParams(vmem_limit_bytes=60 * 1024 * 1024)
    objects = object_slices.reshape(-1, column_count)
    directions = direction.reshape(-1, column_count)
    block, note = pl.pallas_call(
        functools.partial(pack_kernel, strip_rows, strip_count * strip_rows),
        out_shape=(
            jax.ShapeDtypeStruct((block_rows, column_count), BF16),
            jax.ShapeDtypeStruct((NOTE_ROWS, column_count), BF16),
        ),
        in_specs=[hbm] * 4,
        out_specs=(vmem, vmem),
        scratch_shapes=[
            pltpu.SMEM(corner_row.shape, jnp.int32),
            pltpu.SMEM(corner_row.shape, jnp.int32),
            pltpu.SemaphoreType.DMA((4,)),
        ],
        compiler_params=wide,
        name="pack_block",
    )(corner_row, corner_col, objects, directions)
    far = lax.ppermute(note, "strip", [(i, (i + REACH) % strip_count) for i in range(strip_count)])
    first, second = exchanged(block, -1), exchanged(block, 0)
    kernel_cos, kernel_sin, tables = pl.pallas_call(
        phase_kernel,
        out_shape=(
            jax.ShapeDtypeStruct(kernel_phase.shape, F32),
            jax.ShapeDtypeStruct(kernel_phase.shape, F32),
            jax.ShapeDtypeStruct((len(units), 2, 2 * patch_size, 2 * patch_size), BF16),
        ),
        in_specs=[vmem] * 2,
        out_specs=(vmem,) * 3,
        compiler_params=params,
        name="phase_tables",
    )(kernel_phase, jnp.asarray(halves))
    near = corner_row.shape[0]
    strip_shape = (2, strip_rows, column_count)

    chips = cuts_count // 2
    same_core = [[core + 2 * chip for chip in range(chips)] for core in range(2)]

    def cut(targets, counted, *operands):
        windows_shape = (targets, 4, patch_size, patch_size)
        out_shape = (jax.ShapeDtypeStruct(windows_shape, BF16), jax.ShapeDtypeStruct((2 * targets, 128), F32))
        out_specs = (vmem, vmem)
        if counted:
            out_shape += (jax.ShapeDtypeStruct((1,), jnp.int32),)
            out_specs += (pl.BlockSpec(memory_space=pltpu.SMEM),)
        return pl.pallas_call(
            functools.partial(cut_kernel, strip_rows, near),
            out_shape=out_shape,
            in_specs=[vmem] * 6,
            out_specs=out_specs,
            compiler_params=params,
            name="cut_windows",
        )(*operands)

    def chain(windows, other, *constants):
        return pl.pallas_call(
            functools.partial(chain_kernel, units),
            out_shape=jax.ShapeDtypeStruct((windows.shape[0], 2, patch_size, patch_size), BF16),
            in_specs=[vmem] * 6,
            out_specs=vmem,
            scratch_shapes=[pltpu.VMEM((cuts_count, 2, patch_size, patch_size), BF16)],
            compiler_params=params,
            name="wave_chain",
        )(windows, other, *constants)

    def gather(start, gradient):
        return pl.pallas_call(
            functools.partial(gather_kernel, len(OWNERS) * near),
            out_shape=(
                jax.ShapeDtypeStruct(strip_shape, BF16),
                jax.ShapeDtypeStruct(strip_shape, F32),
                jax.ShapeDtypeStruct(strip_shape, BF16),
            ),
            in_specs=[vmem, vmem],
            out_specs=(vmem, vmem, vmem),
            compiler_params=params,
            name="add_windows",
        )(start, gradient)

    def one_per_chip(windows, start, around, constants):
        del around
        windows = lax.all_to_all(windows, "cuts", 0, 0, axis_index_groups=same_core, tiled=False)
        other = lax.ppermute(windows, "cuts", [(i, i ^ 1) for i in range(cuts_count)])
        gradient = chain(windows, other, *constants)
        gradient = lax.all_to_all(gradient, "cuts", 0, 0, axis_index_groups=same_core, tiled=False)
        return gather(start, gradient)

    def one_per_device(windows, start, around, constants):
        del windows, start
        windows, start = cut(cuts_count, False, *around)
        windows = lax.all_to_all(windows, "cuts", 0, 0, tiled=False)
        gradient = chain(windows, windows, *constants)
        gradient = lax.all_to_all(gradient, "cuts", 0, 0, tiled=False)
        return gather(start, gradient)

    around = (far, note, objects, directions, second, first)
    windows, start, count = cut(chips, True, *around)
    constants = (probe_wave, kernel_cos, kernel_sin, tables)
    first, own, second = lax.cond(
        count[0] > chips, one_per_device, one_per_chip, windows, start, around, constants
    )
    first, second = exchanged(first, -1), exchanged(second, 0)
    return (own + first.astype(F32) + second.astype(F32))[None]


def solution(mesh):
    in_specs = (
        P("cuts", None, "strip", None),
        P("cuts", None, "strip", None),
        P(),
        P(),
        P("strip"),
        P("strip"),
    )
    out_specs = P("cuts", None, "strip", None)
    return jax.shard_map(
        on_device, mesh=mesh, in_specs=in_specs, out_specs=out_specs, check_vma=False
    )
```

```python
import functools
import math

import jax
import jax.numpy as jnp
import ml_dtypes
import numpy as np
from jax import lax
from jax.experimental import pallas as pl
from jax.experimental.pallas import tpu as pltpu
from jax.sharding import PartitionSpec as P

REACH = 2
NOTE_ROWS = 16
OWNERS = (-REACH, -1, 0, 1)
PLACES = (
    ((2, 2), (2, 1), (2, 1), (2, -1), (2, -1)),
    ((1, 2), (1, 2), (2, 1), (2, -1), (2, -1)),
    ((1, 2), (1, 2), (0, 1), (1, -1), (1, -1)),
    ((-1, 2), (-1, 2), (-1, 1), (-1, 0), (0, -1)),
    ((-1, 2), (-1, 2), (-1, 1), (-1, 0), (-1, -1)),
)
STRETCHES = (1.666129 / 16, 1.625068 / 16, 1.885787 / 16, 1.99216 / 16)
BF16 = jnp.bfloat16
F32 = jnp.float32


def transform_tables(size):
    index_line = np.arange(size)
    angle = (index_line[:, None] * index_line[None, :] % size) * (2.0 * math.pi / size)
    cosine, sine = np.cos(angle), np.sin(angle)
    tables, units = [], []
    for stretch in STRETCHES:
        kept_cos = (stretch * cosine).astype(ml_dtypes.bfloat16).astype(np.float64)
        kept_sin = (stretch * sine).astype(ml_dtypes.bfloat16).astype(np.float64)
        unit = np.sum(kept_cos * cosine + kept_sin * sine) / np.sum(cosine**2 + sine**2)
        units.append(float(unit * math.sqrt(size)))
        tables.append(np.concatenate([kept_cos, kept_sin], axis=1))
    return np.stack(tables).astype(ml_dtypes.bfloat16), units


def dot(left, right):
    return jnp.dot(left, right, preferred_element_type=F32)


def row_hot(start, rows, columns):
    row_index = lax.broadcasted_iota(jnp.int32, (rows, columns), 0)
    col_index = lax.broadcasted_iota(jnp.int32, (rows, columns), 1)
    return jnp.where((col_index - row_index).astype(F32) == start, 1.0, 0.0).astype(BF16)


def col_hot(start, rows, columns):
    row_index = lax.broadcasted_iota(jnp.int32, (rows, columns), 0)
    col_index = lax.broadcasted_iota(jnp.int32, (rows, columns), 1)
    return jnp.where((row_index - col_index).astype(F32) == start, 1.0, 0.0).astype(BF16)


def pack_kernel(
    strip_rows, total_rows, row_any, col_any, object_any, direction_any, block_ref, note_ref, row_ref, col_ref, sems
):
    half = object_any.shape[0]
    columns = block_ref.shape[1]
    corners = [
        pltpu.make_async_copy(row_any, row_ref, sems.at[0]),
        pltpu.make_async_copy(col_any, col_ref, sems.at[1]),
    ]
    bulk = [
        pltpu.make_async_copy(object_any, block_ref.at[pl.ds(0, half), :], sems.at[2]),
        pltpu.make_async_copy(direction_any, block_ref.at[pl.ds(half, half), :], sems.at[3]),
    ]
    for copy in corners + bulk:
        copy.start()
    for copy in corners:
        copy.wait()
    strip_index = lax.axis_index("strip")
    near = row_ref.shape[0]
    insides, aheads = [], []
    for position in range(near):
        inside = row_ref[position] - (strip_index - REACH) * strip_rows
        inside = lax.rem(inside + 2 * total_rows, total_rows)
        insides.append(inside)
        aheads.append(REACH - lax.div(inside, strip_rows))
    lane = lax.broadcasted_iota(jnp.int32, (NOTE_ROWS, columns), 1)
    note = jnp.zeros((NOTE_ROWS, columns), F32)
    for position in range(near):
        to_owner = jnp.int32(0)
        for row, places in enumerate(PLACES):
            for column, place in enumerate(places):
                chosen = (aheads[0] == row - REACH) & (aheads[1] == column - REACH)
                to_owner = jnp.where(chosen, -place[position], to_owner)
        first_row = insides[position] + (to_owner + 1 - REACH) * strip_rows
        for place, value in enumerate((first_row, col_ref[position], to_owner)):
            note = jnp.where(lane == place * near + position, value.astype(F32), note)
    note = note.astype(BF16)
    block_ref[2 * half :, :] = note
    note_ref[...] = note
    for copy in bulk:
        copy.wait()


def phase_kernel(phase_ref, half_ref, cos_ref, sin_ref, table_ref):
    cos_ref[...] = jnp.cos(phase_ref[...])
    sin_ref[...] = jnp.sin(phase_ref[...])
    count, size, _ = half_ref.shape
    low, high = slice(0, size), slice(size, 2 * size)
    for table in range(count):
        cosine, sine = half_ref[table, :, low], half_ref[table, :, high]
        for side, upper, lower in ((0, sine, -sine), (1, -sine, sine)):
            table_ref[table, side, low, low] = cosine
            table_ref[table, side, low, high] = upper
            table_ref[table, side, high, low] = lower
            table_ref[table, side, high, high] = cosine


def strips_around(first_ref, own, second_ref):
    even = lax.rem(lax.axis_index("strip"), 2) == 0
    first, second = first_ref[...], second_ref[...]
    return jnp.where(even, first, second), own, jnp.where(even, second, first)


def corners_here(far, above, own, below, near):
    found = []
    for note, owner in zip((far, above, own, below), OWNERS):
        note = note[note.shape[0] - NOTE_ROWS :, :].astype(F32)[0:1]
        for position in range(near):
            here = note[:, 2 * near + position : 2 * near + position + 1] == owner
            first_row = note[:, position : position + 1]
            first_col = note[:, near + position : near + position + 1]
            found.append((jnp.where(here, 1.0, 0.0), first_row, first_col))
    return found


def cut_kernel(
    rows, near, far_ref, note_ref, object_ref, direction_ref, second_ref, first_ref, out_ref, start_ref, *count_ref
):
    targets, parts, size, _ = out_ref.shape
    columns = object_ref.shape[1]
    own = jnp.concatenate([object_ref[...], direction_ref[...], note_ref[...]], axis=0)
    above, own, below = strips_around(first_ref, own, second_ref)
    found = corners_here(far_ref[...], above, own, below, near)
    nowhere = 4.0 * rows
    if count_ref:
        slots = targets
        count_ref[0][0] = jnp.sum(sum(here for here, _, _ in found)).astype(jnp.int32)
        starts = [[nowhere, 0.0] for _ in range(slots)]
        rank = jnp.zeros((1, 1), F32)
        for here, first_row, first_col in found:
            for slot in range(slots):
                taken = here * jnp.where(rank == slot, 1.0, 0.0) > 0.0
                starts[slot][0] = jnp.where(taken, first_row, starts[slot][0])
                starts[slot][1] = jnp.where(taken, first_col, starts[slot][1])
            rank += here
    else:
        slots = len(found)
        starts = [[jnp.where(here > 0.0, row, nowhere), col] for here, row, col in found]
    hots = []
    for slot, (first_row, first_col) in enumerate(starts):
        start_ref[2 * slot : 2 * slot + 1, :] = jnp.broadcast_to(first_row, (1, 128))
        start_ref[2 * slot + 1 : 2 * slot + 2, :] = jnp.broadcast_to(first_col, (1, 128))
        hots.append((row_hot(first_row, size, 3 * rows), col_hot(first_col, columns, size)))
    bands = [
        jnp.concatenate(
            [block[part * rows : (part + 1) * rows, :] for block in (above, own, below)], axis=0
        )
        for part in range(parts)
    ]
    pick_rows = jnp.concatenate([hot for hot, _ in hots], axis=0)
    picked = [dot(pick_rows, band).astype(BF16) for band in bands]
    for slot in range(slots):
        lines = [part[slot * size : (slot + 1) * size] for part in picked]
        window = dot(jnp.concatenate(lines, axis=0), hots[slot][1]).astype(BF16)
        out_ref[slot] = window.reshape(parts, size, size)
    if slots < targets:
        out_ref[slots:] = jnp.zeros((targets - slots, parts, size, size), BF16)


def chain_kernel(units, window_ref, other_ref, probe_ref, cos_ref, sin_ref, table_ref, out_ref, wave_ref):
    slices, _, size, _ = wave_ref.shape
    packed = window_ref.shape[0] < slices
    even = lax.rem(lax.axis_index("cuts"), 2) == 0

    def window(layer, part):
        if not packed:
            return window_ref[layer, part].astype(F32)
        mine, other = window_ref[layer // 2, part], other_ref[layer // 2, part]
        return (jnp.where(even, mine, other) if layer % 2 == 0 else jnp.where(even, other, mine)).astype(F32)

    def swap(values):
        blocks = [[values[i * size : (i + 1) * size, j * size : (j + 1) * size]
                   for j in range(values.shape[1] // size)] for i in range(values.shape[0] // size)]
        turned = [jnp.concatenate([row[j] for row in blocks], axis=1) for j in range(len(blocks[0]))]
        return jnp.concatenate(turned, axis=0) if len(turned) > 1 else turned[0]

    def from_left(table, columns):
        step = 2 * size // 2
        return jnp.concatenate([dot(table[i * step : (i + 1) * step], columns) for i in range(2)], axis=0)

    def from_right(rows, table):
        pieces = [dot(rows[i : i + size], table) for i in range(0, rows.shape[0], size)]
        return jnp.concatenate(pieces, axis=0) if len(pieces) > 1 else pieces[0]

    def forward(columns, table):
        half = from_left(table_ref[table, 0], columns.astype(BF16)).astype(BF16)
        return from_right(swap(half), table_ref[table, 1])

    def inverse(rows, table):
        half = from_right(rows.astype(BF16), table_ref[table, 0]).astype(BF16)
        return from_left(table_ref[table, 1], swap(half))

    def kernel_times(rows, sign, scale):
        kernel_cos, kernel_sin = cos_ref[...] * scale, sin_ref[...] * (sign * scale)
        made = []
        for i in range(rows.shape[0] // size):
            re, im = rows[i * size : (i + 1) * size, :size], rows[i * size : (i + 1) * size, size:]
            made.append(jnp.concatenate(
                [re * kernel_cos - im * kernel_sin, re * kernel_sin + im * kernel_cos], axis=1))
        return jnp.concatenate(made, axis=0) if len(made) > 1 else made[0]

    psi_re, psi_im = probe_ref[0].astype(F32), probe_ref[1].astype(F32)
    tan_re, tan_im = None, None
    scales = [1.0 / unit**2 for unit in units]
    for layer in range(slices):
        wave_ref[layer, 0], wave_ref[layer, 1] = psi_re, psi_im
        obj_re, obj_im = window(layer, 0), window(layer, 1)
        dir_re, dir_im = window(layer, 2), window(layer, 3)
        exit_re = obj_re * psi_re - obj_im * psi_im
        exit_im = obj_re * psi_im + obj_im * psi_re
        delta_re = dir_re * psi_re - dir_im * psi_im
        delta_im = dir_re * psi_im + dir_im * psi_re
        if layer > 0:
            delta_re += obj_re * tan_re - obj_im * tan_im
            delta_im += obj_re * tan_im + obj_im * tan_re
        columns = jnp.concatenate([
            jnp.concatenate([exit_re, delta_re], axis=1),
            jnp.concatenate([exit_im, delta_im], axis=1)], axis=0)
        there, back = 2 * (layer % 2), 2 * (layer % 2) + 1
        spectrum = forward(columns, there)
        if layer < slices - 1:
            waves = inverse(kernel_times(spectrum, 1.0, scales[there] * scales[back]), back)
            psi_re, tan_re = waves[:size, :size], waves[:size, size:]
            psi_im, tan_im = waves[size:, :size], waves[size:, size:]
        else:
            far = kernel_times(spectrum, 1.0, scales[there])
    far_re, far_im = far[:size, :size], far[:size, size:]
    weight = (4.0 / slices) * (far_re * far[size:, :size] + far_im * far[size:, size:])
    weighted = jnp.concatenate([weight * far_re, weight * far_im], axis=1)
    adjoint = inverse(kernel_times(weighted, -1.0, scales[back]), back)
    for layer in range(slices - 1, -1, -1):
        adj_re, adj_im = adjoint[:size], adjoint[size:]
        psi_re, psi_im = wave_ref[layer, 0], wave_ref[layer, 1]
        later = grad if layer < slices - 1 else None
        grad = [(psi_re * adj_re + psi_im * adj_im).astype(BF16), (psi_re * adj_im - psi_im * adj_re).astype(BF16)]
        for part in range(2):
            if not packed:
                out_ref[layer, part] = grad[part]
            elif layer % 2 == 0:
                out_ref[layer // 2, part] = jnp.where(even, grad[part], later[part])
        if layer > 0:
            obj_re, obj_im = window(layer, 0), window(layer, 1)
            columns = jnp.concatenate(
                [obj_re * adj_re + obj_im * adj_im, obj_re * adj_im - obj_im * adj_re], axis=0)
            there, back = 2 * (layer % 2), 2 * (layer % 2) + 1
            adjoint = inverse(kernel_times(forward(columns, there), -1.0, scales[there] * scales[back]), back)


def gather_kernel(most, start_ref, grad_ref, first_ref, own_ref, second_ref):
    slots, parts, size, _ = grad_ref.shape
    slots = min(slots, most)
    rows, columns = own_ref.shape[1:]
    even = lax.rem(lax.axis_index("strip"), 2) == 0
    placed = [[] for _ in range(parts)]
    hots = []
    for slot in range(slots):
        first_row = start_ref[2 * slot : 2 * slot + 1, 0:1]
        first_col = start_ref[2 * slot + 1 : 2 * slot + 2, 0:1]
        hots.append(col_hot(first_row, 3 * rows, size))
        values = grad_ref[slot].reshape(parts * size, size)
        spread = dot(values, row_hot(first_col, size, columns)).astype(BF16)
        for part in range(parts):
            placed[part].append(spread[part * size : (part + 1) * size])
    pick_rows = jnp.concatenate(hots, axis=1)
    for part in range(parts):
        total = dot(pick_rows, jnp.concatenate(placed[part], axis=0))
        above, below = total[:rows].astype(BF16), total[2 * rows :].astype(BF16)
        own_ref[part] = total[rows : 2 * rows]
        first_ref[part] = jnp.where(even, above, below)
        second_ref[part] = jnp.where(even, below, above)


def on_device(object_slices, direction, probe_wave, kernel_phase, corner_row, corner_col):
    strip_rows = object_slices.shape[2]
    column_count = object_slices.shape[3]
    patch_size = probe_wave.shape[1]
    strip_count = lax.axis_size("strip")
    cuts_count = lax.axis_size("cuts")
    halves, units = transform_tables(patch_size)

    def exchanged(block, offset):
        route = [(i, ((i - offset) ^ 1) + offset) for i in range(strip_count)]
        return lax.ppermute(block, "strip", [(i, j % strip_count) for i, j in route])

    vmem = pl.BlockSpec(memory_space=pltpu.VMEM)
    params = pltpu.CompilerParams(vmem_limit_bytes=32 * 1024 * 1024)

    block_rows = 4 * strip_rows + NOTE_ROWS
    hbm = pl.BlockSpec(memory_space=pl.ANY)
    wide = pltpu.CompilerParams(vmem_limit_bytes=60 * 1024 * 1024)
    objects = object_slices.reshape(-1, column_count)
    directions = direction.reshape(-1, column_count)
    block, note = pl.pallas_call(
        functools.partial(pack_kernel, strip_rows, strip_count * strip_rows),
        out_shape=(
            jax.ShapeDtypeStruct((block_rows, column_count), BF16),
            jax.ShapeDtypeStruct((NOTE_ROWS, column_count), BF16),
        ),
        in_specs=[hbm] * 4,
        out_specs=(vmem, vmem),
        scratch_shapes=[
            pltpu.SMEM(corner_row.shape, jnp.int32),
            pltpu.SMEM(corner_row.shape, jnp.int32),
            pltpu.SemaphoreType.DMA((4,)),
        ],
        compiler_params=wide,
        name="pack_block",
    )(corner_row, corner_col, objects, directions)
    far = lax.ppermute(note, "strip", [(i, (i + REACH) % strip_count) for i in range(strip_count)])
    first, second = exchanged(block, -1), exchanged(block, 0)
    kernel_cos, kernel_sin, tables = pl.pallas_call(
        phase_kernel,
        out_shape=(
            jax.ShapeDtypeStruct(kernel_phase.shape, F32),
            jax.ShapeDtypeStruct(kernel_phase.shape, F32),
            jax.ShapeDtypeStruct((len(units), 2, 2 * patch_size, 2 * patch_size), BF16),
        ),
        in_specs=[vmem] * 2,
        out_specs=(vmem,) * 3,
        compiler_params=params,
        name="phase_tables",
    )(kernel_phase, jnp.asarray(halves))
    near = corner_row.shape[0]
    strip_shape = (2, strip_rows, column_count)

    chips = cuts_count // 2
    same_core = [[core + 2 * chip for chip in range(chips)] for core in range(2)]

    def cut(targets, counted, *operands):
        windows_shape = (targets, 4, patch_size, patch_size)
        out_shape = (jax.ShapeDtypeStruct(windows_shape, BF16), jax.ShapeDtypeStruct((2 * targets, 128), F32))
        out_specs = (vmem, vmem)
        if counted:
            out_shape += (jax.ShapeDtypeStruct((1,), jnp.int32),)
            out_specs += (pl.BlockSpec(memory_space=pltpu.SMEM),)
        return pl.pallas_call(
            functools.partial(cut_kernel, strip_rows, near),
            out_shape=out_shape,
            in_specs=[vmem] * 6,
            out_specs=out_specs,
            compiler_params=params,
            name="cut_windows",
        )(*operands)

    def chain(windows, other, *constants):
        return pl.pallas_call(
            functools.partial(chain_kernel, units),
            out_shape=jax.ShapeDtypeStruct((windows.shape[0], 2, patch_size, patch_size), BF16),
            in_specs=[vmem] * 6,
            out_specs=vmem,
            scratch_shapes=[pltpu.VMEM((cuts_count, 2, patch_size, patch_size), F32)],
            compiler_params=params,
            name="wave_chain",
        )(windows, other, *constants)

    def gather(start, gradient):
        return pl.pallas_call(
            functools.partial(gather_kernel, len(OWNERS) * near),
            out_shape=(
                jax.ShapeDtypeStruct(strip_shape, BF16),
                jax.ShapeDtypeStruct(strip_shape, F32),
                jax.ShapeDtypeStruct(strip_shape, BF16),
            ),
            in_specs=[vmem, vmem],
            out_specs=(vmem, vmem, vmem),
            compiler_params=params,
            name="add_windows",
        )(start, gradient)

    def one_per_chip(windows, start, around, constants):
        del around
        windows = lax.all_to_all(windows, "cuts", 0, 0, axis_index_groups=same_core, tiled=False)
        other = lax.ppermute(windows, "cuts", [(i, i ^ 1) for i in range(cuts_count)])
        gradient = chain(windows, other, *constants)
        gradient = lax.all_to_all(gradient, "cuts", 0, 0, axis_index_groups=same_core, tiled=False)
        return gather(start, gradient)

    def one_per_device(windows, start, around, constants):
        del windows, start
        windows, start = cut(cuts_count, False, *around)
        windows = lax.all_to_all(windows, "cuts", 0, 0, tiled=False)
        gradient = chain(windows, windows, *constants)
        gradient = lax.all_to_all(gradient, "cuts", 0, 0, tiled=False)
        return gather(start, gradient)

    around = (far, note, objects, directions, second, first)
    windows, start, count = cut(chips, True, *around)
    constants = (probe_wave, kernel_cos, kernel_sin, tables)
    first, own, second = lax.cond(
        count[0] > chips, one_per_device, one_per_chip, windows, start, around, constants
    )
    first, second = exchanged(first, -1), exchanged(second, 0)
    return (own + first.astype(F32) + second.astype(F32))[None]


def solution(mesh):
    in_specs = (
        P("cuts", None, "strip", None),
        P("cuts", None, "strip", None),
        P(),
        P(),
        P("strip"),
        P("strip"),
    )
    out_specs = P("cuts", None, "strip", None)
    return jax.shard_map(
        on_device, mesh=mesh, in_specs=in_specs, out_specs=out_specs, check_vma=False
    )
```
